32 devices in a mesh: groups: 2 (over y), date: 4 (over x, core), col: 4 (over z).
Axes of the slice: x: 2, y: 2, z: 4, core: 2. Of those that a mesh axis runs over, the one named last changes fastest.
Arguments:
- scenes: bfloat16 [16, 2, 128, 1024], P('date', None, 'groups', 'col'), parts along dimension 2, may hold values from -6 to 6
- pair_dates: int32 [96, 2], P('date'), may hold values from 0 to 15, as said below
- pair_count: int32 [4], P('date'), may hold values from 12 to 24, as said below
- inverse: float32 [15, 96], replicated, may hold values from -0.625 to 0.625
Outputs:
- series: float32 [15, 2, 64, 128], P(None, None, ('groups', 'date'), 'col'), parts along dimension 2
The draws below stay inside these ranges and needn't reach their ends.
There are 2 independent parts, one for each index of `groups`. The reference program is written for one: setup_inputs(seed, part) draws one part's arguments, and reference() takes and returns one part's arrays. A program takes and returns all parts, laid end to end along the dimension named above; an argument that names none is the same for every part. Nothing has to cross between parts.
Inputs may be any that keep to these rules, and one draw needn't show every extreme that they name: `pair_dates`: each row names a reference acquisition and a later secondary one. Slots i * 24 to (i + 1) * 24 - 1 belong to owner i (index i of date); every slot of owner i names acquisitions held by indices i - 2 to i + 2 of date (as far as these exist), and one live pair of every owner names the lowest and the highest acquisition of that range. `pair_count`: entry i is the number of live slots of owner i; they come first in its block and the other slots are ignored. Some owner has all its slots live.
All inputs are finite; a program needn't handle non-finite values.
Results may differ from the reference program's by a relative error of at most 0.0003.
Values may be sent and summed in bfloat16 or wider, within the bound.
No kernel may reach another device: no remote copies, remote signals or barrier semaphores. Data moves between devices by JAX's collectives and lax.ppermute only.
A program may use at most 64 MiB of HBM per device.

```python
import jax
import jax.numpy as jnp
from jax import lax

DATE_DEV = 4
PAIR_DEV = 24
HOPS = 2
ROWS = 64
DATES = 16
PAIRS = 96
NPAR = 15
COLS = 1024
MLR = 32
MLC = 128


def draw_pair_dates(key, part):
    indices = jnp.arange(PAIRS, dtype=jnp.int32)
    owners = indices // PAIR_DEV
    within = indices % PAIR_DEV
    lowest = jnp.maximum(0, (owners - HOPS) * DATE_DEV)
    highest = jnp.minimum(DATES, (owners + HOPS + 1) * DATE_DEV)
    key_first, key_step = jax.random.split(jax.random.fold_in(key, 11))
    leading = jax.random.randint(key_first, (PAIRS,), lowest, highest - 1)
    stepping = jax.random.randint(key_step, (PAIRS,), 1, 7)
    trailing = jnp.minimum(leading + stepping, highest - 1)
    leading = jnp.where(within == 0, lowest, leading)
    trailing = jnp.where(within == 0, jnp.minimum(lowest + stepping, highest - 1), trailing)
    leading = jnp.where(within == 1, jnp.maximum(lowest, highest - 1 - stepping), leading)
    trailing = jnp.where(within == 1, highest - 1, trailing)
    leading = jnp.where(within == 2, lowest, leading)
    trailing = jnp.where(within == 2, highest - 1, trailing)
    return jnp.stack([leading, trailing], axis=1).astype(jnp.int32)


def draw_pair_count(key, part):
    owner_total = PAIRS // PAIR_DEV
    key_counts, key_full = jax.random.split(jax.random.fold_in(key, 23))
    counts = jax.random.randint(key_counts, (owner_total,), PAIR_DEV // 2, PAIR_DEV + 1)
    busiest = jax.random.randint(key_full, (), 0, owner_total)
    return jnp.where(jnp.arange(owner_total) == busiest, PAIR_DEV, counts).astype(jnp.int32)


def shard_levels(stream_key, dims, cuts, smallest, largest):
    def one(dim, blocks):
        heights = jax.random.uniform(jax.random.fold_in(jax.random.fold_in(stream_key, 6), dim), (blocks,), jnp.float32, smallest / len(cuts), largest / len(cuts))
        return jnp.repeat(jnp.exp(heights), dims[dim] // blocks).reshape((-1,) + (1,) * (len(dims) - dim - 1))

    factor_of = one(*cuts[0])
    for cut in cuts[1:]:
        factor_of = factor_of * one(*cut)
    return factor_of


def noise(own_key, dims, spread, reach, pieces=(), kind=jnp.bfloat16):
    array = spread * jax.random.normal(own_key, dims, jnp.float32)
    if pieces:
        array = array * shard_levels(own_key, dims, pieces, -0.22, 0.18)
    return jnp.clip(array, -reach, reach).astype(kind)


def setup_inputs(seed: int = 0, part: int = 0) -> dict:
    seeds = jax.random.split(jax.random.key(seed), 5)
    part_keys = jax.random.split(jax.random.fold_in(seeds[4], part), 5)
    return {
        "scenes": noise(part_keys[0], (DATES, 2, ROWS, COLS), 1.0, 6.0, ((0, 4), (3, 4))),
        "pair_dates": draw_pair_dates(jax.random.fold_in(seeds[4], 71), part),
        "pair_count": draw_pair_count(jax.random.fold_in(seeds[4], 71), part),
        "inverse": noise(seeds[3], (NPAR, PAIRS), PAIRS ** -0.5, 0.625, (), jnp.float32),
    }


def look_weights():
    offsets = jnp.arange(16).astype(jnp.float32)
    return (8.0 - jnp.abs(offsets - 7.5)) / 64.0


def reference(scenes, pair_dates, pair_count, inverse):
    indices = jnp.arange(PAIRS).astype(jnp.int32)
    owners = indices // PAIR_DEV
    within = indices % PAIR_DEV
    living = (within < pair_count[owners]).astype(jnp.float32)
    weights = look_weights()

    def one_pair(member):
        pair_row, alive = member
        primary = scenes[pair_row[0]].astype(jnp.float32)
        secondary = scenes[pair_row[1]].astype(jnp.float32)
        real_part = primary[0] * secondary[0] + primary[1] * secondary[1]
        imaginary = primary[1] * secondary[0] - primary[0] * secondary[1]
        products = jnp.stack([real_part, imaginary]) * alive
        halved = 0.5 * (products[:, 0::2, :] + products[:, 1::2, :])
        padded = jnp.pad(halved, ((0, 0), (0, 0), (4, 4)))
        looked = jnp.zeros((2, MLR, MLC), jnp.float32)
        for offset in range(16):
            looked = looked + weights[offset] * padded[:, :, offset: offset + COLS: 8]
        return looked

    multilooked = lax.map(one_pair, (pair_dates, living))
    flattened = multilooked.reshape(PAIRS, 2 * MLR * MLC)
    series = jnp.dot(inverse, flattened, precision=lax.Precision.HIGHEST, preferred_element_type=jnp.float32)
    return series.reshape(NPAR, 2, MLR, MLC)
```

```python
import functools

import jax
import jax.numpy as jnp
from jax import lax
from jax.experimental import pallas as pl
from jax.experimental.pallas import tpu as pltpu
from jax.sharding import PartitionSpec as P

F32, BF16 = jnp.float32, jnp.bfloat16
LANES = 128
NOTE_ROWS = 16
IN_VMEM = pl.BlockSpec(memory_space=pltpu.VMEM)
IN_SMEM = pl.BlockSpec(memory_space=pltpu.SMEM)


def round_up(value, step):
    return -(-value // step) * step


def held(array):
    return pltpu.with_memory_space_constraint(array, pltpu.VMEM)


def iota(shape, axis):
    return lax.broadcasted_iota(jnp.int32, shape, axis)


def halves(value):
    high = value.astype(BF16)
    return high, (value - high.astype(F32)).astype(BF16)


def note_of(pair_dates, count):
    slots = pair_dates.shape[0]
    here = iota((slots, LANES), 0) == iota((slots, LANES), 1)
    dates = pair_dates.astype(F32)
    row, lane = iota((NOTE_ROWS, LANES), 0), iota((NOTE_ROWS, LANES), 1)
    note = jnp.where((row == 2) & (lane < jnp.minimum(count, slots)), 1.0, 0.0)
    for side in range(2):
        along = jnp.sum(jnp.where(here, dates[:, side : side + 1], 0.0), axis=0, keepdims=True)
        note = jnp.where(row == side, along, note)
    return note.astype(BF16)


def cut_kernel(count_ref, scenes_ref, dates_ref, inverse_ref, *outs):
    *block_refs, wide_ref = outs
    owners = len(block_refs)
    me = lax.axis_index("date")
    rows = scenes_ref.shape[2] // owners
    note = note_of(dates_ref[...], count_ref[0])
    for step, block_ref in enumerate(block_refs):
        first = pl.multiple_of(lax.rem(me + owners - step, owners) * rows, rows)
        cells = scenes_ref[:, :, pl.ds(first, rows), :]
        height = block_ref.shape[0] - NOTE_ROWS
        block_ref[:height] = cells.reshape(height, block_ref.shape[1])
        block_ref[height:, :LANES] = note
    wide_ref[...] = jnp.zeros_like(wide_ref)
    wide_ref[: inverse_ref.shape[0], : inverse_ref.shape[1]] = inverse_ref[...]


def note_kernel(count_ref, dates_ref, inverse_ref, note_ref, wide_ref):
    note_ref[...] = jnp.zeros_like(note_ref)
    note_ref[:, :LANES] = note_of(dates_ref[...], count_ref[0])
    wide_ref[...] = jnp.zeros_like(wide_ref)
    wide_ref[: inverse_ref.shape[0], : inverse_ref.shape[1]] = inverse_ref[...]


def cut(scenes, pair_dates, pair_count, inverse, owners):
    dates_here, parts, all_rows, columns = scenes.shape
    rows = all_rows // owners
    height = dates_here * parts * rows
    wide = pltpu.VMEM(
        (round_up(inverse.shape[0], 16), round_up(inverse.shape[1], LANES)), F32
    )
    if rows % 16 == 0:
        *blocks, wide = pl.pallas_call(
            cut_kernel,
            out_shape=[pltpu.VMEM((height + NOTE_ROWS, columns), BF16)] * owners + [wide],
            in_specs=[IN_SMEM] + [IN_VMEM] * 3,
            out_specs=[IN_VMEM] * (owners + 1),
        )(pair_count, scenes, pair_dates, inverse)
        return blocks, wide
    note, wide = pl.pallas_call(
        note_kernel,
        out_shape=[pltpu.VMEM((NOTE_ROWS, columns), BF16), wide],
        in_specs=[IN_SMEM] + [IN_VMEM] * 2,
        out_specs=[IN_VMEM] * 2,
    )(pair_count, pair_dates, inverse)
    me = lax.axis_index("date")
    apart = scenes.reshape(dates_here * parts, owners, rows, columns)
    blocks = []
    for step in range(owners):
        cells = lax.dynamic_index_in_dim(apart, lax.rem(me + owners - step, owners), 1, False)
        blocks.append(jnp.concatenate([cells.reshape(height, columns), note], axis=0))
    return blocks, wide


def pair_weights(block_refs, wide, dates_here, slots):
    owners = len(block_refs)
    dates = owners * dates_here
    reach = dates // 2
    me = lax.axis_index("date")
    lanes = wide.shape[1]
    ring = jnp.zeros((8, lanes), F32)
    for step, block_ref in enumerate(block_refs):
        height = block_ref.shape[0]
        note = block_ref[height - NOTE_ROWS : height, :LANES].astype(F32)[:8]
        if lanes > LANES:
            note = jnp.concatenate([note, jnp.zeros((8, lanes - LANES), F32)], axis=1)
        ring = ring + pltpu.roll(note, lax.rem(me + step, owners) * slots, 1)
    start = jnp.full((1, lanes), me * dates_here, jnp.int32).astype(F32)

    def wrapped(value):
        return jnp.where(value < 0.0, value + dates, value)

    first, second = wrapped(ring[0:1] - start), wrapped(ring[1:2] - start)
    ahead = wrapped(second - first)
    onward = ahead <= reach
    place = jnp.where(onward, (ahead - 1.0) * dates + first, (dates - ahead - 1.0) * dates + second)
    place = jnp.where(ring[2:3] > 0.5, place, -1.0)
    pairs = reach * dates
    chosen = jnp.where(iota((pairs, lanes), 0).astype(F32) == place, 1.0, 0.0).astype(BF16)
    signed = jnp.where(onward, wide, -wide)
    stacked = jnp.concatenate([*halves(wide), *halves(signed)], axis=0)
    spread = lax.dot_general(
        stacked, chosen, (((1,), (1,)), ((), ())), preferred_element_type=F32
    )
    tall = wide.shape[0]
    weights = []
    for part in range(2):
        summed = spread[2 * part * tall : (2 * part + 1) * tall]
        summed = summed + spread[(2 * part + 1) * tall : (2 * part + 2) * tall]
        high, low = halves(summed)
        weights.append(
            jnp.concatenate(
                [jnp.concatenate([high, high], axis=1), jnp.concatenate([low, low], axis=1)], axis=0
            )
        )
    return weights


def look_weights(columns):
    looks = columns // 8
    column, look = iota((columns, LANES), 0), iota((columns, LANES), 1)
    target = jnp.where(look == looks + 1, -1, look)
    offset = (column - 8 * target + 4).astype(F32)
    inside = (offset >= 0.0) & (offset < 16.0) & (look < looks + 2)
    return jnp.where(inside, (8.0 - jnp.abs(offset - 7.5)) / 128.0, 0.0).astype(BF16)


def series_kernel(dates_here, slots, *refs):
    *block_refs, wide_ref, looked_ref, first_ref, second_ref, ring_ref, pair_ref = refs
    owners = len(block_refs)
    dates = owners * dates_here
    reach = dates // 2
    pairs = reach * dates
    columns = block_refs[0].shape[1]
    looks = columns // 8
    rows = (block_refs[0].shape[0] - NOTE_ROWS) // (2 * dates_here)
    extent = ring_ref.shape[2] // rows
    tall = wide_ref.shape[0]

    for step, block_ref in enumerate(block_refs):
        for own in range(dates_here):
            for part in range(2):
                at = (own * 2 + part) * rows
                cells = block_ref[at : at + rows].astype(F32)
                date = step * dates_here + own
                for place in range(date, extent, dates):
                    for side in range(columns // LANES):
                        ring_ref[part, side, pl.ds(place, rows, stride=extent), :] = cells[
                            :, side * LANES : (side + 1) * LANES
                        ]

    weights = pair_weights(block_refs, wide_ref[...], dates_here, slots)
    look = look_weights(columns)

    lane = iota((tall, LANES), 1)
    to_right = jnp.zeros((tall, LANES), F32)
    to_left = jnp.zeros((tall, LANES), F32)
    for half_row in range(rows // 2):
        for side in range(columns // LANES):

            def load(part, odd, shift):
                at = (2 * half_row + odd) * extent + shift
                return ring_ref[part, side, at : at + dates, :]

            real_0, real_1, imag_0, imag_1 = (load(c, o, 0) for c in range(2) for o in range(2))
            for shift in range(1, reach + 1):
                other_0, other_1 = load(0, 0, shift), load(0, 1, shift)
                turned_0, turned_1 = load(1, 0, shift), load(1, 1, shift)
                real = (real_0 * other_0 + imag_0 * turned_0) + (
                    real_1 * other_1 + imag_1 * turned_1
                )
                imaginary = (imag_0 * other_0 - real_0 * turned_0) + (
                    imag_1 * other_1 - real_1 * turned_1
                )
                at = (shift - 1) * dates
                for part, value in enumerate((real, imaginary)):
                    high, low = halves(value)
                    across = slice(
                        part * columns + side * LANES, part * columns + (side + 1) * LANES
                    )
                    pair_ref[half_row, at : at + dates, across] = high
                    pair_ref[half_row, pairs + at : pairs + at + dates, across] = low
        for part in range(2):
            summed = jnp.dot(
                weights[part],
                pair_ref[half_row, :, part * columns : (part + 1) * columns],
                preferred_element_type=F32,
            )
            summed = summed[:tall] + summed[tall:]
            looked = jnp.dot(
                jnp.concatenate(halves(summed), axis=0), look, preferred_element_type=F32
            )
            looked = looked[:tall] + looked[tall:]
            index = part * (rows // 2) + half_row
            looked_ref[index * tall : (index + 1) * tall, :] = looked
            to_right = jnp.where(
                lane == index, pltpu.roll(looked, (index - looks) % LANES, 1), to_right
            )
            to_left = jnp.where(
                lane == index, pltpu.roll(looked, (index - looks - 1) % LANES, 1), to_left
            )
    even = lax.rem(lax.axis_index("col"), 2) == 0
    first_ref[...] = jnp.where(even, to_right, to_left)
    second_ref[...] = jnp.where(even, to_left, to_right)


def finish_kernel(looked_ref, first_ref, second_ref, out_ref, sum_ref):
    times, parts, half_rows, looks = out_ref.shape
    tall = first_ref.shape[0]
    here, last = lax.axis_index("col"), lax.axis_size("col") - 1
    even = lax.rem(here, 2) == 0
    first, second = first_ref[...], second_ref[...]
    nothing = jnp.zeros_like(first)
    from_right = jnp.where(here == last, nothing, jnp.where(even, first, second))
    from_left = jnp.where(here == 0, nothing, jnp.where(even, second, first))
    lane = iota((tall, LANES), 1)
    for index in range(parts * half_rows):
        value = looked_ref[index * tall : (index + 1) * tall, :]
        value = value + jnp.where(
            lane == looks - 1, pltpu.roll(from_right, (looks - 1 - index) % LANES, 1), 0.0
        )
        value = value + jnp.where(lane == 0, pltpu.roll(from_left, -index % LANES, 1), 0.0)
        sum_ref[index * tall : (index + 1) * tall, :] = value
    for time in range(times):
        for part in range(parts):
            rows = sum_ref[pl.ds(part * half_rows * tall + time, half_rows, stride=tall), :]
            out_ref[time, part] = rows[:, :looks]


def column_swap(first, owners, count):
    moves = []
    for owner in range(owners):
        for column in range(count):
            partner = column + 1 if (column - first) % 2 == 0 else column - 1
            to = owner
            if not 0 <= partner < count:
                partner = column
                to = owner ^ 1 if owners % 2 == 0 else owner
            moves.append((owner * count + column, to * count + partner))
    return moves


def per_device(scenes, pair_dates, pair_count, inverse):
    owners, count = lax.axis_size("date"), lax.axis_size("col")
    dates_here, parts, all_rows, columns = scenes.shape
    half_rows = all_rows // owners // 2
    dates = owners * dates_here
    reach = dates // 2
    extent = round_up(dates + reach, 8)

    blocks, wide = cut(scenes, pair_dates, pair_count, inverse, owners)
    for step in range(1, owners):
        moves = [(owner, (owner - step) % owners) for owner in range(owners)]
        blocks[step] = lax.ppermute(blocks[step], "date", moves)

    tall = wide.shape[0]
    looked, first, second = pl.pallas_call(
        functools.partial(series_kernel, dates_here, pair_dates.shape[0]),
        out_shape=[
            pltpu.VMEM((parts * half_rows * tall, LANES), F32),
            pltpu.VMEM((tall, LANES), F32),
            pltpu.VMEM((tall, LANES), F32),
        ],
        in_specs=[IN_VMEM] * (owners + 1),
        out_specs=[IN_VMEM] * 3,
        scratch_shapes=[
            pltpu.VMEM((parts, columns // LANES, 2 * half_rows * extent, LANES), F32),
            pltpu.VMEM((half_rows, 2 * reach * dates, parts * columns), BF16),
        ],
        compiler_params=pltpu.CompilerParams(vmem_limit_bytes=40 << 20),
    )(*[held(block) for block in blocks], held(wide))

    first = lax.ppermute(first, ("date", "col"), column_swap(0, owners, count))
    second = lax.ppermute(second, ("date", "col"), column_swap(1, owners, count))
    return pl.pallas_call(
        finish_kernel,
        out_shape=jax.ShapeDtypeStruct(
            (inverse.shape[0], parts, half_rows, columns // 8), F32
        ),
        in_specs=[IN_VMEM] * 3,
        out_specs=IN_VMEM,
        scratch_shapes=[pltpu.VMEM((parts * half_rows * tall, LANES), F32)],
    )(held(looked), held(first), held(second))


def solution(mesh):
    placed = (P("date", None, "groups", "col"), P("date", None), P("date"), P())
    return jax.shard_map(
        per_device,
        mesh=mesh,
        in_specs=placed,
        out_specs=P(None, None, ("groups", "date"), "col"),
        check_vma=False,
    )
```

```python
import functools

import jax
import jax.numpy as jnp
from jax import lax
from jax.experimental import pallas as pl
from jax.experimental.pallas import tpu as pltpu
from jax.sharding import PartitionSpec as P

F32, BF16 = jnp.float32, jnp.bfloat16
LANES = 128
NOTE_ROWS = 16
IN_VMEM = pl.BlockSpec(memory_space=pltpu.VMEM)
IN_SMEM = pl.BlockSpec(memory_space=pltpu.SMEM)


def round_up(value, step):
    return -(-value // step) * step


def held(array):
    return pltpu.with_memory_space_constraint(array, pltpu.VMEM)


def iota(shape, axis):
    return lax.broadcasted_iota(jnp.int32, shape, axis)


def halves(value):
    high = value.astype(BF16)
    return high, (value - high.astype(F32)).astype(BF16)


def note_of(pair_dates, count):
    slots = pair_dates.shape[1]
    dates = jnp.concatenate([pair_dates.astype(F32), jnp.zeros((2, LANES - slots), F32)], axis=1)
    row, lane = iota((NOTE_ROWS, LANES), 0), iota((NOTE_ROWS, LANES), 1)
    note = jnp.where((row == 2) & (lane < jnp.minimum(count, slots)), 1.0, 0.0)
    for side in range(2):
        note = jnp.where(row == side, dates[side : side + 1], note)
    return note.astype(BF16)


def cut_kernel(count_ref, scenes_ref, dates_ref, inverse_ref, *outs):
    *block_refs, wide_ref = outs
    owners = len(block_refs)
    me = lax.axis_index("date")
    rows = scenes_ref.shape[2] // owners
    note = note_of(dates_ref[...], count_ref[0])
    for step, block_ref in enumerate(block_refs):
        first = pl.multiple_of(lax.rem(me + owners - step, owners) * rows, rows)
        cells = scenes_ref[:, :, pl.ds(first, rows), :]
        height = block_ref.shape[0] - NOTE_ROWS
        block_ref[:height] = cells.reshape(height, block_ref.shape[1])
        block_ref[height:, :LANES] = note
    wide_ref[...] = jnp.zeros_like(wide_ref)
    wide_ref[: inverse_ref.shape[0], : inverse_ref.shape[1]] = inverse_ref[...]


def note_kernel(count_ref, dates_ref, inverse_ref, note_ref, wide_ref):
    note_ref[...] = jnp.zeros_like(note_ref)
    note_ref[:, :LANES] = note_of(dates_ref[...], count_ref[0])
    wide_ref[...] = jnp.zeros_like(wide_ref)
    wide_ref[: inverse_ref.shape[0], : inverse_ref.shape[1]] = inverse_ref[...]


def cut(scenes, pair_dates, pair_count, inverse, owners):
    dates_here, parts, all_rows, columns = scenes.shape
    rows = all_rows // owners
    height = dates_here * parts * rows
    wide = pltpu.VMEM(
        (round_up(inverse.shape[0], 16), round_up(inverse.shape[1], LANES)), F32
    )
    if rows % 16 == 0:
        *blocks, wide = pl.pallas_call(
            cut_kernel,
            out_shape=[pltpu.VMEM((height + NOTE_ROWS, columns), BF16)] * owners + [wide],
            in_specs=[IN_SMEM] + [IN_VMEM] * 3,
            out_specs=[IN_VMEM] * (owners + 1),
        )(pair_count, scenes, pair_dates, inverse)
        return blocks, wide
    note, wide = pl.pallas_call(
        note_kernel,
        out_shape=[pltpu.VMEM((NOTE_ROWS, columns), BF16), wide],
        in_specs=[IN_SMEM] + [IN_VMEM] * 2,
        out_specs=[IN_VMEM] * 2,
    )(pair_count, pair_dates, inverse)
    me = lax.axis_index("date")
    apart = scenes.reshape(dates_here * parts, owners, rows, columns)
    blocks = []
    for step in range(owners):
        cells = lax.dynamic_index_in_dim(apart, lax.rem(me + owners - step, owners), 1, False)
        blocks.append(jnp.concatenate([cells.reshape(height, columns), note], axis=0))
    return blocks, wide


def pair_weights(block_refs, wide, dates_here, slots):
    owners = len(block_refs)
    dates = owners * dates_here
    reach = dates // 2
    me = lax.axis_index("date")
    lanes = wide.shape[1]
    ring = jnp.zeros((8, lanes), F32)
    for step, block_ref in enumerate(block_refs):
        height = block_ref.shape[0]
        note = block_ref[height - NOTE_ROWS : height, :LANES].astype(F32)[:8]
        if lanes > LANES:
            note = jnp.concatenate([note, jnp.zeros((8, lanes - LANES), F32)], axis=1)
        ring = ring + pltpu.roll(note, lax.rem(me + step, owners) * slots, 1)
    start = jnp.full((1, lanes), me * dates_here, jnp.int32).astype(F32)

    def wrapped(value):
        return jnp.where(value < 0.0, value + dates, value)

    first, second = wrapped(ring[0:1] - start), wrapped(ring[1:2] - start)
    ahead = wrapped(second - first)
    onward = ahead <= reach
    place = jnp.where(onward, (ahead - 1.0) * dates + first, (dates - ahead - 1.0) * dates + second)
    place = jnp.where(ring[2:3] > 0.5, place, -1.0)
    pairs = reach * dates
    chosen = jnp.where(iota((pairs, lanes), 0).astype(F32) == place, 1.0, 0.0).astype(BF16)
    signed = jnp.where(onward, wide, -wide)
    stacked = jnp.concatenate([*halves(wide), *halves(signed)], axis=0)
    spread = lax.dot_general(
        stacked, chosen, (((1,), (1,)), ((), ())), preferred_element_type=F32
    )
    tall = wide.shape[0]
    weights = []
    for part in range(2):
        summed = spread[2 * part * tall : (2 * part + 1) * tall]
        summed = summed + spread[(2 * part + 1) * tall : (2 * part + 2) * tall]
        high, low = halves(summed)
        weights.append(
            jnp.concatenate(
                [jnp.concatenate([high, high], axis=1), jnp.concatenate([low, low], axis=1)], axis=0
            )
        )
    return weights


def look_weights(columns):
    looks = columns // 8
    column, look = iota((columns, LANES), 0), iota((columns, LANES), 1)
    target = jnp.where(look == looks + 1, -1, look)
    offset = (column - 8 * target + 4).astype(F32)
    inside = (offset >= 0.0) & (offset < 16.0) & (look < looks + 2)
    return jnp.where(inside, (8.0 - jnp.abs(offset - 7.5)) / 128.0, 0.0).astype(BF16)


def series_kernel(dates_here, slots, *refs):
    *block_refs, wide_ref, looked_ref, first_ref, second_ref, ring_ref, pair_ref = refs
    owners = len(block_refs)
    dates = owners * dates_here
    reach = dates // 2
    pairs = reach * dates
    columns = block_refs[0].shape[1]
    looks = columns // 8
    rows = (block_refs[0].shape[0] - NOTE_ROWS) // (2 * dates_here)
    extent = ring_ref.shape[2] // rows
    tall = wide_ref.shape[0]

    for step, block_ref in enumerate(block_refs):
        for own in range(dates_here):
            for part in range(2):
                at = (own * 2 + part) * rows
                cells = block_ref[at : at + rows].astype(F32)
                date = step * dates_here + own
                for place in range(date, extent, dates):
                    for side in range(columns // LANES):
                        ring_ref[part, side, pl.ds(place, rows, stride=extent), :] = cells[
                            :, side * LANES : (side + 1) * LANES
                        ]

    weights = pair_weights(block_refs, wide_ref[...], dates_here, slots)
    look = look_weights(columns)

    lane = iota((tall, LANES), 1)
    to_right = jnp.zeros((tall, LANES), F32)
    to_left = jnp.zeros((tall, LANES), F32)
    for half_row in range(rows // 2):
        for side in range(columns // LANES):

            def load(part, odd, shift):
                at = (2 * half_row + odd) * extent + shift
                return ring_ref[part, side, at : at + dates, :]

            real_0, real_1, imag_0, imag_1 = (load(c, o, 0) for c in range(2) for o in range(2))
            for shift in range(1, reach + 1):
                other_0, other_1 = load(0, 0, shift), load(0, 1, shift)
                turned_0, turned_1 = load(1, 0, shift), load(1, 1, shift)
                real = (real_0 * other_0 + imag_0 * turned_0) + (
                    real_1 * other_1 + imag_1 * turned_1
                )
                imaginary = (imag_0 * other_0 - real_0 * turned_0) + (
                    imag_1 * other_1 - real_1 * turned_1
                )
                at = (shift - 1) * dates
                for part, value in enumerate((real, imaginary)):
                    high, low = halves(value)
                    across = slice(
                        part * columns + side * LANES, part * columns + (side + 1) * LANES
                    )
                    pair_ref[half_row, at : at + dates, across] = high
                    pair_ref[half_row, pairs + at : pairs + at + dates, across] = low
        for part in range(2):
            summed = jnp.dot(
                weights[part],
                pair_ref[half_row, :, part * columns : (part + 1) * columns],
                preferred_element_type=F32,
            )
            summed = summed[:tall] + summed[tall:]
            looked = jnp.dot(
                jnp.concatenate(halves(summed), axis=0), look, preferred_element_type=F32
            )
            looked = looked[:tall] + looked[tall:]
            index = part * (rows // 2) + half_row
            looked_ref[index * tall : (index + 1) * tall, :] = looked
            to_right = jnp.where(
                lane == index, pltpu.roll(looked, (index - looks) % LANES, 1), to_right
            )
            to_left = jnp.where(
                lane == index, pltpu.roll(looked, (index - looks - 1) % LANES, 1), to_left
            )
    even = lax.rem(lax.axis_index("col"), 2) == 0
    first_ref[...] = jnp.where(even, to_right, to_left)
    second_ref[...] = jnp.where(even, to_left, to_right)


def finish_kernel(looked_ref, first_ref, second_ref, out_ref, sum_ref):
    times, parts, half_rows, looks = out_ref.shape
    tall = first_ref.shape[0]
    here, last = lax.axis_index("col"), lax.axis_size("col") - 1
    even = lax.rem(here, 2) == 0
    first, second = first_ref[...], second_ref[...]
    nothing = jnp.zeros_like(first)
    from_right = jnp.where(here == last, nothing, jnp.where(even, first, second))
    from_left = jnp.where(here == 0, nothing, jnp.where(even, second, first))
    lane = iota((tall, LANES), 1)
    for index in range(parts * half_rows):
        value = looked_ref[index * tall : (index + 1) * tall, :]
        value = value + jnp.where(
            lane == looks - 1, pltpu.roll(from_right, (looks - 1 - index) % LANES, 1), 0.0
        )
        value = value + jnp.where(lane == 0, pltpu.roll(from_left, -index % LANES, 1), 0.0)
        sum_ref[index * tall : (index + 1) * tall, :] = value
    for time in range(times):
        for part in range(parts):
            rows = sum_ref[pl.ds(part * half_rows * tall + time, half_rows, stride=tall), :]
            out_ref[time, part] = rows[:, :looks]


def column_swap(first, owners, count):
    moves = []
    for owner in range(owners):
        for column in range(count):
            partner = column + 1 if (column - first) % 2 == 0 else column - 1
            to = owner
            if not 0 <= partner < count:
                partner = column
                to = owner ^ 1 if owners % 2 == 0 else owner
            moves.append((owner * count + column, to * count + partner))
    return moves


def per_device(scenes, pair_dates, pair_count, inverse):
    owners, count = lax.axis_size("date"), lax.axis_size("col")
    dates_here, parts, all_rows, columns = scenes.shape
    half_rows = all_rows // owners // 2
    dates = owners * dates_here
    reach = dates // 2
    extent = round_up(dates + reach, 8)

    blocks, wide = cut(scenes, pair_dates.T, pair_count, inverse, owners)
    for step in reversed(range(1, owners)):
        moves = [(owner, (owner - step) % owners) for owner in range(owners)]
        blocks[step] = lax.ppermute(blocks[step], "date", moves)

    tall = wide.shape[0]
    looked, first, second = pl.pallas_call(
        functools.partial(series_kernel, dates_here, pair_dates.shape[0]),
        out_shape=[
            pltpu.VMEM((parts * half_rows * tall, LANES), F32),
            pltpu.VMEM((tall, LANES), F32),
            pltpu.VMEM((tall, LANES), F32),
        ],
        in_specs=[IN_VMEM] * (owners + 1),
        out_specs=[IN_VMEM] * 3,
        scratch_shapes=[
            pltpu.VMEM((parts, columns // LANES, 2 * half_rows * extent, LANES), F32),
            pltpu.VMEM((half_rows, 2 * reach * dates, parts * columns), BF16),
        ],
        compiler_params=pltpu.CompilerParams(vmem_limit_bytes=40 << 20),
    )(*[held(block) for block in blocks], held(wide))

    first = lax.ppermute(first, ("date", "col"), column_swap(0, owners, count))
    second = lax.ppermute(second, ("date", "col"), column_swap(1, owners, count))
    return pl.pallas_call(
        finish_kernel,
        out_shape=jax.ShapeDtypeStruct(
            (inverse.shape[0], parts, half_rows, columns // 8), F32
        ),
        in_specs=[IN_VMEM] * 3,
        out_specs=IN_VMEM,
        scratch_shapes=[pltpu.VMEM((parts * half_rows * tall, LANES), F32)],
    )(held(looked), held(first), held(second))


def solution(mesh):
    placed = (P("date", None, "groups", "col"), P("date", None), P("date"), P())
    return jax.shard_map(
        per_device,
        mesh=mesh,
        in_specs=placed,
        out_specs=P(None, None, ("groups", "date"), "col"),
        check_vma=False,
    )
```

```python
import functools

import jax
import jax.numpy as jnp
from jax import lax
from jax.experimental import pallas as pl
from jax.experimental.pallas import tpu as pltpu
from jax.sharding import PartitionSpec as P

F32, BF16 = jnp.float32, jnp.bfloat16
LANES = 128
NOTE_ROWS = 16
IN_VMEM = pl.BlockSpec(memory_space=pltpu.VMEM)
IN_SMEM = pl.BlockSpec(memory_space=pltpu.SMEM)


def round_up(value, step):
    return -(-value // step) * step


def held(array):
    return pltpu.with_memory_space_constraint(array, pltpu.VMEM)


def iota(shape, axis):
    return lax.broadcasted_iota(jnp.int32, shape, axis)


def halves(value):
    high = value.astype(BF16)
    return high, (value - high.astype(F32)).astype(BF16)


def note_of(pair_dates, count):
    slots = pair_dates.shape[1]
    dates = jnp.concatenate([pair_dates.astype(F32), jnp.zeros((2, LANES - slots), F32)], axis=1)
    row, lane = iota((NOTE_ROWS, LANES), 0), iota((NOTE_ROWS, LANES), 1)
    note = jnp.where((row == 2) & (lane < jnp.minimum(count, slots)), 1.0, 0.0)
    for side in range(2):
        note = jnp.where(row == side, dates[side : side + 1], note)
    return note.astype(BF16)


def cut_kernel(count_ref, scenes_ref, dates_ref, inverse_ref, *outs):
    *block_refs, wide_ref = outs
    owners = len(block_refs)
    me = lax.axis_index("date")
    rows = scenes_ref.shape[2] // owners
    note = note_of(dates_ref[...], count_ref[0])
    for step, block_ref in enumerate(block_refs):
        first = pl.multiple_of(lax.rem(me + owners - step, owners) * rows, rows)
        cells = scenes_ref[:, :, pl.ds(first, rows), :]
        height = block_ref.shape[0] - NOTE_ROWS
        block_ref[:height] = cells.reshape(height, block_ref.shape[1])
        block_ref[height:, :LANES] = note
    wide_ref[...] = jnp.zeros_like(wide_ref)
    wide_ref[: inverse_ref.shape[0], : inverse_ref.shape[1]] = inverse_ref[...]


def note_kernel(count_ref, dates_ref, inverse_ref, note_ref, wide_ref):
    note_ref[...] = jnp.zeros_like(note_ref)
    note_ref[:, :LANES] = note_of(dates_ref[...], count_ref[0])
    wide_ref[...] = jnp.zeros_like(wide_ref)
    wide_ref[: inverse_ref.shape[0], : inverse_ref.shape[1]] = inverse_ref[...]


def cut(scenes, pair_dates, pair_count, inverse, owners):
    dates_here, parts, all_rows, columns = scenes.shape
    rows = all_rows // owners
    height = dates_here * parts * rows
    wide = pltpu.VMEM(
        (round_up(inverse.shape[0], 16), round_up(inverse.shape[1], LANES)), F32
    )
    if rows % 16 == 0:
        *blocks, wide = pl.pallas_call(
            cut_kernel,
            out_shape=[pltpu.VMEM((height + NOTE_ROWS, columns), BF16)] * owners + [wide],
            in_specs=[IN_SMEM] + [IN_VMEM] * 3,
            out_specs=[IN_VMEM] * (owners + 1),
        )(pair_count, scenes, pair_dates, inverse)
        return blocks, wide
    note, wide = pl.pallas_call(
        note_kernel,
        out_shape=[pltpu.VMEM((NOTE_ROWS, columns), BF16), wide],
        in_specs=[IN_SMEM] + [IN_VMEM] * 2,
        out_specs=[IN_VMEM] * 2,
    )(pair_count, pair_dates, inverse)
    me = lax.axis_index("date")
    apart = scenes.reshape(dates_here * parts, owners, rows, columns)
    blocks = []
    for step in range(owners):
        cells = lax.dynamic_index_in_dim(apart, lax.rem(me + owners - step, owners), 1, False)
        blocks.append(jnp.concatenate([cells.reshape(height, columns), note], axis=0))
    return blocks, wide


def pair_weights(block_refs, wide, dates_here, slots):
    owners = len(block_refs)
    dates = owners * dates_here
    reach = dates // 2
    me = lax.axis_index("date")
    lanes = wide.shape[1]
    ring = jnp.zeros((8, lanes), F32)
    for step, block_ref in enumerate(block_refs):
        height = block_ref.shape[0]
        note = block_ref[height - NOTE_ROWS : height, :LANES].astype(F32)[:8]
        if lanes > LANES:
            note = jnp.concatenate([note, jnp.zeros((8, lanes - LANES), F32)], axis=1)
        ring = ring + pltpu.roll(note, lax.rem(me + step, owners) * slots, 1)
    start = jnp.full((1, lanes), me * dates_here, jnp.int32).astype(F32)

    def wrapped(value):
        return jnp.where(value < 0.0, value + dates, value)

    first, second = wrapped(ring[0:1] - start), wrapped(ring[1:2] - start)
    ahead = wrapped(second - first)
    onward = ahead <= reach
    place = jnp.where(onward, (ahead - 1.0) * dates + first, (dates - ahead - 1.0) * dates + second)
    place = jnp.where(ring[2:3] > 0.5, place, -1.0)
    pairs = reach * dates
    chosen = jnp.where(iota((pairs, lanes), 0).astype(F32) == place, 1.0, 0.0).astype(BF16)
    signed = jnp.where(onward, wide, -wide)
    stacked = jnp.concatenate([*halves(wide), *halves(signed)], axis=0)
    spread = lax.dot_general(
        stacked, chosen, (((1,), (1,)), ((), ())), preferred_element_type=F32
    )
    tall = wide.shape[0]
    weights = []
    for part in range(2):
        summed = spread[2 * part * tall : (2 * part + 1) * tall]
        summed = summed + spread[(2 * part + 1) * tall : (2 * part + 2) * tall]
        high, low = halves(summed)
        weights.append(
            jnp.concatenate(
                [jnp.concatenate([high, high], axis=1), jnp.concatenate([low, low], axis=1)], axis=0
            )
        )
    return weights


def look_weights(columns):
    looks = columns // 8
    column, look = iota((columns, LANES), 0), iota((columns, LANES), 1)
    target = jnp.where(look == looks + 1, -1, look)
    offset = (column - 8 * target + 4).astype(F32)
    inside = (offset >= 0.0) & (offset < 16.0) & (look < looks + 2)
    return jnp.where(inside, (8.0 - jnp.abs(offset - 7.5)) / 128.0, 0.0).astype(BF16)


def series_kernel(dates_here, slots, *refs):
    *block_refs, wide_ref, looked_ref, first_ref, second_ref, ring_ref, pair_ref, sum_ref = refs
    block_refs = block_refs[:1] + block_refs[:0:-1]
    owners = len(block_refs)
    dates = owners * dates_here
    reach = dates // 2
    pairs = reach * dates
    columns = block_refs[0].shape[1]
    looks = columns // 8
    rows = (block_refs[0].shape[0] - NOTE_ROWS) // (2 * dates_here)
    extent = ring_ref.shape[2] // rows
    tall = wide_ref.shape[0]

    for step, block_ref in enumerate(block_refs):
        for own in range(dates_here):
            for part in range(2):
                at = (own * 2 + part) * rows
                cells = block_ref[at : at + rows].astype(F32)
                date = step * dates_here + own
                for place in range(date, extent, dates):
                    for side in range(columns // LANES):
                        ring_ref[part, side, pl.ds(place, rows, stride=extent), :] = cells[
                            :, side * LANES : (side + 1) * LANES
                        ]

    weights = pair_weights(block_refs, wide_ref[...], dates_here, slots)
    look = look_weights(columns)

    lane = iota((tall, LANES), 1)
    to_right = jnp.zeros((tall, LANES), F32)
    to_left = jnp.zeros((tall, LANES), F32)
    for half_row in range(rows // 2):
        for side in range(columns // LANES):

            def load(part, odd, shift):
                at = (2 * half_row + odd) * extent + shift
                return ring_ref[part, side, at : at + dates, :]

            real_0, real_1, imag_0, imag_1 = (load(c, o, 0) for c in range(2) for o in range(2))
            for shift in range(1, reach + 1):
                other_0, other_1 = load(0, 0, shift), load(0, 1, shift)
                turned_0, turned_1 = load(1, 0, shift), load(1, 1, shift)
                real = (real_0 * other_0 + imag_0 * turned_0) + (
                    real_1 * other_1 + imag_1 * turned_1
                )
                imaginary = (imag_0 * other_0 - real_0 * turned_0) + (
                    imag_1 * other_1 - real_1 * turned_1
                )
                at = (shift - 1) * dates
                for part, value in enumerate((real, imaginary)):
                    high, low = halves(value)
                    across = slice(
                        part * columns + side * LANES, part * columns + (side + 1) * LANES
                    )
                    pair_ref[half_row, at : at + dates, across] = high
                    pair_ref[half_row, pairs + at : pairs + at + dates, across] = low
        for part in range(2):
            summed = jnp.dot(
                weights[part],
                pair_ref[half_row, :, part * columns : (part + 1) * columns],
                preferred_element_type=F32,
            )
            high, low = halves(summed[:tall] + summed[tall:])
            at = (part * (rows // 2) + half_row) * tall
            sum_ref[0, at : at + tall, :] = high
            sum_ref[1, at : at + tall, :] = low
    looked = jnp.dot(sum_ref[0], look, preferred_element_type=F32)
    looked = looked + jnp.dot(sum_ref[1], look, preferred_element_type=F32)
    looked_ref[...] = looked
    for index in range(rows):
        one = looked[index * tall : (index + 1) * tall]
        to_right = jnp.where(
            lane == index, pltpu.roll(one, (index - looks) % LANES, 1), to_right
        )
        to_left = jnp.where(
            lane == index, pltpu.roll(one, (index - looks - 1) % LANES, 1), to_left
        )
    even = lax.rem(lax.axis_index("col"), 2) == 0
    first_ref[...] = jnp.where(even, to_right, to_left)
    second_ref[...] = jnp.where(even, to_left, to_right)


def finish_kernel(looked_ref, first_ref, second_ref, out_ref, sum_ref):
    times, parts, half_rows, looks = out_ref.shape
    tall = first_ref.shape[0]
    here, last = lax.axis_index("col"), lax.axis_size("col") - 1
    even = lax.rem(here, 2) == 0
    first, second = first_ref[...], second_ref[...]
    nothing = jnp.zeros_like(first)
    from_right = jnp.where(here == last, nothing, jnp.where(even, first, second))
    from_left = jnp.where(here == 0, nothing, jnp.where(even, second, first))
    lane = iota((tall, LANES), 1)
    for index in range(parts * half_rows):
        value = looked_ref[index * tall : (index + 1) * tall, :]
        value = value + jnp.where(
            lane == looks - 1, pltpu.roll(from_right, (looks - 1 - index) % LANES, 1), 0.0
        )
        value = value + jnp.where(lane == 0, pltpu.roll(from_left, -index % LANES, 1), 0.0)
        sum_ref[index * tall : (index + 1) * tall, :] = value
    for time in range(times):
        for part in range(parts):
            rows = sum_ref[pl.ds(part * half_rows * tall + time, half_rows, stride=tall), :]
            out_ref[time, part] = rows[:, :looks]


def column_swap(first, owners, count):
    moves = []
    for owner in range(owners):
        for column in range(count):
            partner = column + 1 if (column - first) % 2 == 0 else column - 1
            to = owner
            if not 0 <= partner < count:
                partner = column
                to = owner ^ 1 if owners % 2 == 0 else owner
            moves.append((owner * count + column, to * count + partner))
    return moves


def per_device(scenes, pair_dates, pair_count, inverse):
    owners, count = lax.axis_size("date"), lax.axis_size("col")
    dates_here, parts, all_rows, columns = scenes.shape
    half_rows = all_rows // owners // 2
    dates = owners * dates_here
    reach = dates // 2
    extent = round_up(dates + reach, 8)

    blocks, wide = cut(scenes, pair_dates.T, pair_count, inverse, owners)
    for step in range(1, owners):
        moves = [(owner, (owner - step) % owners) for owner in range(owners)]
        blocks[step] = lax.ppermute(blocks[step], "date", moves)

    tall = wide.shape[0]
    looked, first, second = pl.pallas_call(
        functools.partial(series_kernel, dates_here, pair_dates.shape[0]),
        out_shape=[
            pltpu.VMEM((parts * half_rows * tall, LANES), F32),
            pltpu.VMEM((tall, LANES), F32),
            pltpu.VMEM((tall, LANES), F32),
        ],
        in_specs=[IN_VMEM] * (owners + 1),
        out_specs=[IN_VMEM] * 3,
        scratch_shapes=[
            pltpu.VMEM((parts, columns // LANES, 2 * half_rows * extent, LANES), F32),
            pltpu.VMEM((half_rows, 2 * reach * dates, parts * columns), BF16),
            pltpu.VMEM((2, parts * half_rows * tall, columns), BF16),
        ],
        compiler_params=pltpu.CompilerParams(vmem_limit_bytes=40 << 20),
    )(*[held(block) for block in blocks[:1] + blocks[:0:-1]], held(wide))

    first = lax.ppermute(first, ("date", "col"), column_swap(0, owners, count))
    second = lax.ppermute(second, ("date", "col"), column_swap(1, owners, count))
    return pl.pallas_call(
        finish_kernel,
        out_shape=jax.ShapeDtypeStruct(
            (inverse.shape[0], parts, half_rows, columns // 8), F32
        ),
        in_specs=[IN_VMEM] * 3,
        out_specs=IN_VMEM,
        scratch_shapes=[pltpu.VMEM((parts * half_rows * tall, LANES), F32)],
    )(held(looked), held(first), held(second))


def solution(mesh):
    placed = (P("date", None, "groups", "col"), P("date", None), P("date"), P())
    return jax.shard_map(
        per_device,
        mesh=mesh,
        in_specs=placed,
        out_specs=P(None, None, ("groups", "date"), "col"),
        check_vma=False,
    )
```

```python
import functools

import jax
import jax.numpy as jnp
from jax import lax
from jax.experimental import pallas as pl
from jax.experimental.pallas import tpu as pltpu
from jax.sharding import PartitionSpec as P

F32, BF16 = jnp.float32, jnp.bfloat16
LANES = 128
NOTE_ROWS = 16
GROUP = 8
IN_VMEM = pl.BlockSpec(memory_space=pltpu.VMEM)
IN_SMEM = pl.BlockSpec(memory_space=pltpu.SMEM)


def round_up(value, step):
    return -(-value // step) * step


def held(array):
    return pltpu.with_memory_space_constraint(array, pltpu.VMEM)


def iota(shape, axis):
    return lax.broadcasted_iota(jnp.int32, shape, axis)


def halves(value):
    high = value.astype(BF16)
    return high, (value - high.astype(F32)).astype(BF16)


def note_of(pair_dates, count):
    slots = pair_dates.shape[1]
    dates = jnp.concatenate([pair_dates.astype(F32), jnp.zeros((2, LANES - slots), F32)], axis=1)
    row, lane = iota((NOTE_ROWS, LANES), 0), iota((NOTE_ROWS, LANES), 1)
    note = jnp.where((row == 2) & (lane < jnp.minimum(count, slots)), 1.0, 0.0)
    for side in range(2):
        note = jnp.where(row == side, dates[side : side + 1], note)
    return note.astype(BF16)


def cut_kernel(count_ref, scenes_ref, dates_ref, inverse_ref, *outs):
    *block_refs, wide_ref = outs
    owners = len(block_refs)
    me = lax.axis_index("date")
    rows = scenes_ref.shape[2] // owners
    note = note_of(dates_ref[...], count_ref[0])
    for step, block_ref in enumerate(block_refs):
        first = pl.multiple_of(lax.rem(me + owners - step, owners) * rows, rows)
        cells = scenes_ref[:, :, pl.ds(first, rows), :]
        height = block_ref.shape[0] - NOTE_ROWS
        block_ref[:height] = cells.reshape(height, block_ref.shape[1])
        block_ref[height:, :LANES] = note
    wide_ref[...] = jnp.zeros_like(wide_ref)
    wide_ref[: inverse_ref.shape[0], : inverse_ref.shape[1]] = inverse_ref[...]


def note_kernel(count_ref, dates_ref, inverse_ref, note_ref, wide_ref):
    note_ref[...] = jnp.zeros_like(note_ref)
    note_ref[:, :LANES] = note_of(dates_ref[...], count_ref[0])
    wide_ref[...] = jnp.zeros_like(wide_ref)
    wide_ref[: inverse_ref.shape[0], : inverse_ref.shape[1]] = inverse_ref[...]


def cut(scenes, pair_dates, pair_count, inverse, owners):
    dates_here, parts, all_rows, columns = scenes.shape
    rows = all_rows // owners
    height = dates_here * parts * rows
    wide = pltpu.VMEM(
        (round_up(inverse.shape[0], 16), round_up(inverse.shape[1], LANES)), F32
    )
    if rows % 16 == 0:
        *blocks, wide = pl.pallas_call(
            cut_kernel,
            out_shape=[pltpu.VMEM((height + NOTE_ROWS, columns), BF16)] * owners + [wide],
            in_specs=[IN_SMEM] + [IN_VMEM] * 3,
            out_specs=[IN_VMEM] * (owners + 1),
        )(pair_count, scenes, pair_dates, inverse)
        return blocks, wide
    note, wide = pl.pallas_call(
        note_kernel,
        out_shape=[pltpu.VMEM((NOTE_ROWS, columns), BF16), wide],
        in_specs=[IN_SMEM] + [IN_VMEM] * 2,
        out_specs=[IN_VMEM] * 2,
    )(pair_count, pair_dates, inverse)
    me = lax.axis_index("date")
    apart = scenes.reshape(dates_here * parts, owners, rows, columns)
    blocks = []
    for step in range(owners):
        cells = lax.dynamic_index_in_dim(apart, lax.rem(me + owners - step, owners), 1, False)
        blocks.append(jnp.concatenate([cells.reshape(height, columns), note], axis=0))
    return blocks, wide


def pair_places(first, second, dates):
    groups = dates // GROUP

    def group_of(date):
        return jnp.floor(date * (1.0 / GROUP))

    first_group, second_group = group_of(first), group_of(second)
    first_seat, second_seat = first - GROUP * first_group, second - GROUP * second_group
    ahead = second_seat - first_seat
    ahead = jnp.where(ahead < 0.0, ahead + GROUP, ahead)
    behind = jnp.where(ahead > 0.0, GROUP - ahead, 0.0)
    near = ahead <= GROUP // 2
    inside = first_group * (GROUP * GROUP // 2)
    inside = inside + jnp.where(
        near, (ahead - 1.0) * GROUP + first_seat, (behind - 1.0) * GROUP + second_seat
    )
    upward = first_group < second_group
    low, high = jnp.minimum(first_group, second_group), jnp.maximum(first_group, second_group)
    between = low * (2 * groups - 1.0 - low) * 0.5 + high - low - 1.0
    across = groups * (GROUP * GROUP // 2) + between * (GROUP * GROUP)
    across = across + jnp.where(
        upward, ahead * GROUP + first_seat, behind * GROUP + second_seat
    )
    same = first_group == second_group
    sign = jnp.where(same, jnp.where(near, 1.0, -1.0), jnp.where(upward, 1.0, -1.0))
    return jnp.where(same, inside, across), sign


def pair_weights(block_refs, wide, dates_here, slots):
    owners = len(block_refs)
    dates = owners * dates_here
    me = lax.axis_index("date")
    lanes = wide.shape[1]
    ring = jnp.zeros((8, lanes), F32)
    for step, block_ref in enumerate(block_refs):
        height = block_ref.shape[0]
        note = block_ref[height - NOTE_ROWS : height, :LANES].astype(F32)[:8]
        if lanes > LANES:
            note = jnp.concatenate([note, jnp.zeros((8, lanes - LANES), F32)], axis=1)
        ring = ring + pltpu.roll(note, lax.rem(me + step, owners) * slots, 1)
    start = lax.rem(me + owners - 1, owners) * dates_here
    start = jnp.full((1, lanes), start, jnp.int32).astype(F32)

    def wrapped(value):
        return jnp.where(value < 0.0, value + dates, value)

    place, sign = pair_places(wrapped(ring[0:1] - start), wrapped(ring[1:2] - start), dates)
    place = jnp.where(ring[2:3] > 0.5, place, -1.0)
    pairs = pair_rows(dates)
    chosen = jnp.where(iota((pairs, lanes), 0).astype(F32) == place, 1.0, 0.0).astype(BF16)
    scaled = wide * (1.0 / 128.0)
    signed = scaled * sign
    stacked = jnp.concatenate([*halves(scaled), *halves(signed)], axis=0)
    spread = lax.dot_general(
        stacked, chosen, (((1,), (1,)), ((), ())), preferred_element_type=F32
    )
    tall = wide.shape[0]
    weights = []
    for part in range(2):
        summed = spread[2 * part * tall : (2 * part + 1) * tall]
        summed = summed + spread[(2 * part + 1) * tall : (2 * part + 2) * tall]
        high, low = halves(summed)
        weights.append(
            jnp.concatenate(
                [jnp.concatenate([high, high], axis=1), jnp.concatenate([low, low], axis=1)], axis=0
            )
        )
    return weights


def pair_rows(dates):
    groups = dates // GROUP
    return GROUP * GROUP // 2 * groups + GROUP * GROUP * (groups * (groups - 1) // 2)


def pair_units(dates):
    groups = dates // GROUP
    half = GROUP // 2
    units = [(group, group, range(1, half + 1)) for group in range(groups)]
    for low in range(groups):
        for high in range(low + 1, groups):
            units += [(low, high, range(at, at + half)) for at in range(0, GROUP, half)]
    return units


def comb_of(columns):
    looks = columns // 8
    column, lane = iota((columns, columns), 0), iota((columns, columns), 1)
    here = (column // 8 == lane % looks) & (column % 8 == lane // looks)
    return jnp.where(here, 1.0, 0.0).astype(BF16)


def spread_block(block_ref, comb, dates_here, seat, rows_ref):
    height = block_ref.shape[0] - NOTE_ROWS
    rows = height // (2 * dates_here)
    combed = jnp.dot(block_ref[:height], comb, preferred_element_type=F32)
    for own in range(dates_here):
        for part in range(2):
            at = (own * 2 + part) * rows
            for side in range(rows_ref.shape[1]):
                rows_ref[part, side, pl.ds(seat + own, rows, stride=GROUP), :] = combed[
                    at : at + rows, side * LANES : (side + 1) * LANES
                ]


def pack_group(rows_ref, looks, half_rows, store):
    pack = LANES // looks
    lane = iota((GROUP, LANES), 1)
    for part in range(2):
        for odd in range(2):
            for tile in range(-(-half_rows // pack)):
                for side in range(rows_ref.shape[1]):
                    cells = []
                    for near in range(pack):
                        half_row = tile * pack + near
                        at = (2 * half_row + odd) * GROUP
                        if half_row < half_rows:
                            cells.append(rows_ref[part, side, at : at + GROUP, :])
                        else:
                            cells.append(jnp.zeros((GROUP, LANES), F32))
                    bit = pack // 2
                    while bit:
                        clear = (lane // looks) & bit == 0
                        for near in range(pack):
                            if not near & bit:
                                one, two = cells[near], cells[near + bit]
                                cells[near] = jnp.where(
                                    clear, one, pltpu.roll(two, bit * looks, 1)
                                )
                                cells[near + bit] = jnp.where(
                                    clear, pltpu.roll(one, LANES - bit * looks, 1), two
                                )
                        bit //= 2
                    for near in range(pack):
                        store(part, odd, side * pack + near, tile, cells[near])


def unit_products(tiles, looks, turns, mine_of, turned_of, store):
    lane = iota((GROUP, LANES), 1) % looks
    at_first, at_last = lane == 0, lane == looks - 1
    rims = [None] * (2 * len(turns))
    for tile in range(tiles):

        def product(place):
            mine = [[mine_of(part, odd, place, tile) for odd in range(2)] for part in range(2)]
            values = []
            for turn in turns:
                other = [
                    [turned_of(part, odd, place, tile, turn, mine) for odd in range(2)]
                    for part in range(2)
                ]
                real = (mine[0][0] * other[0][0] + mine[1][0] * other[1][0]) + (
                    mine[0][1] * other[0][1] + mine[1][1] * other[1][1]
                )
                imaginary = (mine[1][0] * other[0][0] - mine[0][0] * other[1][0]) + (
                    mine[1][1] * other[0][1] - mine[0][1] * other[1][1]
                )
                values += [real, imaginary]
            return values

        def running(places):
            total = product(places[0])
            ramp = total
            for place in places[1:]:
                total = [one + two for one, two in zip(total, product(place))]
                share = [0.5 * one for one in total] if place is places[-1] else total
                ramp = [one + two for one, two in zip(ramp, share)]
            return total, ramp

        early, to_left = running((0, 1, 2, 3))
        late, to_right = running((7, 6, 5, 4))
        values = []
        for index in range(len(early)):
            before = pltpu.roll(to_right[index], 1, 1)
            after = pltpu.roll(to_left[index], LANES - 1, 1)
            value = 8.0 * (early[index] + late[index]) - to_left[index] - to_right[index]
            value = value + jnp.where(at_first, 0.0, before) + jnp.where(at_last, 0.0, after)
            values.append(value)
            edge = jnp.where(at_first, before, jnp.where(at_last, after, 0.0))
            if tile:
                edge = rims[index] + pltpu.roll(edge, 2 * tile, 1)
            rims[index] = edge
        for part in range(2):
            store(part, tile, jnp.concatenate(values[part::2], axis=0))
    for part in range(2):
        store(part, tiles, jnp.concatenate(rims[part::2], axis=0))


def turn_here(part, odd, place, tile, turn, mine):
    return pltpu.roll(mine[part][odd], GROUP - turn, 0)


def early_kernel(dates_here, *refs):
    *block_refs, ring_ref, pair_ref, rows_ref = refs
    columns = block_refs[0].shape[1]
    looks = columns // 8
    tiles = ring_ref.shape[3]
    half_rows = rows_ref.shape[2] // GROUP // 2
    comb = comb_of(columns)
    for index, block_ref in enumerate(block_refs):
        spread_block(block_ref, comb, dates_here, index * dates_here, rows_ref)

    def keep(part, odd, place, tile, cells):
        ring_ref[part, odd, place, tile] = cells

    pack_group(rows_ref, looks, half_rows, keep)

    def store(part, tile, value):
        across = slice(tile * LANES, (tile + 1) * LANES)
        high, low = halves(value)
        pair_ref[part, 0, :, across] = high
        pair_ref[part, 1, :, across] = low

    unit_products(
        tiles,
        looks,
        range(1, GROUP // 2 + 1),
        lambda part, odd, place, tile: ring_ref[part, odd, place, tile],
        turn_here,
        store,
    )


def series_kernel(dates_here, slots, *refs):
    *refs, looked_ref, edge_ref, rows_ref, ring_ref, far_ref, pair_ref = refs
    *block_refs, wide_ref, first_ref, first_pair_ref = refs
    block_refs = block_refs[::-1]
    owners = len(block_refs)
    dates = owners * dates_here
    groups = dates // GROUP
    pairs = pair_rows(dates)
    columns = block_refs[0].shape[1]
    looks = columns // 8
    tiles = ring_ref.shape[4]
    half_rows = rows_ref.shape[2] // GROUP // 2
    tall = wide_ref.shape[0]
    together = GROUP // dates_here

    comb = comb_of(columns)
    for group in range(1, groups):
        for index in range(together):
            block_ref = block_refs[group * together + index - 1]
            spread_block(block_ref, comb, dates_here, index * dates_here, rows_ref)

        def keep(part, odd, place, tile, cells):
            ring_ref[group - 1, part, odd, place, tile] = cells
            for copy in range(2):
                at = pl.ds(2 * copy * GROUP + odd, GROUP, stride=2)
                far_ref[group - 1, part, place, tile, at, :] = cells

        pack_group(rows_ref, looks, half_rows, keep)

    weights = pair_weights(block_refs, wide_ref[...], dates_here, slots)

    across = first_pair_ref.shape[3]
    for part in range(2):
        for half in range(2):
            at = half * pairs
            pair_ref[part, at : at + first_pair_ref.shape[2], :across] = first_pair_ref[part, half]
    for unit, (low, high, turns) in enumerate(pair_units(dates)):
        if high == 0:
            continue

        def mine_of(part, odd, place, tile):
            if low == 0:
                return first_ref[part, odd, place, tile]
            return ring_ref[low - 1, part, odd, place, tile]

        def turn_far(part, odd, place, tile, turn, mine):
            at = pl.ds(2 * turn + odd, GROUP, stride=2)
            return far_ref[high - 1, part, place, tile, at, :]

        def store(part, tile, value):
            count = value.shape[0]
            across = slice(tile * LANES, (tile + 1) * LANES)
            bits = halves(value)
            for half in range(2):
                at = half * pairs + unit * count
                pair_ref[part, at : at + count, across] = bits[half]

        turned_of = turn_here if low == high else turn_far
        unit_products(tiles, looks, turns, mine_of, turned_of, store)
    message = jnp.zeros((tall, LANES), F32)
    for part in range(2):
        summed = jnp.dot(weights[part], pair_ref[part], preferred_element_type=F32)
        summed = summed[:tall] + summed[tall:]
        looked_ref[part] = summed[:, : tiles * LANES]
        edge = summed[:, tiles * LANES :]
        message = message + (pltpu.roll(edge, 2 * tiles, 1) if part else edge)
    edge_ref[...] = message


def finish_kernel(looked_ref, second_ref, first_ref, out_ref, sum_ref):
    times, parts, half_rows, looks = out_ref.shape
    tall = first_ref.shape[0]
    pack = LANES // looks
    tiles = looked_ref.shape[2] // LANES
    here, last = lax.axis_index("col"), lax.axis_size("col") - 1
    even = lax.rem(here, 2) == 0
    first, second = first_ref[...], second_ref[...]
    nothing = jnp.zeros_like(first)
    from_right = jnp.where(here == last, nothing, jnp.where(even, first, second))
    from_left = jnp.where(here == 0, nothing, jnp.where(even, second, first))
    lane = iota((tall, LANES), 1) % looks
    for part in range(parts):
        for tile in range(tiles):
            shift = 2 * (tile + tiles * part)
            value = looked_ref[part, :, tile * LANES : (tile + 1) * LANES]
            right = pltpu.roll(from_right, (looks - shift) % LANES, 1)
            left = pltpu.roll(from_left, (-looks - shift) % LANES, 1)
            value = value + jnp.where(lane == looks - 1, right, 0.0)
            value = value + jnp.where(lane == 0, left, 0.0)
            for near in range(min(pack, half_rows - tile * pack)):
                at = (part * half_rows + tile * pack + near) * tall
                sum_ref[at : at + tall, :] = pltpu.roll(value, -near * looks % LANES, 1)
    for time in range(times):
        for part in range(parts):
            rows = sum_ref[pl.ds(part * half_rows * tall + time, half_rows, stride=tall), :]
            out_ref[time, part] = rows[:, :looks]


def column_swap(first, owners, count):
    moves = []
    for owner in range(owners):
        for column in range(count):
            partner = column + 1 if (column - first) % 2 == 0 else column - 1
            to = owner
            if not 0 <= partner < count:
                partner = column
                to = owner ^ 1 if owners % 2 == 0 else owner
            moves.append((owner * count + column, to * count + partner))
    return moves


def per_device(scenes, pair_dates, pair_count, inverse):
    owners, count = lax.axis_size("date"), lax.axis_size("col")
    dates_here, parts, all_rows, columns = scenes.shape
    half_rows = all_rows // owners // 2
    dates = owners * dates_here
    pairs = pair_rows(dates)
    looks = columns // 8
    tiles = -(-half_rows // (LANES // looks))

    blocks, wide = cut(scenes, pair_dates.T, pair_count, inverse, owners)
    for step in range(1, owners):
        moves = [(owner, (owner - step) % owners) for owner in range(owners)]
        blocks[step] = lax.ppermute(blocks[step], "date", moves)

    tall = wide.shape[0]
    rows = 2 * half_rows
    sides = columns // LANES
    order = [blocks[(place - 1) % owners] for place in range(owners)]
    order = [held(block) for block in order]
    by_arrival = [held(block) for block in blocks[:0:-1] + blocks[:1]]
    group_rows = pltpu.VMEM((parts, sides, rows * GROUP, LANES), F32)
    first_group, first_pairs = pl.pallas_call(
        functools.partial(early_kernel, dates_here),
        out_shape=[
            pltpu.VMEM((parts, 2, 8, tiles, GROUP, LANES), F32),
            pltpu.VMEM((parts, 2, GROUP * GROUP // 2, (tiles + 1) * LANES), BF16),
        ],
        in_specs=[IN_VMEM] * (GROUP // dates_here),
        out_specs=[IN_VMEM] * 2,
        scratch_shapes=[group_rows],
        compiler_params=pltpu.CompilerParams(vmem_limit_bytes=40 << 20),
    )(*order[: GROUP // dates_here])
    others = dates // GROUP - 1
    looked, edge = pl.pallas_call(
        functools.partial(series_kernel, dates_here, pair_dates.shape[0]),
        out_shape=[
            pltpu.VMEM((parts, tall, tiles * LANES), F32),
            pltpu.VMEM((tall, LANES), F32),
        ],
        in_specs=[IN_VMEM] * (owners + 3),
        out_specs=[IN_VMEM] * 2,
        scratch_shapes=[
            group_rows,
            pltpu.VMEM((others, parts, 2, 8, tiles, GROUP, LANES), F32),
            pltpu.VMEM((others, parts, 8, tiles, 4 * GROUP, LANES), F32),
            pltpu.VMEM((parts, 2 * pairs, (tiles + 1) * LANES), BF16),
        ],
        compiler_params=pltpu.CompilerParams(vmem_limit_bytes=40 << 20),
    )(*by_arrival, held(wide), held(first_group), held(first_pairs))

    first = lax.ppermute(edge, ("date", "col"), column_swap(0, owners, count))
    second = lax.ppermute(edge, ("date", "col"), column_swap(1, owners, count))
    return pl.pallas_call(
        finish_kernel,
        out_shape=jax.ShapeDtypeStruct(
            (inverse.shape[0], parts, half_rows, columns // 8), F32
        ),
        in_specs=[IN_VMEM] * 3,
        out_specs=IN_VMEM,
        scratch_shapes=[pltpu.VMEM((parts * half_rows * tall, LANES), F32)],
    )(held(looked), held(second), held(first))


def solution(mesh):
    placed = (P("date", None, "groups", "col"), P("date", None), P("date"), P())
    return jax.shard_map(
        per_device,
        mesh=mesh,
        in_specs=placed,
        out_specs=P(None, None, ("groups", "date"), "col"),
        check_vma=False,
    )
```

```python
import functools

import jax
import jax.numpy as jnp
from jax import lax
from jax.experimental import pallas as pl
from jax.experimental.pallas import tpu as pltpu
from jax.sharding import PartitionSpec as P

F32, BF16 = jnp.float32, jnp.bfloat16
LANES = 128
NOTE_ROWS = 16
GROUP = 8
IN_VMEM = pl.BlockSpec(memory_space=pltpu.VMEM)
IN_SMEM = pl.BlockSpec(memory_space=pltpu.SMEM)


def round_up(value, step):
    return -(-value // step) * step


def held(array):
    return pltpu.with_memory_space_constraint(array, pltpu.VMEM)


def iota(shape, axis):
    return lax.broadcasted_iota(jnp.int32, shape, axis)


def halves(value):
    high = value.astype(BF16)
    return high, (value - high.astype(F32)).astype(BF16)


def comb_kernel(comb_ref, blank_ref):
    comb_ref[...] = comb_of(comb_ref.shape[0])
    blank_ref[...] = jnp.zeros_like(blank_ref)


def note_kernel(count_ref, dates_ref, blank_ref, note_ref):
    slots = dates_ref.shape[1]
    dates = dates_ref[...].astype(F32)
    dates = jnp.concatenate([dates, jnp.zeros((2, LANES - slots), F32)], axis=1)
    row, lane = iota((NOTE_ROWS, LANES), 0), iota((NOTE_ROWS, LANES), 1)
    note = jnp.where((row == 2) & (lane < jnp.minimum(count_ref[0], slots)), 1.0, 0.0)
    for side in range(2):
        note = jnp.where(row == side, dates[side : side + 1], note)
    note_ref[...] = blank_ref[...]
    note_ref[:, :LANES] = note.astype(BF16)


def cut_kernel(scenes_ref, note_ref, *block_refs):
    owners = len(block_refs)
    me = lax.axis_index("date")
    rows = scenes_ref.shape[2] // owners
    for step, block_ref in enumerate(block_refs):
        first = pl.multiple_of(lax.rem(me + owners - step, owners) * rows, rows)
        cells = scenes_ref[:, :, pl.ds(first, rows), :]
        height = block_ref.shape[0] - NOTE_ROWS
        block_ref[:height] = cells.reshape(height, block_ref.shape[1])
        block_ref[height:] = note_ref[...]


def cut(scenes, pair_dates, pair_count, owners):
    dates_here, parts, all_rows, columns = scenes.shape
    rows = all_rows // owners
    height = dates_here * parts * rows
    comb, blank = pl.pallas_call(
        comb_kernel,
        out_shape=[pltpu.VMEM((columns, columns), BF16), pltpu.VMEM((NOTE_ROWS, columns), BF16)],
        out_specs=[IN_VMEM] * 2,
        cost_estimate=pl.CostEstimate(flops=10**9, bytes_accessed=10**7, transcendentals=0),
    )()
    note = pl.pallas_call(
        note_kernel,
        out_shape=pltpu.VMEM((NOTE_ROWS, columns), BF16),
        in_specs=[IN_SMEM] + [IN_VMEM] * 2,
        out_specs=IN_VMEM,
    )(pair_count, held(pair_dates), held(blank))
    if rows % 16 == 0:
        blocks = pl.pallas_call(
            cut_kernel,
            out_shape=[pltpu.VMEM((height + NOTE_ROWS, columns), BF16)] * owners,
            in_specs=[IN_VMEM] * 2,
            out_specs=[IN_VMEM] * owners,
        )(held(scenes), held(note))
        return list(blocks), comb
    me = lax.axis_index("date")
    apart = scenes.reshape(dates_here * parts, owners, rows, columns)
    blocks = []
    for step in range(owners):
        cells = lax.dynamic_index_in_dim(apart, lax.rem(me + owners - step, owners), 1, False)
        blocks.append(jnp.concatenate([cells.reshape(height, columns), note], axis=0))
    return blocks, comb


def pair_places(first, second, dates):
    groups = dates // GROUP

    def group_of(date):
        return jnp.floor(date * (1.0 / GROUP))

    first_group, second_group = group_of(first), group_of(second)
    first_seat, second_seat = first - GROUP * first_group, second - GROUP * second_group
    ahead = second_seat - first_seat
    ahead = jnp.where(ahead < 0.0, ahead + GROUP, ahead)
    behind = jnp.where(ahead > 0.0, GROUP - ahead, 0.0)
    near = ahead <= GROUP // 2
    inside = first_group * (GROUP * GROUP // 2)
    inside = inside + jnp.where(
        near, (ahead - 1.0) * GROUP + first_seat, (behind - 1.0) * GROUP + second_seat
    )
    upward = first_group < second_group
    low, high = jnp.minimum(first_group, second_group), jnp.maximum(first_group, second_group)
    between = low * (2 * groups - 1.0 - low) * 0.5 + high - low - 1.0
    across = groups * (GROUP * GROUP // 2) + between * (GROUP * GROUP)
    across = across + jnp.where(
        upward, ahead * GROUP + first_seat, behind * GROUP + second_seat
    )
    same = first_group == second_group
    sign = jnp.where(same, jnp.where(near, 1.0, -1.0), jnp.where(upward, 1.0, -1.0))
    return jnp.where(same, inside, across), sign


def pair_weights(block_refs, wide, dates_here, slots):
    owners = len(block_refs)
    dates = owners * dates_here
    me = lax.axis_index("date")
    lanes = wide.shape[1]
    ring = jnp.zeros((8, lanes), F32)
    for step, block_ref in enumerate(block_refs):
        height = block_ref.shape[0]
        note = block_ref[height - NOTE_ROWS : height, :LANES].astype(F32)[:8]
        if lanes > LANES:
            note = jnp.concatenate([note, jnp.zeros((8, lanes - LANES), F32)], axis=1)
        ring = ring + pltpu.roll(note, lax.rem(me + step, owners) * slots, 1)
    start = lax.rem(me + owners - 1, owners) * dates_here
    start = jnp.full((1, lanes), start, jnp.int32).astype(F32)

    def wrapped(value):
        return jnp.where(value < 0.0, value + dates, value)

    place, sign = pair_places(wrapped(ring[0:1] - start), wrapped(ring[1:2] - start), dates)
    place = jnp.where(ring[2:3] > 0.5, place, -1.0)
    pairs = pair_rows(dates)
    chosen = jnp.where(iota((pairs, lanes), 0).astype(F32) == place, 1.0, 0.0).astype(BF16)
    scaled = wide * (1.0 / 128.0)
    signed = scaled * sign
    stacked = jnp.concatenate([*halves(scaled), *halves(signed)], axis=0)
    spread = lax.dot_general(
        stacked, chosen, (((1,), (1,)), ((), ())), preferred_element_type=F32
    )
    tall = wide.shape[0]
    weights = []
    for part in range(2):
        summed = spread[2 * part * tall : (2 * part + 1) * tall]
        summed = summed + spread[(2 * part + 1) * tall : (2 * part + 2) * tall]
        high, low = halves(summed)
        weights.append(
            jnp.concatenate(
                [jnp.concatenate([high, high], axis=1), jnp.concatenate([low, low], axis=1)], axis=0
            )
        )
    return weights


def pair_rows(dates):
    groups = dates // GROUP
    return GROUP * GROUP // 2 * groups + GROUP * GROUP * (groups * (groups - 1) // 2)


def pair_units(dates):
    groups = dates // GROUP
    half = GROUP // 2
    units = [(group, group, range(1, half + 1)) for group in range(groups)]
    for low in range(groups):
        for high in range(low + 1, groups):
            units += [(low, high, range(at, at + half)) for at in range(0, GROUP, half)]
    return units


def comb_of(columns):
    looks = columns // 8
    column, lane = iota((columns, columns), 0), iota((columns, columns), 1)
    here = (column // 8 == lane % looks) & (column % 8 == lane // looks)
    return jnp.where(here, 1.0, 0.0).astype(BF16)


def spread_block(block_ref, comb, dates_here, seat, rows_ref):
    height = block_ref.shape[0] - NOTE_ROWS
    rows = height // (2 * dates_here)
    combed = jnp.dot(block_ref[:height], comb, preferred_element_type=F32)
    for own in range(dates_here):
        for part in range(2):
            at = (own * 2 + part) * rows
            for side in range(rows_ref.shape[1]):
                rows_ref[part, side, pl.ds(seat + own, rows, stride=GROUP), :] = combed[
                    at : at + rows, side * LANES : (side + 1) * LANES
                ]


def pack_group(rows_ref, looks, half_rows, store):
    pack = LANES // looks
    lane = iota((GROUP, LANES), 1)
    for part in range(2):
        for odd in range(2):
            for tile in range(-(-half_rows // pack)):
                for side in range(rows_ref.shape[1]):
                    cells = []
                    for near in range(pack):
                        half_row = tile * pack + near
                        at = (2 * half_row + odd) * GROUP
                        if half_row < half_rows:
                            cells.append(rows_ref[part, side, at : at + GROUP, :])
                        else:
                            cells.append(jnp.zeros((GROUP, LANES), F32))
                    bit = pack // 2
                    while bit:
                        clear = (lane // looks) & bit == 0
                        for near in range(pack):
                            if not near & bit:
                                one, two = cells[near], cells[near + bit]
                                cells[near] = jnp.where(
                                    clear, one, pltpu.roll(two, bit * looks, 1)
                                )
                                cells[near + bit] = jnp.where(
                                    clear, pltpu.roll(one, LANES - bit * looks, 1), two
                                )
                        bit //= 2
                    for near in range(pack):
                        store(part, odd, side * pack + near, tile, cells[near])


def unit_products(tiles, looks, turns, mine_of, turned_of, store):
    lane = iota((GROUP, LANES), 1) % looks
    at_first, at_last = lane == 0, lane == looks - 1
    for tile in range(tiles):

        def product(place):
            mine = [[mine_of(part, odd, place, tile) for odd in range(2)] for part in range(2)]
            values = []
            for turn in turns:
                other = [
                    [turned_of(part, odd, place, tile, turn, mine) for odd in range(2)]
                    for part in range(2)
                ]
                real = (mine[0][0] * other[0][0] + mine[1][0] * other[1][0]) + (
                    mine[0][1] * other[0][1] + mine[1][1] * other[1][1]
                )
                imaginary = (mine[1][0] * other[0][0] - mine[0][0] * other[1][0]) + (
                    mine[1][1] * other[0][1] - mine[0][1] * other[1][1]
                )
                values += [real, imaginary]
            return values

        def running(places):
            total = product(places[0])
            ramp = total
            for place in places[1:]:
                total = [one + two for one, two in zip(total, product(place))]
                share = [0.5 * one for one in total] if place is places[-1] else total
                ramp = [one + two for one, two in zip(ramp, share)]
            return total, ramp

        early, to_left = running((0, 1, 2, 3))
        late, to_right = running((7, 6, 5, 4))
        values = []
        for index in range(len(early)):
            before = pltpu.roll(to_right[index], 1, 1)
            after = pltpu.roll(to_left[index], LANES - 1, 1)
            value = 8.0 * (early[index] + late[index]) - to_left[index] - to_right[index]
            value = value + jnp.where(at_first, 0.0, before) + jnp.where(at_last, 0.0, after)
            values.append(value)
        for part in range(2):
            store(part, tile, jnp.concatenate(values[part::2], axis=0))


def turn_here(part, odd, place, tile, turn, mine):
    return pltpu.roll(mine[part][odd], GROUP - turn, 0)


def seam_of(block_ref, dates_here, seat, seam_ref):
    height = block_ref.shape[0] - NOTE_ROWS
    columns = block_ref.shape[1]
    rows = height // (2 * dates_here)
    column, lane = iota((columns, LANES), 0), iota((columns, LANES), 1) % 8
    wanted = jnp.where(lane < 4, lane, columns - 8 + lane)
    pick = jnp.where(column == wanted, 1.0, 0.0).astype(BF16)
    cells = jnp.dot(block_ref[:height], pick, preferred_element_type=F32)
    row, lane = iota((height, LANES), 0), iota((height, LANES), 1)
    cells = jnp.where(row % rows == lane // 8, cells, 0.0).astype(BF16)
    line, row = iota((16, height), 0), iota((16, height), 1) // rows
    gather = jnp.where((line < 2 * dates_here) & (row == line % dates_here * 2 + line // dates_here), 1.0, 0.0)
    lines = jnp.dot(gather.astype(BF16), cells, preferred_element_type=F32)
    for part in range(2):
        seam_ref[part, seat : seat + dates_here, :] = lines[
            part * dates_here : (part + 1) * dates_here
        ]


def early_kernel(dates_here, *refs):
    comb_ref, *block_refs, ring_ref, pair_ref, seam_ref, rows_ref = refs
    columns = block_refs[0].shape[1]
    looks = columns // 8
    tiles = ring_ref.shape[3]
    half_rows = rows_ref.shape[2] // GROUP // 2
    comb = comb_ref[...]
    for index, block_ref in enumerate(block_refs):
        spread_block(block_ref, comb, dates_here, index * dates_here, rows_ref)
        seam_of(block_ref, dates_here, index * dates_here, seam_ref)

    def keep(part, odd, place, tile, cells):
        ring_ref[part, odd, place, tile] = cells

    pack_group(rows_ref, looks, half_rows, keep)

    def store(part, tile, value):
        across = slice(tile * LANES, (tile + 1) * LANES)
        high, low = halves(value)
        pair_ref[part, 0, :, across] = high
        pair_ref[part, 1, :, across] = low

    unit_products(
        tiles,
        looks,
        range(1, GROUP // 2 + 1),
        lambda part, odd, place, tile: ring_ref[part, odd, place, tile],
        turn_here,
        store,
    )


def edge_kernel(dates_here, slots, *refs):
    *refs, weights_ref, message_ref, wide_ref, seams_ref, pair_ref = refs
    *block_refs, inverse_ref, seam_ref = refs
    block_refs = block_refs[::-1]
    owners = len(block_refs)
    dates = owners * dates_here
    groups = dates // GROUP
    pairs = pair_rows(dates)
    together = GROUP // dates_here
    tall = wide_ref.shape[0]

    for group in range(1, groups):
        for index in range(together):
            block_ref = block_refs[group * together + index - 1]
            seam_of(block_ref, dates_here, index * dates_here, seams_ref.at[group - 1])
    wide_ref[...] = jnp.zeros_like(wide_ref)
    wide_ref[: inverse_ref.shape[0], : inverse_ref.shape[1]] = inverse_ref[...]
    weights = pair_weights(block_refs, wide_ref[...], dates_here, slots)
    for part in range(2):
        weights_ref[part] = weights[part]

    lane = iota((GROUP, LANES), 1) % 8
    ramp = jnp.where(lane < 4, 3.5 - lane.astype(F32), lane.astype(F32) - 3.5)
    for unit, (low, high, turns) in enumerate(pair_units(dates)):
        mine = [(seams_ref[low - 1, part] if low else seam_ref[part]) * ramp for part in range(2)]
        theirs = [seams_ref[high - 1, part] if high else seam_ref[part] for part in range(2)]
        values = []
        for turn in turns:
            other = [pltpu.roll(cells, GROUP - turn, 0) if turn else cells for cells in theirs]
            values.append(mine[0] * other[0] + mine[1] * other[1])
            values.append(mine[1] * other[0] - mine[0] * other[1])
        for part in range(2):
            value = jnp.concatenate(values[part::2], axis=0)
            count = value.shape[0]
            bits = halves(value)
            for half in range(2):
                at = half * pairs + unit * count
                pair_ref[part, at : at + count, :] = bits[half]
    sums = []
    for part in range(2):
        summed = jnp.dot(weights[part], pair_ref[part], preferred_element_type=F32)
        summed = summed[:tall] + summed[tall:]
        for shift in (1, 2, 8):
            summed = summed + pltpu.roll(summed, LANES - shift, 1)
        sums.append(summed)
    lane = iota((tall, LANES), 1)
    message_ref[...] = jnp.where(lane % 4 == 1, pltpu.roll(sums[1], 1, 1), sums[0])


def series_kernel(dates_here, *refs):
    *refs, looked_ref, rows_ref, ring_ref, far_ref, pair_ref = refs
    *block_refs, comb_ref, weights_ref, first_ref, first_pair_ref = refs
    block_refs = block_refs[::-1]
    groups = 1 + ring_ref.shape[0]
    dates = groups * GROUP
    pairs = pair_rows(dates)
    columns = block_refs[0].shape[1]
    looks = columns // 8
    tiles = ring_ref.shape[4]
    half_rows = rows_ref.shape[2] // GROUP // 2
    tall = looked_ref.shape[1]
    together = GROUP // dates_here

    comb = comb_ref[...]
    for group in range(1, groups):
        for index in range(together):
            block_ref = block_refs[(group - 1) * together + index]
            spread_block(block_ref, comb, dates_here, index * dates_here, rows_ref)

        def keep(part, odd, place, tile, cells):
            ring_ref[group - 1, part, odd, place, tile] = cells
            for copy in range(2):
                at = pl.ds(2 * copy * GROUP + odd, GROUP, stride=2)
                far_ref[group - 1, part, place, tile, at, :] = cells

        pack_group(rows_ref, looks, half_rows, keep)

    for part in range(2):
        for half in range(2):
            at = half * pairs
            pair_ref[part, at : at + first_pair_ref.shape[2], :] = first_pair_ref[part, half]
    for unit, (low, high, turns) in enumerate(pair_units(dates)):
        if high == 0:
            continue

        def mine_of(part, odd, place, tile):
            if low == 0:
                return first_ref[part, odd, place, tile]
            return ring_ref[low - 1, part, odd, place, tile]

        def turn_far(part, odd, place, tile, turn, mine):
            at = pl.ds(2 * turn + odd, GROUP, stride=2)
            return far_ref[high - 1, part, place, tile, at, :]

        def store(part, tile, value):
            count = value.shape[0]
            across = slice(tile * LANES, (tile + 1) * LANES)
            bits = halves(value)
            for half in range(2):
                at = half * pairs + unit * count
                pair_ref[part, at : at + count, across] = bits[half]

        turned_of = turn_here if low == high else turn_far
        unit_products(tiles, looks, turns, mine_of, turned_of, store)
    for part in range(2):
        summed = jnp.dot(weights_ref[part], pair_ref[part], preferred_element_type=F32)
        looked_ref[part] = summed[:tall] + summed[tall:]


def finish_kernel(looked_ref, second_ref, first_ref, out_ref, sum_ref):
    times, parts, half_rows, looks = out_ref.shape
    tall = first_ref.shape[0]
    pack = LANES // looks
    here, last = lax.axis_index("col"), lax.axis_size("col") - 1
    even = lax.rem(here, 2) == 0
    first, second = first_ref[...], second_ref[...]
    nothing = jnp.zeros_like(first)
    from_right = jnp.where(here == last, nothing, jnp.where(even, first, second))
    from_left = jnp.where(here == 0, nothing, jnp.where(even, second, first))
    lane = iota((tall, LANES), 1)
    for part in range(parts):
        for half_row in range(half_rows):
            tile, near = half_row // pack, half_row % pack
            value = looked_ref[part, :, tile * LANES : (tile + 1) * LANES]
            value = pltpu.roll(value, -near * looks % LANES, 1)
            at = 16 * half_row + part
            right = pltpu.roll(from_right, (looks - 1 - at) % LANES, 1)
            left = pltpu.roll(from_left, (-4 - at) % LANES, 1)
            value = value + jnp.where(lane == looks - 1, right, 0.0)
            value = value + jnp.where(lane == 0, left, 0.0)
            at = (part * half_rows + half_row) * tall
            sum_ref[at : at + tall, :] = value
    for time in range(times):
        for part in range(parts):
            rows = sum_ref[pl.ds(part * half_rows * tall + time, half_rows, stride=tall), :]
            out_ref[time, part] = rows[:, :looks]


def column_swap(first, owners, count):
    moves = []
    for owner in range(owners):
        for column in range(count):
            partner = column + 1 if (column - first) % 2 == 0 else column - 1
            to = owner
            if not 0 <= partner < count:
                partner = column
                to = owner ^ 1 if owners % 2 == 0 else owner
            moves.append((owner * count + column, to * count + partner))
    return moves


def per_device(scenes, pair_dates, pair_count, inverse):
    owners, count = lax.axis_size("date"), lax.axis_size("col")
    dates_here, parts, all_rows, columns = scenes.shape
    half_rows = all_rows // owners // 2
    dates = owners * dates_here
    pairs = pair_rows(dates)
    looks = columns // 8
    tiles = -(-half_rows // (LANES // looks))

    blocks, comb = cut(scenes, pair_dates.T, pair_count, owners)
    for step in range(1, owners):
        moves = [(owner, (owner - step) % owners) for owner in range(owners)]
        blocks[step] = lax.ppermute(blocks[step], "date", moves)

    tall = round_up(inverse.shape[0], 16)
    rows = 2 * half_rows
    sides = columns // LANES
    order = [blocks[(place - 1) % owners] for place in range(owners)]
    order = [held(block) for block in order]
    by_arrival = [held(block) for block in blocks[:0:-1] + blocks[:1]]
    group_rows = pltpu.VMEM((parts, sides, rows * GROUP, LANES), F32)
    first_group, first_pairs, first_seam = pl.pallas_call(
        functools.partial(early_kernel, dates_here),
        out_shape=[
            pltpu.VMEM((parts, 2, 8, tiles, GROUP, LANES), F32),
            pltpu.VMEM((parts, 2, GROUP * GROUP // 2, tiles * LANES), BF16),
            pltpu.VMEM((parts, GROUP, LANES), F32),
        ],
        in_specs=[IN_VMEM] * (GROUP // dates_here + 1),
        out_specs=[IN_VMEM] * 3,
        scratch_shapes=[group_rows],
        compiler_params=pltpu.CompilerParams(vmem_limit_bytes=40 << 20),
    )(held(comb), *order[: GROUP // dates_here])
    others = dates // GROUP - 1
    weights, edge = pl.pallas_call(
        functools.partial(edge_kernel, dates_here, pair_dates.shape[0]),
        out_shape=[
            pltpu.VMEM((parts, 2 * tall, 2 * pairs), BF16),
            pltpu.VMEM((tall, LANES), F32),
        ],
        in_specs=[IN_VMEM] * (owners + 2),
        out_specs=[IN_VMEM] * 2,
        scratch_shapes=[
            pltpu.VMEM((tall, round_up(inverse.shape[1], LANES)), F32),
            pltpu.VMEM((others, parts, GROUP, LANES), F32),
            pltpu.VMEM((parts, 2 * pairs, LANES), BF16),
        ],
        compiler_params=pltpu.CompilerParams(vmem_limit_bytes=40 << 20),
    )(*by_arrival, held(inverse), held(first_seam))
    late = [held(block) for block in order[GROUP // dates_here :]][::-1]
    looked = pl.pallas_call(
        functools.partial(series_kernel, dates_here),
        out_shape=pltpu.VMEM((parts, tall, tiles * LANES), F32),
        in_specs=[IN_VMEM] * (len(late) + 4),
        out_specs=IN_VMEM,
        scratch_shapes=[
            group_rows,
            pltpu.VMEM((others, parts, 2, 8, tiles, GROUP, LANES), F32),
            pltpu.VMEM((others, parts, 8, tiles, 4 * GROUP, LANES), F32),
            pltpu.VMEM((parts, 2 * pairs, tiles * LANES), BF16),
        ],
        compiler_params=pltpu.CompilerParams(vmem_limit_bytes=40 << 20),
        cost_estimate=pl.CostEstimate(
            flops=2 * parts * pairs * columns * rows * 8, bytes_accessed=1 << 20, transcendentals=0
        ),
    )(*late, held(comb), held(weights), held(first_group), held(first_pairs))

    first = lax.ppermute(edge, ("date", "col"), column_swap(0, owners, count))
    second = lax.ppermute(edge, ("date", "col"), column_swap(1, owners, count))
    return pl.pallas_call(
        finish_kernel,
        out_shape=jax.ShapeDtypeStruct(
            (inverse.shape[0], parts, half_rows, columns // 8), F32
        ),
        in_specs=[IN_VMEM] * 3,
        out_specs=IN_VMEM,
        scratch_shapes=[pltpu.VMEM((parts * half_rows * tall, LANES), F32)],
    )(held(looked), held(second), held(first))


def solution(mesh):
    placed = (P("date", None, "groups", "col"), P("date", None), P("date"), P())
    return jax.shard_map(
        per_device,
        mesh=mesh,
        in_specs=placed,
        out_specs=P(None, None, ("groups", "date"), "col"),
        check_vma=False,
    )
```

```python
import functools

import jax
import jax.numpy as jnp
from jax import lax
from jax.experimental import pallas as pl
from jax.experimental.pallas import tpu as pltpu
from jax.sharding import PartitionSpec as P

F32, BF16 = jnp.float32, jnp.bfloat16
LANES = 128
NOTE = 8
NOTE_ROWS = 2 * NOTE
GROUP = 8
ANYWHERE = pl.BlockSpec(memory_space=pl.ANY)
IN_VMEM = pl.BlockSpec(memory_space=pltpu.VMEM)
IN_SMEM = pl.BlockSpec(memory_space=pltpu.SMEM)


def round_up(value, step):
    return -(-value // step) * step


def held(array):
    return pltpu.with_memory_space_constraint(array, pltpu.VMEM)


def iota(shape, axis):
    return lax.broadcasted_iota(jnp.int32, shape, axis)


def halves(value):
    high = value.astype(BF16)
    return high, (value - high.astype(F32)).astype(BF16)


def blank_kernel(blank_ref):
    blank_ref[...] = jnp.zeros_like(blank_ref)


def comb_of(columns):
    looks = columns // 8
    column, lane = iota((columns, columns), 0), iota((columns, columns), 1)
    here = (column // 8 == lane % looks) & (column % 8 == lane // looks)
    return jnp.where(here, 1.0, 0.0).astype(BF16)


def fold_of(shape, looks, half_rows):
    cell, target = iota(shape, 0), iota(shape, 1)
    right = cell < LANES
    cell = cell % LANES
    half_row = cell // 16
    here = right & (cell % 8 < 4) & (target == half_row * looks + looks - 1)
    here = here | ~right & (cell % 8 >= 4) & (target == half_row * looks)
    return jnp.where(here & (half_row < half_rows), 1.0, 0.0).astype(BF16)


def live_kernel(slots, count_ref, blank_ref, live_ref):
    row, lane = iota(live_ref.shape, 0), iota(live_ref.shape, 1)
    live = (row == 2) & (lane < jnp.minimum(count_ref[0], slots))
    live_ref[...] = jnp.where(live, 1.0, blank_ref[...])


def seam_kernel(scenes_ref, dates_ref, live_ref, seams_ref, note_ref, fetched_ref, semaphore):
    fetch = pltpu.make_async_copy(dates_ref, fetched_ref, semaphore)
    fetch.start()
    dates_here, parts, all_rows, columns = scenes_ref.shape
    owners = seams_ref.shape[0]
    rows = all_rows // owners
    height = dates_here * parts * all_rows
    column, lane = iota((columns, LANES), 0), iota((columns, LANES), 1) % 8
    wanted = jnp.where(lane < 4, lane, columns - 8 + lane)
    pick = jnp.where(column == wanted, 1.0, 0.0).astype(BF16)
    cells = scenes_ref[...].reshape(height, columns)
    cells = jnp.dot(cells, pick, preferred_element_type=F32)
    row, lane = iota((height, LANES), 0), iota((height, LANES), 1)
    cells = jnp.where(row % rows == lane // 8, cells, 0.0).astype(BF16)
    line, row = iota((owners * NOTE, height), 0), iota((owners * NOTE, height), 1) // rows
    place = line % NOTE
    wanted = (place % dates_here * parts + place // dates_here) * owners + line // NOTE
    gather = jnp.where((place < parts * dates_here) & (row == wanted), 1.0, 0.0).astype(BF16)
    lines = jnp.dot(gather, cells, preferred_element_type=F32)
    for owner in range(owners):
        seams_ref[owner] = lines[owner * NOTE : (owner + 1) * NOTE]
    note_ref[...] = live_ref[...]
    fetch.wait()
    note_ref[:2, : dates_ref.shape[1]] = fetched_ref[...].astype(F32)


def twin_of(owner, owners):
    return owner + 1 - 2 * (owner % 2) if owners % 2 == 0 else owner


def cut_kernel(scenes_ref, note_ref, seams_ref, *block_refs):
    owners = len(block_refs)
    me = lax.axis_index("date")
    rows = scenes_ref.shape[2] // owners
    sides = scenes_ref.shape[3] // LANES
    for step, block_ref in enumerate(block_refs):
        owner = lax.rem(me + owners - step, owners)
        first = pl.multiple_of(owner * rows, rows)
        height = (block_ref.shape[0] - NOTE_ROWS) // sides
        for side in range(sides):
            cells = scenes_ref[:, :, pl.ds(first, rows), side * LANES : (side + 1) * LANES]
            block_ref[side * height : (side + 1) * height] = cells.reshape(height, LANES)
        seam = seams_ref[twin_of(owner, owners)]
        block_ref[sides * height :] = jnp.concatenate([note_ref[...], seam], axis=0).astype(BF16)


def cells_of(block_ref, sides):
    height = (block_ref.shape[0] - NOTE_ROWS) // sides
    return jnp.concatenate(
        [block_ref[side * height : (side + 1) * height] for side in range(sides)], axis=1
    )


def cut(scenes, pair_dates, pair_count, owners):
    dates_here, parts, all_rows, columns = scenes.shape
    rows = all_rows // owners
    sides = columns // LANES
    height = dates_here * parts * rows
    blank = pl.pallas_call(
        blank_kernel,
        out_shape=pltpu.VMEM((NOTE, LANES), F32),
        out_specs=IN_VMEM,
        cost_estimate=pl.CostEstimate(flops=10**9, bytes_accessed=10**7, transcendentals=0),
    )()
    live = pl.pallas_call(
        functools.partial(live_kernel, pair_dates.shape[1]),
        out_shape=pltpu.VMEM((NOTE, LANES), F32),
        in_specs=[IN_SMEM, IN_VMEM],
        out_specs=IN_VMEM,
    )(pair_count, held(blank))
    seams, note = pl.pallas_call(
        seam_kernel,
        out_shape=[pltpu.VMEM((owners, NOTE, LANES), F32), pltpu.VMEM((NOTE, LANES), F32)],
        in_specs=[IN_VMEM, ANYWHERE, IN_VMEM],
        out_specs=[IN_VMEM] * 2,
        scratch_shapes=[pltpu.VMEM(pair_dates.shape, jnp.int32), pltpu.SemaphoreType.DMA],
    )(held(scenes), pair_dates, held(live))
    if rows % 16 == 0:
        blocks = pl.pallas_call(
            cut_kernel,
            out_shape=[pltpu.VMEM((sides * height + NOTE_ROWS, LANES), BF16)] * owners,
            in_specs=[IN_VMEM] * 3,
            out_specs=[IN_VMEM] * owners,
        )(held(scenes), held(note), held(seams))
        return list(blocks)
    me = lax.axis_index("date")
    apart = scenes.reshape(dates_here * parts, owners, rows, columns)
    blocks = []
    for step in range(owners):
        owner = lax.rem(me + owners - step, owners)
        cells = lax.dynamic_index_in_dim(apart, owner, 1, False).reshape(height, columns)
        strips = [cells[:, side * LANES : (side + 1) * LANES] for side in range(sides)]
        seam = lax.dynamic_index_in_dim(seams, twin_of(owner, owners), 0, False)
        strips += [note.astype(BF16), seam.astype(BF16)]
        blocks.append(jnp.concatenate(strips, axis=0))
    return blocks


def pair_places(first, second, dates):
    groups = dates // GROUP

    def group_of(date):
        return jnp.floor(date * (1.0 / GROUP))

    first_group, second_group = group_of(first), group_of(second)
    first_seat, second_seat = first - GROUP * first_group, second - GROUP * second_group
    ahead = second_seat - first_seat
    ahead = jnp.where(ahead < 0.0, ahead + GROUP, ahead)
    behind = jnp.where(ahead > 0.0, GROUP - ahead, 0.0)
    near = ahead <= GROUP // 2
    inside = first_group * (GROUP * GROUP // 2)
    inside = inside + jnp.where(
        near, (ahead - 1.0) * GROUP + first_seat, (behind - 1.0) * GROUP + second_seat
    )
    upward = first_group < second_group
    low, high = jnp.minimum(first_group, second_group), jnp.maximum(first_group, second_group)
    between = low * (2 * groups - 1.0 - low) * 0.5 + high - low - 1.0
    across = groups * (GROUP * GROUP // 2) + between * (GROUP * GROUP)
    across = across + jnp.where(
        upward, ahead * GROUP + first_seat, behind * GROUP + second_seat
    )
    same = first_group == second_group
    sign = jnp.where(same, jnp.where(near, 1.0, -1.0), jnp.where(upward, 1.0, -1.0))
    return jnp.where(same, inside, across), sign


def inverse_of(wide, step, owners, slots):
    lanes = wide.shape[1]
    owner = lax.rem(lax.axis_index("date") + step, owners)
    moved = pltpu.roll(wide, lax.rem(lanes - owner * slots, lanes), 1)
    return moved[:, :LANES] * (1.0 / 128.0)


def slot_weights(block_ref, inverse, owners, dates_here):
    dates = owners * dates_here
    start = lax.rem(lax.axis_index("date") + owners - 1, owners) * dates_here
    start = jnp.full((1, LANES), start, jnp.int32).astype(F32)
    height = block_ref.shape[0]
    note = block_ref[height - NOTE_ROWS : height].astype(F32)

    def wrapped(value):
        return jnp.where(value < 0.0, value + dates, value)

    place, sign = pair_places(wrapped(note[0:1] - start), wrapped(note[1:2] - start), dates)
    place = jnp.where(note[2:3] > 0.5, place, -1.0)
    pairs = pair_rows(dates)
    chosen = jnp.where(iota((pairs, LANES), 0).astype(F32) == place, 1.0, 0.0).astype(BF16)
    stacked = jnp.concatenate([*halves(inverse), *halves(inverse * sign)], axis=0)
    spread = lax.dot_general(
        stacked, chosen, (((1,), (1,)), ((), ())), preferred_element_type=F32
    )
    tall = inverse.shape[0]
    parts = [spread[at * tall : (at + 1) * tall] for at in range(4)]
    return parts[0] + parts[1], parts[2] + parts[3]


def pair_rows(dates):
    groups = dates // GROUP
    return GROUP * GROUP // 2 * groups + GROUP * GROUP * (groups * (groups - 1) // 2)


def pair_units(dates):
    groups = dates // GROUP
    half = GROUP // 2
    units = [(group, group, range(1, half + 1)) for group in range(groups)]
    for low in range(groups):
        for high in range(low + 1, groups):
            units += [(low, high, range(at, at + half)) for at in range(0, GROUP, half)]
    return units


def spread_block(block_ref, comb, dates_here, seat, rows_ref):
    sides = rows_ref.shape[1]
    combed = jnp.dot(cells_of(block_ref, sides), comb, preferred_element_type=F32)
    rows = combed.shape[0] // (2 * dates_here)
    for own in range(dates_here):
        for part in range(2):
            at = (own * 2 + part) * rows
            for side in range(sides):
                rows_ref[part, side, pl.ds(seat + own, rows, stride=GROUP), :] = combed[
                    at : at + rows, side * LANES : (side + 1) * LANES
                ]


def pack_group(rows_ref, looks, half_rows, store):
    pack = LANES // looks
    lane = iota((GROUP, LANES), 1)
    for part in range(2):
        for odd in range(2):
            for tile in range(-(-half_rows // pack)):
                for side in range(rows_ref.shape[1]):
                    cells = []
                    for near in range(pack):
                        half_row = tile * pack + near
                        at = (2 * half_row + odd) * GROUP
                        if half_row < half_rows:
                            cells.append(rows_ref[part, side, at : at + GROUP, :])
                        else:
                            cells.append(jnp.zeros((GROUP, LANES), F32))
                    bit = pack // 2
                    while bit:
                        clear = (lane // looks) & bit == 0
                        for near in range(pack):
                            if not near & bit:
                                one, two = cells[near], cells[near + bit]
                                cells[near] = jnp.where(
                                    clear, one, pltpu.roll(two, bit * looks, 1)
                                )
                                cells[near + bit] = jnp.where(
                                    clear, pltpu.roll(one, LANES - bit * looks, 1), two
                                )
                        bit //= 2
                    for near in range(pack):
                        store(part, odd, side * pack + near, tile, cells[near])


def unit_products(tiles, looks, turns, mine_of, turned_of, store):
    lane = iota((GROUP, LANES), 1) % looks
    at_first, at_last = lane == 0, lane == looks - 1
    for tile in range(tiles):

        def product(place):
            mine = [[mine_of(part, odd, place, tile) for odd in range(2)] for part in range(2)]
            values = []
            for turn in turns:
                other = [
                    [turned_of(part, odd, place, tile, turn, mine) for odd in range(2)]
                    for part in range(2)
                ]
                real = (mine[0][0] * other[0][0] + mine[1][0] * other[1][0]) + (
                    mine[0][1] * other[0][1] + mine[1][1] * other[1][1]
                )
                imaginary = (mine[1][0] * other[0][0] - mine[0][0] * other[1][0]) + (
                    mine[1][1] * other[0][1] - mine[0][1] * other[1][1]
                )
                values += [real, imaginary]
            return values

        def running(places):
            total = product(places[0])
            ramp = total
            for place in places[1:]:
                total = [one + two for one, two in zip(total, product(place))]
                share = [0.5 * one for one in total] if place is places[-1] else total
                ramp = [one + two for one, two in zip(ramp, share)]
            return total, ramp

        early, to_left = running((0, 1, 2, 3))
        late, to_right = running((7, 6, 5, 4))
        values = []
        for index in range(len(early)):
            before = pltpu.roll(to_right[index], 1, 1)
            after = pltpu.roll(to_left[index], LANES - 1, 1)
            value = 8.0 * (early[index] + late[index]) - to_left[index] - to_right[index]
            value = value + jnp.where(at_first, 0.0, before) + jnp.where(at_last, 0.0, after)
            values.append(value)
        for part in range(2):
            store(part, tile, jnp.concatenate(values[part::2], axis=0))


def turn_here(part, odd, place, tile, turn, mine):
    return pltpu.roll(mine[part][odd], GROUP - turn, 0)


def seam_of(block_ref, dates_here, seat, seam_ref):
    height = block_ref.shape[0]
    lines = block_ref[height - NOTE_ROWS : height].astype(F32)
    for part in range(2):
        at = NOTE + part * dates_here
        seam_ref[part, seat : seat + dates_here, :] = lines[at : at + dates_here]


def early_kernel(dates_here, *refs):
    *block_refs, comb_ref, fold_ref, ring_ref, pair_ref, seam_ref, rows_ref = refs
    columns = comb_ref.shape[0]
    looks = columns // 8
    tiles = ring_ref.shape[3]
    half_rows = rows_ref.shape[2] // GROUP // 2
    comb = comb_of(columns)
    comb_ref[...] = comb
    fold_ref[...] = fold_of(fold_ref.shape, looks, half_rows)
    for index, block_ref in enumerate(block_refs):
        spread_block(block_ref, comb, dates_here, index * dates_here, rows_ref)
        seam_of(block_ref, dates_here, index * dates_here, seam_ref)

    def keep(part, odd, place, tile, cells):
        ring_ref[part, odd, place, tile] = cells

    pack_group(rows_ref, looks, half_rows, keep)

    def store(part, tile, value):
        across = slice(tile * LANES, (tile + 1) * LANES)
        high, low = halves(value)
        pair_ref[part, 0, :, across] = high
        pair_ref[part, 1, :, across] = low

    unit_products(
        tiles,
        looks,
        range(1, GROUP // 2 + 1),
        lambda part, odd, place, tile: ring_ref[part, odd, place, tile],
        turn_here,
        store,
    )


def place_of(step, owners, dates_here):
    date = (step + 1) % owners * dates_here
    return date // GROUP, date % GROUP


def middle_kernel(dates_here, slots, steps, *refs):
    *refs, rows_ref, seams_ref, partial_ref, rest_ref, wide_ref = refs
    comb_ref, inverse_ref, *block_refs = refs
    owners = len(block_refs) + 1
    comb = comb_ref[...]
    wide_ref[...] = jnp.zeros_like(wide_ref)
    wide_ref[: inverse_ref.shape[0], : inverse_ref.shape[1]] = inverse_ref[...]
    wide = wide_ref[...]
    sums = [0.0, 0.0]
    for step, block_ref in zip(steps, block_refs):
        group, seat = place_of(step, owners, dates_here)
        if group:
            spread_block(block_ref, comb, dates_here, seat, rows_ref.at[group - 1])
            seam_of(block_ref, dates_here, seat, seams_ref.at[group - 1])
        more = slot_weights(block_ref, inverse_of(wide, step, owners, slots), owners, dates_here)
        sums = [one + two for one, two in zip(sums, more)]
    for part in range(2):
        partial_ref[part] = sums[part]
    rest_ref[...] = inverse_of(wide, 1, owners, slots)


def edge_kernel(dates_here, owners, *refs):
    block_ref, seam_ref, others_ref, partial_ref, rest_ref, *refs = refs
    weights_ref, message_ref, seams_ref, pair_ref = refs
    dates = owners * dates_here
    pairs = pair_rows(dates)
    tall = rest_ref.shape[0]

    seams_ref[...] = others_ref[...]
    group, seat = place_of(1, owners, dates_here)
    seam_of(block_ref, dates_here, seat, seams_ref.at[group - 1])
    weights = []
    for part, more in enumerate(slot_weights(block_ref, rest_ref[...], owners, dates_here)):
        high, low = halves(partial_ref[part] + more)
        wide = [jnp.concatenate([half, half], axis=1) for half in (high, low)]
        weights.append(jnp.concatenate(wide, axis=0))
        weights_ref[part] = weights[part]

    lane = iota((GROUP, LANES), 1) % 8
    ramp = jnp.where(lane < 4, 3.5 - lane.astype(F32), lane.astype(F32) - 3.5)
    for unit, (low, high, turns) in enumerate(pair_units(dates)):
        mine = [(seams_ref[low - 1, part] if low else seam_ref[part]) * ramp for part in range(2)]
        theirs = [seams_ref[high - 1, part] if high else seam_ref[part] for part in range(2)]
        values = []
        for turn in turns:
            other = [pltpu.roll(cells, GROUP - turn, 0) if turn else cells for cells in theirs]
            values.append(mine[0] * other[0] + mine[1] * other[1])
            values.append(mine[1] * other[0] - mine[0] * other[1])
        for part in range(2):
            value = jnp.concatenate(values[part::2], axis=0)
            count = value.shape[0]
            bits = halves(value)
            for half in range(2):
                at = half * pairs + unit * count
                pair_ref[part, at : at + count, :] = bits[half]
    for part in range(2):
        summed = jnp.dot(weights[part], pair_ref[part], preferred_element_type=F32)
        message_ref[part * tall : (part + 1) * tall] = summed[:tall] + summed[tall:]


def series_kernel(dates_here, *refs):
    *refs, looked_ref, rows_ref, ring_ref, far_ref, pair_ref = refs
    block_ref, comb_ref, weights_ref, first_ref, first_pair_ref, others_ref = refs
    groups = 1 + ring_ref.shape[0]
    dates = groups * GROUP
    pairs = pair_rows(dates)
    columns = comb_ref.shape[0]
    looks = columns // 8
    tiles = ring_ref.shape[4]
    half_rows = rows_ref.shape[3] // GROUP // 2
    tall = looked_ref.shape[1]

    rows_ref[...] = others_ref[...]
    last_group, seat = place_of(1, dates // dates_here, dates_here)
    spread_block(block_ref, comb_ref[...], dates_here, seat, rows_ref.at[last_group - 1])
    for group in range(1, groups):

        def keep(part, odd, place, tile, cells):
            ring_ref[group - 1, part, odd, place, tile] = cells
            for copy in range(2):
                at = pl.ds(2 * copy * GROUP + odd, GROUP, stride=2)
                far_ref[group - 1, part, place, tile, at, :] = cells

        pack_group(rows_ref.at[group - 1], looks, half_rows, keep)

    for part in range(2):
        for half in range(2):
            at = half * pairs
            pair_ref[part, at : at + first_pair_ref.shape[2], :] = first_pair_ref[part, half]
    for unit, (low, high, turns) in enumerate(pair_units(dates)):
        if high == 0:
            continue

        def mine_of(part, odd, place, tile):
            if low == 0:
                return first_ref[part, odd, place, tile]
            return ring_ref[low - 1, part, odd, place, tile]

        def turn_far(part, odd, place, tile, turn, mine):
            at = pl.ds(2 * turn + odd, GROUP, stride=2)
            return far_ref[high - 1, part, place, tile, at, :]

        def store(part, tile, value):
            count = value.shape[0]
            across = slice(tile * LANES, (tile + 1) * LANES)
            bits = halves(value)
            for half in range(2):
                at = half * pairs + unit * count
                pair_ref[part, at : at + count, across] = bits[half]

        turned_of = turn_here if low == high else turn_far
        unit_products(tiles, looks, turns, mine_of, turned_of, store)
    for part in range(2):
        summed = jnp.dot(weights_ref[part], pair_ref[part], preferred_element_type=F32)
        looked_ref[part] = summed[:tall] + summed[tall:]


def finish_kernel(looked_ref, fold_ref, second_ref, first_ref, out_ref, sum_ref):
    times, parts, half_rows, looks = out_ref.shape
    tall = looked_ref.shape[1]
    pack = LANES // looks
    here, last = lax.axis_index("col"), lax.axis_size("col") - 1
    even = lax.rem(here, 2) == 0
    first, second = first_ref[...], second_ref[...]
    nothing = jnp.zeros_like(first)
    from_right = jnp.where(here == last, nothing, jnp.where(even, first, second))
    from_left = jnp.where(here == 0, nothing, jnp.where(even, second, first))
    edges = jnp.concatenate(halves(jnp.concatenate([from_right, from_left], axis=1)), axis=0)
    edges = jnp.dot(edges, fold_ref[...], preferred_element_type=F32)
    edges = edges[: parts * tall] + edges[parts * tall :]
    for part in range(parts):
        value = looked_ref[part] + edges[part * tall : (part + 1) * tall]
        for half_row in range(half_rows):
            tile, near = half_row // pack, half_row % pack
            one = value[:, tile * LANES : (tile + 1) * LANES]
            at = (part * half_rows + half_row) * tall
            sum_ref[at : at + tall, :] = pltpu.roll(one, -near * looks % LANES, 1)
    for time in range(times):
        for part in range(parts):
            rows = sum_ref[pl.ds(part * half_rows * tall + time, half_rows, stride=tall), :]
            out_ref[time, part] = rows[:, :looks]


def column_swap(first, owners, count):
    moves = []
    for owner in range(owners):
        for column in range(count):
            partner = column + 1 if (column - first) % 2 == 0 else column - 1
            partner = partner if 0 <= partner < count else column
            moves.append((owner * count + column, twin_of(owner, owners) * count + partner))
    return moves


def per_device(scenes, pair_dates, pair_count, inverse):
    owners, count = lax.axis_size("date"), lax.axis_size("col")
    dates_here, parts, all_rows, columns = scenes.shape
    half_rows = all_rows // owners // 2
    dates = owners * dates_here
    pairs = pair_rows(dates)
    looks = columns // 8
    tiles = -(-half_rows // (LANES // looks))

    blocks = cut(scenes, pair_dates.T, pair_count, owners)
    for step in range(1, owners):
        moves = [(owner, (owner - step) % owners) for owner in range(owners)]
        blocks[step] = lax.ppermute(blocks[step], "date", moves)

    tall = round_up(inverse.shape[0], 16)
    rows = 2 * half_rows
    sides = columns // LANES
    order = [blocks[(place - 1) % owners] for place in range(owners)]
    order = [held(block) for block in order]
    group_rows = pltpu.VMEM((parts, sides, rows * GROUP, LANES), F32)
    comb, fold, first_group, first_pairs, first_seam = pl.pallas_call(
        functools.partial(early_kernel, dates_here),
        out_shape=[
            pltpu.VMEM((columns, columns), BF16),
            pltpu.VMEM((2 * LANES, tiles * LANES), BF16),
            pltpu.VMEM((parts, 2, 8, tiles, GROUP, LANES), F32),
            pltpu.VMEM((parts, 2, GROUP * GROUP // 2, tiles * LANES), BF16),
            pltpu.VMEM((parts, GROUP, LANES), F32),
        ],
        in_specs=[IN_VMEM] * (GROUP // dates_here),
        out_specs=[IN_VMEM] * 5,
        scratch_shapes=[group_rows],
        compiler_params=pltpu.CompilerParams(vmem_limit_bytes=40 << 20),
    )(*order[: GROUP // dates_here])
    others = dates // GROUP - 1
    steps = [*range(owners - 1, 1, -1), 0]
    group_rows = pltpu.VMEM((others, *group_rows.shape), F32)
    other_rows, other_seams, partial, rest = pl.pallas_call(
        functools.partial(middle_kernel, dates_here, pair_dates.shape[0], steps),
        out_shape=[
            group_rows,
            pltpu.VMEM((others, parts, GROUP, LANES), F32),
            pltpu.VMEM((parts, tall, pairs), F32),
            pltpu.VMEM((tall, LANES), F32),
        ],
        in_specs=[IN_VMEM] * (owners + 1),
        out_specs=[IN_VMEM] * 4,
        scratch_shapes=[pltpu.VMEM((tall, round_up(inverse.shape[1], LANES)), F32)],
        compiler_params=pltpu.CompilerParams(vmem_limit_bytes=40 << 20),
    )(held(comb), held(inverse), *[held(blocks[step]) for step in steps])
    weights, edge = pl.pallas_call(
        functools.partial(edge_kernel, dates_here, owners),
        out_shape=[
            pltpu.VMEM((parts, 2 * tall, 2 * pairs), BF16),
            pltpu.VMEM((parts * tall, LANES), F32),
        ],
        in_specs=[IN_VMEM] * 5,
        out_specs=[IN_VMEM] * 2,
        scratch_shapes=[
            pltpu.VMEM((others, parts, GROUP, LANES), F32),
            pltpu.VMEM((parts, 2 * pairs, LANES), BF16),
        ],
        compiler_params=pltpu.CompilerParams(vmem_limit_bytes=40 << 20),
    )(*[held(array) for array in (blocks[1], first_seam, other_seams, partial, rest)])
    looked = pl.pallas_call(
        functools.partial(series_kernel, dates_here),
        out_shape=pltpu.VMEM((parts, tall, tiles * LANES), F32),
        in_specs=[IN_VMEM] * 6,
        out_specs=IN_VMEM,
        scratch_shapes=[
            group_rows,
            pltpu.VMEM((others, parts, 2, 8, tiles, GROUP, LANES), F32),
            pltpu.VMEM((others, parts, 8, tiles, 4 * GROUP, LANES), F32),
            pltpu.VMEM((parts, 2 * pairs, tiles * LANES), BF16),
        ],
        compiler_params=pltpu.CompilerParams(vmem_limit_bytes=40 << 20),
        cost_estimate=pl.CostEstimate(
            flops=2 * parts * pairs * columns * rows * 8, bytes_accessed=1 << 20, transcendentals=0
        ),
    )(*[held(one) for one in (blocks[1], comb, weights, first_group, first_pairs, other_rows)])

    first = lax.ppermute(edge, ("date", "col"), column_swap(0, owners, count))
    second = lax.ppermute(edge, ("date", "col"), column_swap(1, owners, count))
    return pl.pallas_call(
        finish_kernel,
        out_shape=jax.ShapeDtypeStruct(
            (inverse.shape[0], parts, half_rows, columns // 8), F32
        ),
        in_specs=[IN_VMEM] * 4,
        out_specs=IN_VMEM,
        scratch_shapes=[pltpu.VMEM((parts * half_rows * tall, LANES), F32)],
    )(held(looked), held(fold), held(second), held(first))


def solution(mesh):
    placed = (P("date", None, "groups", "col"), P("date", None), P("date"), P())
    return jax.shard_map(
        per_device,
        mesh=mesh,
        in_specs=placed,
        out_specs=P(None, None, ("groups", "date"), "col"),
        check_vma=False,
    )
```

```python
import functools

import jax
import jax.numpy as jnp
from jax import lax
from jax.experimental import pallas as pl
from jax.experimental.pallas import tpu as pltpu
from jax.sharding import PartitionSpec as P

F32, BF16 = jnp.float32, jnp.bfloat16
LANES = 128
NOTE = 8
NOTE_ROWS = 2 * NOTE
GROUP = 8
ANYWHERE = pl.BlockSpec(memory_space=pl.ANY)
IN_VMEM = pl.BlockSpec(memory_space=pltpu.VMEM)
IN_SMEM = pl.BlockSpec(memory_space=pltpu.SMEM)


def round_up(value, step):
    return -(-value // step) * step


def held(array):
    return pltpu.with_memory_space_constraint(array, pltpu.VMEM)


def iota(shape, axis):
    return lax.broadcasted_iota(jnp.int32, shape, axis)


def halves(value):
    high = value.astype(BF16)
    return high, (value - high.astype(F32)).astype(BF16)


def blank_kernel(blank_ref):
    blank_ref[...] = jnp.zeros_like(blank_ref)


def comb_of(columns):
    looks = columns // 8
    column, lane = iota((columns, columns), 0), iota((columns, columns), 1)
    here = (column // 8 == lane % looks) & (column % 8 == lane // looks)
    return jnp.where(here, 1.0, 0.0).astype(BF16)


def fold_of(shape, looks, half_rows):
    cell, target = iota(shape, 0), iota(shape, 1)
    right = cell < LANES
    cell = cell % LANES
    half_row = cell // 16
    here = right & (target == half_row * looks + looks - 1)
    here = here | ~right & (target == half_row * looks)
    return jnp.where(here & (half_row < half_rows), 1.0, 0.0).astype(BF16)


def note_kernel(rows, count_ref, dates_ref, blank_ref, *refs):
    note_ref, pick_ref, own_ref, gather_ref, fetched_ref, semaphore = refs
    fetch = pltpu.make_async_copy(dates_ref, fetched_ref, semaphore)
    fetch.start()
    columns, (all_rows, lanes), (lines, height) = pick_ref.shape[0], own_ref.shape, gather_ref.shape
    column, lane = iota((columns, lanes), 0), iota((columns, lanes), 1) % 8
    wanted = jnp.where(lane < 4, lane, columns - 8 + lane)
    pick_ref[...] = jnp.where(column == wanted, 1.0, 0.0).astype(BF16)
    row, lane = iota((all_rows, lanes), 0), iota((all_rows, lanes), 1)
    own_ref[...] = jnp.where(row % rows == lane // 8, 1.0, 0.0)
    owners, images = all_rows // rows, height // all_rows
    line, row = iota((lines, height), 0), iota((lines, height), 1) // rows
    place = line % NOTE
    wanted = (place % (images // 2) * 2 + place // (images // 2)) * owners + line // NOTE
    gather_ref[...] = jnp.where((place < images) & (row == wanted), 1.0, 0.0).astype(BF16)
    row, lane = iota(note_ref.shape, 0), iota(note_ref.shape, 1)
    slots = dates_ref.shape[1]
    live = (row == 2) & (lane < jnp.minimum(count_ref[0], slots))
    note_ref[...] = jnp.where(live, 1.0, blank_ref[...])
    fetch.wait()
    note_ref[:2, :slots] = fetched_ref[...].astype(F32)


def seam_kernel(scenes_ref, pick_ref, own_ref, gather_ref, seams_ref):
    dates_here, parts, all_rows, columns = scenes_ref.shape
    height = dates_here * parts * all_rows
    cells = scenes_ref[...].reshape(height, columns)
    cells = jnp.dot(cells, pick_ref[...], preferred_element_type=F32)
    cells = cells.reshape(dates_here * parts, all_rows, LANES) * own_ref[...][None]
    cells = cells.reshape(height, LANES).astype(BF16)
    lines = jnp.dot(gather_ref[...], cells, preferred_element_type=F32)
    for owner in range(seams_ref.shape[0]):
        seams_ref[owner] = lines[owner * NOTE : (owner + 1) * NOTE]


def twin_of(owner, owners):
    return owner + 1 - 2 * (owner % 2) if owners % 2 == 0 else owner


def cut_kernel(scenes_ref, note_ref, seams_ref, *block_refs):
    owners = len(block_refs)
    me = lax.axis_index("date")
    rows = scenes_ref.shape[2] // owners
    sides = scenes_ref.shape[3] // LANES
    for step, block_ref in enumerate(block_refs):
        owner = lax.rem(me + owners - step, owners)
        first = pl.multiple_of(owner * rows, rows)
        height = (block_ref.shape[0] - NOTE_ROWS) // sides
        for side in range(sides):
            cells = scenes_ref[:, :, pl.ds(first, rows), side * LANES : (side + 1) * LANES]
            block_ref[side * height : (side + 1) * height] = cells.reshape(height, LANES)
        seam = seams_ref[twin_of(owner, owners)]
        block_ref[sides * height :] = jnp.concatenate([note_ref[...], seam], axis=0).astype(BF16)


def cells_of(block_ref, sides):
    height = (block_ref.shape[0] - NOTE_ROWS) // sides
    return jnp.concatenate(
        [block_ref[side * height : (side + 1) * height] for side in range(sides)], axis=1
    )


def cut(scenes, pair_dates, pair_count, owners):
    dates_here, parts, all_rows, columns = scenes.shape
    rows = all_rows // owners
    sides = columns // LANES
    height = dates_here * parts * rows
    blank = pl.pallas_call(
        blank_kernel,
        out_shape=pltpu.VMEM((NOTE, LANES), F32),
        out_specs=IN_VMEM,
        cost_estimate=pl.CostEstimate(flops=10**9, bytes_accessed=10**7, transcendentals=0),
    )()
    note, pick, own, gather = pl.pallas_call(
        functools.partial(note_kernel, rows),
        out_shape=[
            pltpu.VMEM((NOTE, LANES), F32),
            pltpu.VMEM((columns, LANES), BF16),
            pltpu.VMEM((all_rows, LANES), F32),
            pltpu.VMEM((owners * NOTE, dates_here * parts * all_rows), BF16),
        ],
        in_specs=[IN_SMEM, ANYWHERE, IN_VMEM],
        out_specs=[IN_VMEM] * 4,
        scratch_shapes=[pltpu.VMEM(pair_dates.shape, jnp.int32), pltpu.SemaphoreType.DMA],
    )(pair_count, pair_dates, held(blank))
    seams = pl.pallas_call(
        seam_kernel,
        out_shape=pltpu.VMEM((owners, NOTE, LANES), F32),
        in_specs=[IN_VMEM] * 4,
        out_specs=IN_VMEM,
    )(held(scenes), held(pick), held(own), held(gather))
    if rows % 16 == 0:
        blocks = pl.pallas_call(
            cut_kernel,
            out_shape=[pltpu.VMEM((sides * height + NOTE_ROWS, LANES), BF16)] * owners,
            in_specs=[IN_VMEM] * 3,
            out_specs=[IN_VMEM] * owners,
        )(held(scenes), held(note), held(seams))
        return list(blocks)
    me = lax.axis_index("date")
    apart = scenes.reshape(dates_here * parts, owners, rows, columns)
    blocks = []
    for step in range(owners):
        owner = lax.rem(me + owners - step, owners)
        cells = lax.dynamic_index_in_dim(apart, owner, 1, False).reshape(height, columns)
        strips = [cells[:, side * LANES : (side + 1) * LANES] for side in range(sides)]
        seam = lax.dynamic_index_in_dim(seams, twin_of(owner, owners), 0, False)
        strips += [note.astype(BF16), seam.astype(BF16)]
        blocks.append(jnp.concatenate(strips, axis=0))
    return blocks


def pair_places(first, second, dates):
    groups = dates // GROUP

    def group_of(date):
        return jnp.floor(date * (1.0 / GROUP))

    first_group, second_group = group_of(first), group_of(second)
    first_seat, second_seat = first - GROUP * first_group, second - GROUP * second_group
    ahead = second_seat - first_seat
    ahead = jnp.where(ahead < 0.0, ahead + GROUP, ahead)
    behind = jnp.where(ahead > 0.0, GROUP - ahead, 0.0)
    near = ahead <= GROUP // 2
    inside = first_group * (GROUP * GROUP // 2)
    inside = inside + jnp.where(
        near, (ahead - 1.0) * GROUP + first_seat, (behind - 1.0) * GROUP + second_seat
    )
    upward = first_group < second_group
    low, high = jnp.minimum(first_group, second_group), jnp.maximum(first_group, second_group)
    between = low * (2 * groups - 1.0 - low) * 0.5 + high - low - 1.0
    across = groups * (GROUP * GROUP // 2) + between * (GROUP * GROUP)
    across = across + jnp.where(
        upward, ahead * GROUP + first_seat, behind * GROUP + second_seat
    )
    same = first_group == second_group
    sign = jnp.where(same, jnp.where(near, 1.0, -1.0), jnp.where(upward, 1.0, -1.0))
    return jnp.where(same, inside, across), sign


def inverse_of(wide, step, owners, slots):
    lanes = wide.shape[1]
    owner = lax.rem(lax.axis_index("date") + step, owners)
    moved = pltpu.roll(wide, lax.rem(lanes - owner * slots, lanes), 1)
    return moved[:, :LANES] * (1.0 / 128.0)


def slot_weights(block_ref, inverse, owners, dates_here):
    dates = owners * dates_here
    start = lax.rem(lax.axis_index("date") + owners - 1, owners) * dates_here
    start = jnp.full((1, LANES), start, jnp.int32).astype(F32)
    height = block_ref.shape[0]
    note = block_ref[height - NOTE_ROWS : height].astype(F32)

    def wrapped(value):
        return jnp.where(value < 0.0, value + dates, value)

    place, sign = pair_places(wrapped(note[0:1] - start), wrapped(note[1:2] - start), dates)
    place = jnp.where(note[2:3] > 0.5, place, -1.0)
    pairs = pair_rows(dates)
    chosen = jnp.where(iota((pairs, LANES), 0).astype(F32) == place, 1.0, 0.0).astype(BF16)
    stacked = jnp.concatenate([*halves(inverse), *halves(inverse * sign)], axis=0)
    spread = lax.dot_general(
        stacked, chosen, (((1,), (1,)), ((), ())), preferred_element_type=F32
    )
    tall = inverse.shape[0]
    parts = [spread[at * tall : (at + 1) * tall] for at in range(4)]
    return parts[0] + parts[1], parts[2] + parts[3]


def pair_rows(dates):
    groups = dates // GROUP
    return GROUP * GROUP // 2 * groups + GROUP * GROUP * (groups * (groups - 1) // 2)


def pair_units(dates):
    groups = dates // GROUP
    half = GROUP // 2
    units = [(group, group, range(1, half + 1)) for group in range(groups)]
    for low in range(groups):
        for high in range(low + 1, groups):
            units += [(low, high, range(at, at + half)) for at in range(0, GROUP, half)]
    return units


def spread_block(block_ref, comb, dates_here, seat, rows_ref):
    sides = rows_ref.shape[1]
    combed = jnp.dot(cells_of(block_ref, sides), comb, preferred_element_type=F32)
    rows = combed.shape[0] // (2 * dates_here)
    for own in range(dates_here):
        for part in range(2):
            at = (own * 2 + part) * rows
            for side in range(sides):
                rows_ref[part, side, pl.ds(seat + own, rows, stride=GROUP), :] = combed[
                    at : at + rows, side * LANES : (side + 1) * LANES
                ]


def pack_group(rows_ref, looks, half_rows, store):
    pack = LANES // looks
    lane = iota((GROUP, LANES), 1)
    for part in range(2):
        for odd in range(2):
            for tile in range(-(-half_rows // pack)):
                for side in range(rows_ref.shape[1]):
                    cells = []
                    for near in range(pack):
                        half_row = tile * pack + near
                        at = (2 * half_row + odd) * GROUP
                        if half_row < half_rows:
                            cells.append(rows_ref[part, side, at : at + GROUP, :])
                        else:
                            cells.append(jnp.zeros((GROUP, LANES), F32))
                    bit = pack // 2
                    while bit:
                        clear = (lane // looks) & bit == 0
                        for near in range(pack):
                            if not near & bit:
                                one, two = cells[near], cells[near + bit]
                                cells[near] = jnp.where(
                                    clear, one, pltpu.roll(two, bit * looks, 1)
                                )
                                cells[near + bit] = jnp.where(
                                    clear, pltpu.roll(one, LANES - bit * looks, 1), two
                                )
                        bit //= 2
                    for near in range(pack):
                        store(part, odd, side * pack + near, tile, cells[near])


def unit_products(tiles, looks, turns, mine_of, turned_of, store):
    lane = iota((GROUP, LANES), 1) % looks
    at_first, at_last = lane == 0, lane == looks - 1
    for tile in range(tiles):

        def product(place):
            mine = [[mine_of(part, odd, place, tile) for odd in range(2)] for part in range(2)]
            values = []
            for turn in turns:
                other = [
                    [turned_of(part, odd, place, tile, turn, mine) for odd in range(2)]
                    for part in range(2)
                ]
                real = (mine[0][0] * other[0][0] + mine[1][0] * other[1][0]) + (
                    mine[0][1] * other[0][1] + mine[1][1] * other[1][1]
                )
                imaginary = (mine[1][0] * other[0][0] - mine[0][0] * other[1][0]) + (
                    mine[1][1] * other[0][1] - mine[0][1] * other[1][1]
                )
                values += [real, imaginary]
            return values

        def running(places):
            total = product(places[0])
            ramp = total
            for place in places[1:]:
                total = [one + two for one, two in zip(total, product(place))]
                share = [0.5 * one for one in total] if place is places[-1] else total
                ramp = [one + two for one, two in zip(ramp, share)]
            return total, ramp

        early, to_left = running((0, 1, 2, 3))
        late, to_right = running((7, 6, 5, 4))
        values = []
        for index in range(len(early)):
            before = pltpu.roll(to_right[index], 1, 1)
            after = pltpu.roll(to_left[index], LANES - 1, 1)
            value = 8.0 * (early[index] + late[index]) - to_left[index] - to_right[index]
            value = value + jnp.where(at_first, 0.0, before) + jnp.where(at_last, 0.0, after)
            values.append(value)
        for part in range(2):
            store(part, tile, jnp.concatenate(values[part::2], axis=0))


def turn_here(part, odd, place, tile, turn, mine):
    return pltpu.roll(mine[part][odd], GROUP - turn, 0)


def seam_of(block_ref, dates_here, seat, seam_ref):
    height = block_ref.shape[0]
    lines = block_ref[height - NOTE_ROWS : height].astype(F32)
    for part in range(2):
        at = NOTE + part * dates_here
        seam_ref[part, seat : seat + dates_here, :] = lines[at : at + dates_here]


def early_kernel(dates_here, *refs):
    *block_refs, comb_ref, fold_ref, ring_ref, pair_ref, seam_ref, rows_ref = refs
    columns = comb_ref.shape[0]
    looks = columns // 8
    tiles = ring_ref.shape[3]
    half_rows = rows_ref.shape[2] // GROUP // 2
    comb = comb_of(columns)
    comb_ref[...] = comb
    fold_ref[...] = fold_of(fold_ref.shape, looks, half_rows)
    for index, block_ref in enumerate(block_refs):
        spread_block(block_ref, comb, dates_here, index * dates_here, rows_ref)
        seam_of(block_ref, dates_here, index * dates_here, seam_ref)

    def keep(part, odd, place, tile, cells):
        ring_ref[part, odd, place, tile] = cells

    pack_group(rows_ref, looks, half_rows, keep)

    def store(part, tile, value):
        across = slice(tile * LANES, (tile + 1) * LANES)
        high, low = halves(value)
        pair_ref[part, 0, :, across] = high
        pair_ref[part, 1, :, across] = low

    unit_products(
        tiles,
        looks,
        range(1, GROUP // 2 + 1),
        lambda part, odd, place, tile: ring_ref[part, odd, place, tile],
        turn_here,
        store,
    )


def place_of(step, owners, dates_here):
    date = (step + 1) % owners * dates_here
    return date // GROUP, date % GROUP


def middle_kernel(dates_here, slots, steps, *refs):
    *refs, rows_ref, seams_ref, partial_ref, rest_ref, wide_ref = refs
    comb_ref, inverse_ref, *block_refs = refs
    owners = len(block_refs) + 1
    comb = comb_ref[...]
    wide_ref[...] = jnp.zeros_like(wide_ref)
    wide_ref[: inverse_ref.shape[0], : inverse_ref.shape[1]] = inverse_ref[...]
    wide = wide_ref[...]
    sums = [0.0, 0.0]
    for step, block_ref in zip(steps, block_refs):
        group, seat = place_of(step, owners, dates_here)
        if group:
            spread_block(block_ref, comb, dates_here, seat, rows_ref.at[group - 1])
            seam_of(block_ref, dates_here, seat, seams_ref.at[group - 1])
        more = slot_weights(block_ref, inverse_of(wide, step, owners, slots), owners, dates_here)
        sums = [one + two for one, two in zip(sums, more)]
    for part in range(2):
        partial_ref[part] = sums[part]
    rest_ref[...] = inverse_of(wide, 1, owners, slots)


def edge_kernel(dates_here, owners, *refs):
    block_ref, seam_ref, others_ref, partial_ref, rest_ref, *refs = refs
    weights_ref, *message_refs, seams_ref, pair_ref = refs
    dates = owners * dates_here
    pairs = pair_rows(dates)
    tall = rest_ref.shape[0]

    seams_ref[...] = others_ref[...]
    group, seat = place_of(1, owners, dates_here)
    seam_of(block_ref, dates_here, seat, seams_ref.at[group - 1])
    weights = []
    for part, more in enumerate(slot_weights(block_ref, rest_ref[...], owners, dates_here)):
        high, low = halves(partial_ref[part] + more)
        wide = [jnp.concatenate([half, half], axis=1) for half in (high, low)]
        weights.append(jnp.concatenate(wide, axis=0))
        weights_ref[part] = weights[part]

    lane = iota((GROUP, LANES), 1) % 8
    ramp = jnp.where(lane < 4, 3.5 - lane.astype(F32), lane.astype(F32) - 3.5)
    for unit, (low, high, turns) in enumerate(pair_units(dates)):
        mine = [(seams_ref[low - 1, part] if low else seam_ref[part]) * ramp for part in range(2)]
        theirs = [seams_ref[high - 1, part] if high else seam_ref[part] for part in range(2)]
        values = []
        for turn in turns:
            other = [pltpu.roll(cells, GROUP - turn, 0) if turn else cells for cells in theirs]
            values.append(mine[0] * other[0] + mine[1] * other[1])
            values.append(mine[1] * other[0] - mine[0] * other[1])
        for part in range(2):
            value = jnp.concatenate(values[part::2], axis=0)
            count = value.shape[0]
            bits = halves(value)
            for half in range(2):
                at = half * pairs + unit * count
                pair_ref[part, at : at + count, :] = bits[half]
    sums = []
    for part in range(2):
        summed = jnp.dot(weights[part], pair_ref[part], preferred_element_type=F32)
        sums.append(summed[:tall] + summed[tall:])
    head = iota((tall, LANES), 1) % 8 < 4
    to_left = jnp.where(head, sums[0], pltpu.roll(sums[1], 4, 1))
    to_right = jnp.where(head, pltpu.roll(sums[0], LANES - 4, 1), sums[1])
    here = lax.rem(lax.axis_index("col"), len(message_refs))
    for swap, message_ref in enumerate(message_refs):
        message_ref[...] = jnp.where(here == swap, to_right, to_left)


def series_kernel(dates_here, *refs):
    *refs, looked_ref, rows_ref, ring_ref, far_ref, pair_ref = refs
    block_ref, comb_ref, weights_ref, first_ref, first_pair_ref, others_ref = refs
    groups = 1 + ring_ref.shape[0]
    dates = groups * GROUP
    pairs = pair_rows(dates)
    columns = comb_ref.shape[0]
    looks = columns // 8
    tiles = ring_ref.shape[4]
    half_rows = rows_ref.shape[3] // GROUP // 2
    tall = looked_ref.shape[1]

    rows_ref[...] = others_ref[...]
    last_group, seat = place_of(1, dates // dates_here, dates_here)
    spread_block(block_ref, comb_ref[...], dates_here, seat, rows_ref.at[last_group - 1])
    for group in range(1, groups):

        def keep(part, odd, place, tile, cells):
            ring_ref[group - 1, part, odd, place, tile] = cells
            for copy in range(2):
                at = pl.ds(2 * copy * GROUP + odd, GROUP, stride=2)
                far_ref[group - 1, part, place, tile, at, :] = cells

        pack_group(rows_ref.at[group - 1], looks, half_rows, keep)

    for part in range(2):
        for half in range(2):
            at = half * pairs
            pair_ref[part, at : at + first_pair_ref.shape[2], :] = first_pair_ref[part, half]
    for unit, (low, high, turns) in enumerate(pair_units(dates)):
        if high == 0:
            continue

        def mine_of(part, odd, place, tile):
            if low == 0:
                return first_ref[part, odd, place, tile]
            return ring_ref[low - 1, part, odd, place, tile]

        def turn_far(part, odd, place, tile, turn, mine):
            at = pl.ds(2 * turn + odd, GROUP, stride=2)
            return far_ref[high - 1, part, place, tile, at, :]

        def store(part, tile, value):
            count = value.shape[0]
            across = slice(tile * LANES, (tile + 1) * LANES)
            bits = halves(value)
            for half in range(2):
                at = half * pairs + unit * count
                pair_ref[part, at : at + count, across] = bits[half]

        turned_of = turn_here if low == high else turn_far
        unit_products(tiles, looks, turns, mine_of, turned_of, store)
    for part in range(2):
        summed = jnp.dot(weights_ref[part], pair_ref[part], preferred_element_type=F32)
        looked_ref[part] = summed[:tall] + summed[tall:]


def finish_kernel(looked_ref, fold_ref, *refs):
    *message_refs, out_ref, sum_ref, done_ref, semaphores = refs
    parts, times, half_rows, looks = done_ref.shape
    tall = looked_ref.shape[1]
    pack = LANES // looks
    here, last = lax.axis_index("col"), lax.axis_size("col") - 1
    swaps = len(message_refs)
    from_right = from_left = jnp.zeros((tall, LANES), F32)
    for swap, message_ref in enumerate(message_refs):
        message = message_ref[...]
        from_right = jnp.where((here != last) & (here % swaps == swap), message, from_right)
        from_left = jnp.where((here != 0) & ((here - 1) % swaps == swap), message, from_left)
    edges = jnp.concatenate([from_right, from_left], axis=1)
    head = iota(edges.shape, 1) % 8 < 4
    edges = [jnp.where(head, edges, 0.0), jnp.where(head, 0.0, edges)]
    edges = jnp.concatenate(halves(jnp.concatenate(edges, axis=0)), axis=0)
    edges = jnp.dot(edges, fold_ref[...], preferred_element_type=F32)
    edges = edges[: parts * tall] + edges[parts * tall :]
    sent = []
    for part in range(parts):
        value = looked_ref[part] + edges[part * tall : (part + 1) * tall]
        for half_row in range(half_rows):
            tile, near = half_row // pack, half_row % pack
            one = value[:, tile * LANES : (tile + 1) * LANES]
            at = half_row * tall
            sum_ref[part, at : at + tall, :] = pltpu.roll(one, -near * looks % LANES, 1)
        for time in range(times):
            rows = sum_ref[part, pl.ds(time, half_rows, stride=tall), :]
            done_ref[part, time] = rows[:, :looks]
        sent.append(
            pltpu.make_async_copy(done_ref.at[part], out_ref.at[:, part], semaphores.at[part])
        )
        sent[part].start()
    for copy in sent:
        copy.wait()


def column_swap(swap, swaps, owners, count):
    moves = []
    for owner in range(owners):
        for column in range(count):
            partner = column
            if column % swaps == swap and column + 1 < count:
                partner = column + 1
            elif column and (column - 1) % swaps == swap:
                partner = column - 1
            moves.append((owner * count + column, twin_of(owner, owners) * count + partner))
    return moves


def per_device(scenes, pair_dates, pair_count, inverse):
    owners, count = lax.axis_size("date"), lax.axis_size("col")
    dates_here, parts, all_rows, columns = scenes.shape
    half_rows = all_rows // owners // 2
    dates = owners * dates_here
    pairs = pair_rows(dates)
    looks = columns // 8
    tiles = -(-half_rows // (LANES // looks))

    blocks = cut(scenes, pair_dates.T, pair_count, owners)
    for step in range(1, owners):
        moves = [(owner, (owner - step) % owners) for owner in range(owners)]
        blocks[step] = lax.ppermute(blocks[step], "date", moves)

    tall = round_up(inverse.shape[0], 16)
    rows = 2 * half_rows
    sides = columns // LANES
    order = [blocks[(place - 1) % owners] for place in range(owners)]
    order = [held(block) for block in order]
    group_rows = pltpu.VMEM((parts, sides, rows * GROUP, LANES), F32)
    comb, fold, first_group, first_pairs, first_seam = pl.pallas_call(
        functools.partial(early_kernel, dates_here),
        out_shape=[
            pltpu.VMEM((columns, columns), BF16),
            pltpu.VMEM((2 * LANES, tiles * LANES), BF16),
            pltpu.VMEM((parts, 2, 8, tiles, GROUP, LANES), F32),
            pltpu.VMEM((parts, 2, GROUP * GROUP // 2, tiles * LANES), BF16),
            pltpu.VMEM((parts, GROUP, LANES), F32),
        ],
        in_specs=[IN_VMEM] * (GROUP // dates_here),
        out_specs=[IN_VMEM] * 5,
        scratch_shapes=[group_rows],
        compiler_params=pltpu.CompilerParams(vmem_limit_bytes=40 << 20),
    )(*order[: GROUP // dates_here])
    others = dates // GROUP - 1
    steps = [*range(owners - 1, 1, -1), 0]
    group_rows = pltpu.VMEM((others, *group_rows.shape), F32)
    other_rows, other_seams, partial, rest = pl.pallas_call(
        functools.partial(middle_kernel, dates_here, pair_dates.shape[0], steps),
        out_shape=[
            group_rows,
            pltpu.VMEM((others, parts, GROUP, LANES), F32),
            pltpu.VMEM((parts, tall, pairs), F32),
            pltpu.VMEM((tall, LANES), F32),
        ],
        in_specs=[IN_VMEM] * (owners + 1),
        out_specs=[IN_VMEM] * 4,
        scratch_shapes=[pltpu.VMEM((tall, round_up(inverse.shape[1], LANES)), F32)],
        compiler_params=pltpu.CompilerParams(vmem_limit_bytes=40 << 20),
    )(held(comb), held(inverse), *[held(blocks[step]) for step in steps])
    swaps = min(3, count - 1)
    weights, *messages = pl.pallas_call(
        functools.partial(edge_kernel, dates_here, owners),
        out_shape=[
            pltpu.VMEM((parts, 2 * tall, 2 * pairs), BF16),
            *[pltpu.VMEM((tall, LANES), F32)] * swaps,
        ],
        in_specs=[IN_VMEM] * 5,
        out_specs=[IN_VMEM] * (swaps + 1),
        scratch_shapes=[
            pltpu.VMEM((others, parts, GROUP, LANES), F32),
            pltpu.VMEM((parts, 2 * pairs, LANES), BF16),
        ],
        compiler_params=pltpu.CompilerParams(vmem_limit_bytes=40 << 20),
    )(*[held(array) for array in (blocks[1], first_seam, other_seams, partial, rest)])
    looked = pl.pallas_call(
        functools.partial(series_kernel, dates_here),
        out_shape=pltpu.VMEM((parts, tall, tiles * LANES), F32),
        in_specs=[IN_VMEM] * 6,
        out_specs=IN_VMEM,
        scratch_shapes=[
            group_rows,
            pltpu.VMEM((others, parts, 2, 8, tiles, GROUP, LANES), F32),
            pltpu.VMEM((others, parts, 8, tiles, 4 * GROUP, LANES), F32),
            pltpu.VMEM((parts, 2 * pairs, tiles * LANES), BF16),
        ],
        compiler_params=pltpu.CompilerParams(vmem_limit_bytes=40 << 20),
        cost_estimate=pl.CostEstimate(
            flops=2 * parts * pairs * columns * rows * 8, bytes_accessed=1 << 20, transcendentals=0
        ),
    )(*[held(one) for one in (blocks[1], comb, weights, first_group, first_pairs, other_rows)])

    for swap in range(swaps):
        moves = column_swap(swap, swaps, owners, count)
        messages[swap] = held(lax.ppermute(messages[swap], ("date", "col"), moves))
    return pl.pallas_call(
        finish_kernel,
        out_shape=jax.ShapeDtypeStruct(
            (inverse.shape[0], parts, half_rows, columns // 8), F32
        ),
        in_specs=[IN_VMEM] * (swaps + 2),
        out_specs=ANYWHERE,
        scratch_shapes=[
            pltpu.VMEM((parts, half_rows * tall, LANES), F32),
            pltpu.VMEM((parts, inverse.shape[0], half_rows, columns // 8), F32),
            pltpu.SemaphoreType.DMA((parts,)),
        ],
    )(held(looked), held(fold), *messages)


def solution(mesh):
    placed = (P("date", None, "groups", "col"), P("date", None), P("date"), P())
    return jax.shard_map(
        per_device,
        mesh=mesh,
        in_specs=placed,
        out_specs=P(None, None, ("groups", "date"), "col"),
        check_vma=False,
    )
```

```python
import functools

import jax
import jax.numpy as jnp
from jax import lax
from jax.experimental import pallas as pl
from jax.experimental.pallas import tpu as pltpu
from jax.sharding import PartitionSpec as P

F32, BF16 = jnp.float32, jnp.bfloat16
LANES = 128
NOTE = 8
NOTE_ROWS = 2 * NOTE
GROUP = 8
ANYWHERE = pl.BlockSpec(memory_space=pl.ANY)
IN_VMEM = pl.BlockSpec(memory_space=pltpu.VMEM)
IN_SMEM = pl.BlockSpec(memory_space=pltpu.SMEM)


def round_up(value, step):
    return -(-value // step) * step


def held(array):
    return pltpu.with_memory_space_constraint(array, pltpu.VMEM)


def iota(shape, axis):
    return lax.broadcasted_iota(jnp.int32, shape, axis)


def halves(value):
    high = value.astype(BF16)
    return high, (value - high.astype(F32)).astype(BF16)


def blank_kernel(blank_ref):
    blank_ref[...] = jnp.zeros_like(blank_ref)


def comb_of(columns):
    looks = columns // 8
    column, lane = iota((columns, columns), 0), iota((columns, columns), 1)
    here = (column // 8 == lane % looks) & (column % 8 == lane // looks)
    return jnp.where(here, 1.0, 0.0).astype(BF16)


def fold_of(shape, looks, half_rows):
    cell, target = iota(shape, 0), iota(shape, 1)
    right = cell < LANES
    cell = cell % LANES
    half_row = cell // 16
    here = right & (target == half_row * looks + looks - 1)
    here = here | ~right & (target == half_row * looks)
    return jnp.where(here & (half_row < half_rows), 1.0, 0.0).astype(BF16)


def live_kernel(rows, slots, count_ref, blank_ref, live_ref, pick_ref, own_ref, gather_ref):
    columns, (all_rows, lanes), (lines, height) = pick_ref.shape[0], own_ref.shape, gather_ref.shape
    column, lane = iota((columns, lanes), 0), iota((columns, lanes), 1) % 8
    wanted = jnp.where(lane < 4, lane, columns - 8 + lane)
    pick_ref[...] = jnp.where(column == wanted, 1.0, 0.0).astype(BF16)
    row, lane = iota((all_rows, lanes), 0), iota((all_rows, lanes), 1)
    own_ref[...] = jnp.where(row % rows == lane // 8, 1.0, 0.0)
    owners, images = all_rows // rows, height // all_rows
    line, row = iota((lines, height), 0), iota((lines, height), 1) // rows
    place = line % NOTE
    wanted = (place % (images // 2) * 2 + place // (images // 2)) * owners + line // NOTE
    gather_ref[...] = jnp.where((place < images) & (row == wanted), 1.0, 0.0).astype(BF16)
    row, lane = iota(live_ref.shape, 0), iota(live_ref.shape, 1)
    live = (row == 2) & (lane < jnp.minimum(count_ref[0], slots))
    live_ref[...] = jnp.where(live, 1.0, blank_ref[...])


def seam_kernel(scenes_ref, dates_ref, live_ref, pick_ref, own_ref, gather_ref, *refs):
    seams_ref, note_ref, fetched_ref, semaphore = refs
    fetch = pltpu.make_async_copy(dates_ref, fetched_ref, semaphore)
    fetch.start()
    dates_here, parts, all_rows, columns = scenes_ref.shape
    height = dates_here * parts * all_rows
    cells = scenes_ref[...].reshape(height, columns)
    cells = jnp.dot(cells, pick_ref[...], preferred_element_type=F32)
    cells = cells.reshape(dates_here * parts, all_rows, LANES) * own_ref[...][None]
    cells = cells.reshape(height, LANES).astype(BF16)
    lines = jnp.dot(gather_ref[...], cells, preferred_element_type=F32)
    for owner in range(seams_ref.shape[0]):
        seams_ref[owner] = lines[owner * NOTE : (owner + 1) * NOTE]
    note_ref[...] = live_ref[...]
    fetch.wait()
    note_ref[:2, : dates_ref.shape[1]] = fetched_ref[...].astype(F32)


def twin_of(owner, owners):
    return owner + 1 - 2 * (owner % 2) if owners % 2 == 0 else owner


def cut_kernel(scenes_ref, note_ref, seams_ref, *block_refs):
    owners = len(block_refs)
    me = lax.axis_index("date")
    rows = scenes_ref.shape[2] // owners
    sides = scenes_ref.shape[3] // LANES
    for step, block_ref in enumerate(block_refs):
        owner = lax.rem(me + owners - step, owners)
        first = pl.multiple_of(owner * rows, rows)
        height = (block_ref.shape[0] - NOTE_ROWS) // sides
        for side in range(sides):
            cells = scenes_ref[:, :, pl.ds(first, rows), side * LANES : (side + 1) * LANES]
            block_ref[side * height : (side + 1) * height] = cells.reshape(height, LANES)
        seam = seams_ref[twin_of(owner, owners)]
        block_ref[sides * height :] = jnp.concatenate([note_ref[...], seam], axis=0).astype(BF16)


def cells_of(block_ref, sides):
    height = (block_ref.shape[0] - NOTE_ROWS) // sides
    return jnp.concatenate(
        [block_ref[side * height : (side + 1) * height] for side in range(sides)], axis=1
    )


def cut(scenes, pair_dates, pair_count, owners):
    dates_here, parts, all_rows, columns = scenes.shape
    rows = all_rows // owners
    sides = columns // LANES
    height = dates_here * parts * rows
    blank = pl.pallas_call(
        blank_kernel,
        out_shape=pltpu.VMEM((NOTE, LANES), F32),
        out_specs=IN_VMEM,
        cost_estimate=pl.CostEstimate(flops=10**9, bytes_accessed=10**7, transcendentals=0),
    )()
    live, *constants = pl.pallas_call(
        functools.partial(live_kernel, rows, pair_dates.shape[1]),
        out_shape=[
            pltpu.VMEM((NOTE, LANES), F32),
            pltpu.VMEM((columns, LANES), BF16),
            pltpu.VMEM((all_rows, LANES), F32),
            pltpu.VMEM((owners * NOTE, dates_here * parts * all_rows), BF16),
        ],
        in_specs=[IN_SMEM, IN_VMEM],
        out_specs=[IN_VMEM] * 4,
    )(pair_count, held(blank))
    seams, note = pl.pallas_call(
        seam_kernel,
        out_shape=[pltpu.VMEM((owners, NOTE, LANES), F32), pltpu.VMEM((NOTE, LANES), F32)],
        in_specs=[IN_VMEM, ANYWHERE] + [IN_VMEM] * 4,
        out_specs=[IN_VMEM] * 2,
        scratch_shapes=[pltpu.VMEM(pair_dates.shape, jnp.int32), pltpu.SemaphoreType.DMA],
    )(held(scenes), pair_dates, held(live), *[held(array) for array in constants])
    if rows % 16 == 0:
        blocks = pl.pallas_call(
            cut_kernel,
            out_shape=[pltpu.VMEM((sides * height + NOTE_ROWS, LANES), BF16)] * owners,
            in_specs=[IN_VMEM] * 3,
            out_specs=[IN_VMEM] * owners,
        )(held(scenes), held(note), held(seams))
        return list(blocks)
    me = lax.axis_index("date")
    apart = scenes.reshape(dates_here * parts, owners, rows, columns)
    blocks = []
    for step in range(owners):
        owner = lax.rem(me + owners - step, owners)
        cells = lax.dynamic_index_in_dim(apart, owner, 1, False).reshape(height, columns)
        strips = [cells[:, side * LANES : (side + 1) * LANES] for side in range(sides)]
        seam = lax.dynamic_index_in_dim(seams, twin_of(owner, owners), 0, False)
        strips += [note.astype(BF16), seam.astype(BF16)]
        blocks.append(jnp.concatenate(strips, axis=0))
    return blocks


def pair_places(first, second, dates):
    groups = dates // GROUP

    def group_of(date):
        return jnp.floor(date * (1.0 / GROUP))

    first_group, second_group = group_of(first), group_of(second)
    first_seat, second_seat = first - GROUP * first_group, second - GROUP * second_group
    ahead = second_seat - first_seat
    ahead = jnp.where(ahead < 0.0, ahead + GROUP, ahead)
    behind = jnp.where(ahead > 0.0, GROUP - ahead, 0.0)
    near = ahead <= GROUP // 2
    inside = first_group * (GROUP * GROUP // 2)
    inside = inside + jnp.where(
        near, (ahead - 1.0) * GROUP + first_seat, (behind - 1.0) * GROUP + second_seat
    )
    upward = first_group < second_group
    low, high = jnp.minimum(first_group, second_group), jnp.maximum(first_group, second_group)
    between = low * (2 * groups - 1.0 - low) * 0.5 + high - low - 1.0
    across = groups * (GROUP * GROUP // 2) + between * (GROUP * GROUP)
    across = across + jnp.where(
        upward, ahead * GROUP + first_seat, behind * GROUP + second_seat
    )
    same = first_group == second_group
    sign = jnp.where(same, jnp.where(near, 1.0, -1.0), jnp.where(upward, 1.0, -1.0))
    return jnp.where(same, inside, across), sign


def inverse_of(wide, step, owners, slots):
    lanes = wide.shape[1]
    owner = lax.rem(lax.axis_index("date") + step, owners)
    moved = pltpu.roll(wide, lax.rem(lanes - owner * slots, lanes), 1)
    return moved[:, :LANES] * (1.0 / 128.0)


def slot_weights(block_ref, inverse, owners, dates_here):
    dates = owners * dates_here
    start = lax.rem(lax.axis_index("date") + owners - 1, owners) * dates_here
    start = jnp.full((1, LANES), start, jnp.int32).astype(F32)
    height = block_ref.shape[0]
    note = block_ref[height - NOTE_ROWS : height].astype(F32)

    def wrapped(value):
        return jnp.where(value < 0.0, value + dates, value)

    place, sign = pair_places(wrapped(note[0:1] - start), wrapped(note[1:2] - start), dates)
    place = jnp.where(note[2:3] > 0.5, place, -1.0)
    pairs = pair_rows(dates)
    chosen = jnp.where(iota((pairs, LANES), 0).astype(F32) == place, 1.0, 0.0).astype(BF16)
    stacked = jnp.concatenate([*halves(inverse), *halves(inverse * sign)], axis=0)
    spread = lax.dot_general(
        stacked, chosen, (((1,), (1,)), ((), ())), preferred_element_type=F32
    )
    tall = inverse.shape[0]
    parts = [spread[at * tall : (at + 1) * tall] for at in range(4)]
    return parts[0] + parts[1], parts[2] + parts[3]


def pair_rows(dates):
    groups = dates // GROUP
    return GROUP * GROUP // 2 * groups + GROUP * GROUP * (groups * (groups - 1) // 2)


def pair_units(dates):
    groups = dates // GROUP
    half = GROUP // 2
    units = [(group, group, range(1, half + 1)) for group in range(groups)]
    for low in range(groups):
        for high in range(low + 1, groups):
            units += [(low, high, range(at, at + half)) for at in range(0, GROUP, half)]
    return units


def spread_block(block_ref, comb, dates_here, seat, rows_ref):
    sides = rows_ref.shape[1]
    combed = jnp.dot(cells_of(block_ref, sides), comb, preferred_element_type=F32)
    rows = combed.shape[0] // (2 * dates_here)
    for own in range(dates_here):
        for part in range(2):
            at = (own * 2 + part) * rows
            for side in range(sides):
                rows_ref[part, side, pl.ds(seat + own, rows, stride=GROUP), :] = combed[
                    at : at + rows, side * LANES : (side + 1) * LANES
                ]


def pack_group(rows_ref, looks, half_rows, store):
    pack = LANES // looks
    lane = iota((GROUP, LANES), 1)
    for part in range(2):
        for odd in range(2):
            for tile in range(-(-half_rows // pack)):
                for side in range(rows_ref.shape[1]):
                    cells = []
                    for near in range(pack):
                        half_row = tile * pack + near
                        at = (2 * half_row + odd) * GROUP
                        if half_row < half_rows:
                            cells.append(rows_ref[part, side, at : at + GROUP, :])
                        else:
                            cells.append(jnp.zeros((GROUP, LANES), F32))
                    bit = pack // 2
                    while bit:
                        clear = (lane // looks) & bit == 0
                        for near in range(pack):
                            if not near & bit:
                                one, two = cells[near], cells[near + bit]
                                cells[near] = jnp.where(
                                    clear, one, pltpu.roll(two, bit * looks, 1)
                                )
                                cells[near + bit] = jnp.where(
                                    clear, pltpu.roll(one, LANES - bit * looks, 1), two
                                )
                        bit //= 2
                    for near in range(pack):
                        store(part, odd, side * pack + near, tile, cells[near])


def unit_products(tile, looks, turns, mine_of, turned_of, store):
    lane = iota((GROUP, LANES), 1) % looks
    at_first, at_last = lane == 0, lane == looks - 1

    def product(place):
        mine = [[mine_of(part, odd, place, tile) for odd in range(2)] for part in range(2)]
        values = []
        for turn in turns:
            other = [
                [turned_of(part, odd, place, tile, turn, mine) for odd in range(2)]
                for part in range(2)
            ]
            real = (mine[0][0] * other[0][0] + mine[1][0] * other[1][0]) + (
                mine[0][1] * other[0][1] + mine[1][1] * other[1][1]
            )
            imaginary = (mine[1][0] * other[0][0] - mine[0][0] * other[1][0]) + (
                mine[1][1] * other[0][1] - mine[0][1] * other[1][1]
            )
            values += [real, imaginary]
        return values

    def running(places):
        total = product(places[0])
        ramp = total
        for place in places[1:]:
            total = [one + two for one, two in zip(total, product(place))]
            share = [0.5 * one for one in total] if place is places[-1] else total
            ramp = [one + two for one, two in zip(ramp, share)]
        return total, ramp

    early, to_left = running((0, 1, 2, 3))
    late, to_right = running((7, 6, 5, 4))
    values = []
    for index in range(len(early)):
        before = pltpu.roll(to_right[index], 1, 1)
        after = pltpu.roll(to_left[index], LANES - 1, 1)
        value = 8.0 * (early[index] + late[index]) - to_left[index] - to_right[index]
        value = value + jnp.where(at_first, 0.0, before) + jnp.where(at_last, 0.0, after)
        values.append(value)
    for part in range(2):
        store(part, tile, jnp.concatenate(values[part::2], axis=0))


def turn_here(part, odd, place, tile, turn, mine):
    return pltpu.roll(mine[part][odd], GROUP - turn, 0)


def seam_of(block_ref, dates_here, seat, seam_ref):
    height = block_ref.shape[0]
    lines = block_ref[height - NOTE_ROWS : height].astype(F32)
    for part in range(2):
        at = NOTE + part * dates_here
        seam_ref[part, seat : seat + dates_here, :] = lines[at : at + dates_here]


def early_kernel(dates_here, *refs):
    *block_refs, comb_ref, fold_ref, ring_ref, pair_ref, seam_ref, rows_ref = refs
    columns = comb_ref.shape[0]
    looks = columns // 8
    tiles = ring_ref.shape[3]
    half_rows = rows_ref.shape[2] // GROUP // 2
    comb = comb_of(columns)
    comb_ref[...] = comb
    fold_ref[...] = fold_of(fold_ref.shape, looks, half_rows)
    for index, block_ref in enumerate(block_refs):
        spread_block(block_ref, comb, dates_here, index * dates_here, rows_ref)
        seam_of(block_ref, dates_here, index * dates_here, seam_ref)

    def keep(part, odd, place, tile, cells):
        ring_ref[part, odd, place, tile] = cells

    pack_group(rows_ref, looks, half_rows, keep)

    def store(part, tile, value):
        across = slice(tile * LANES, (tile + 1) * LANES)
        high, low = halves(value)
        pair_ref[part, 0, :, across] = high
        pair_ref[part, 1, :, across] = low

    for tile in range(tiles):
        unit_products(
            tile,
            looks,
            range(1, GROUP // 2 + 1),
            lambda part, odd, place, tile: ring_ref[part, odd, place, tile],
            turn_here,
            store,
        )


def place_of(step, owners, dates_here):
    date = (step + 1) % owners * dates_here
    return date // GROUP, date % GROUP


def middle_kernel(dates_here, slots, steps, *refs):
    *refs, rows_ref, seams_ref, partial_ref, rest_ref, wide_ref = refs
    comb_ref, inverse_ref, *block_refs = refs
    owners = len(block_refs) + 1
    comb = comb_ref[...]
    wide_ref[...] = jnp.zeros_like(wide_ref)
    wide_ref[: inverse_ref.shape[0], : inverse_ref.shape[1]] = inverse_ref[...]
    wide = wide_ref[...]
    sums = [0.0, 0.0]
    for step, block_ref in zip(steps, block_refs):
        group, seat = place_of(step, owners, dates_here)
        if group:
            spread_block(block_ref, comb, dates_here, seat, rows_ref.at[group - 1])
            seam_of(block_ref, dates_here, seat, seams_ref.at[group - 1])
        more = slot_weights(block_ref, inverse_of(wide, step, owners, slots), owners, dates_here)
        sums = [one + two for one, two in zip(sums, more)]
    for part in range(2):
        partial_ref[part] = sums[part]
    rest_ref[...] = inverse_of(wide, 1, owners, slots)


def edge_kernel(dates_here, owners, *refs):
    block_ref, seam_ref, others_ref, partial_ref, rest_ref, comb_ref, other_rows_ref, *refs = refs
    weights_ref, ring_ref, far_ref, *message_refs, seams_ref, pair_ref, rows_ref = refs
    dates = owners * dates_here
    pairs = pair_rows(dates)
    tall = rest_ref.shape[0]

    group, seat = place_of(1, owners, dates_here)
    rows_ref[...] = other_rows_ref[...]
    spread_block(block_ref, comb_ref[...], dates_here, seat, rows_ref.at[group - 1])
    seams_ref[...] = others_ref[...]
    seam_of(block_ref, dates_here, seat, seams_ref.at[group - 1])
    weights = []
    for part, more in enumerate(slot_weights(block_ref, rest_ref[...], owners, dates_here)):
        high, low = halves(partial_ref[part] + more)
        wide = [jnp.concatenate([half, half], axis=1) for half in (high, low)]
        weights.append(jnp.concatenate(wide, axis=0))
        weights_ref[part] = weights[part]

    lane = iota((GROUP, LANES), 1) % 8
    ramp = jnp.where(lane < 4, 3.5 - lane.astype(F32), lane.astype(F32) - 3.5)
    for unit, (low, high, turns) in enumerate(pair_units(dates)):
        mine = [(seams_ref[low - 1, part] if low else seam_ref[part]) * ramp for part in range(2)]
        theirs = [seams_ref[high - 1, part] if high else seam_ref[part] for part in range(2)]
        values = []
        for turn in turns:
            other = [pltpu.roll(cells, GROUP - turn, 0) if turn else cells for cells in theirs]
            values.append(mine[0] * other[0] + mine[1] * other[1])
            values.append(mine[1] * other[0] - mine[0] * other[1])
        for part in range(2):
            value = jnp.concatenate(values[part::2], axis=0)
            count = value.shape[0]
            bits = halves(value)
            for half in range(2):
                at = half * pairs + unit * count
                pair_ref[part, at : at + count, :] = bits[half]
    looks = comb_ref.shape[0] // 8
    half_rows = rows_ref.shape[3] // GROUP // 2
    for group in range(1, dates // GROUP):

        def keep(part, odd, place, tile, cells):
            ring_ref[group - 1, part, odd, place, tile] = cells
            for copy in range(2):
                at = pl.ds(2 * copy * GROUP + odd, GROUP, stride=2)
                far_ref[group - 1, part, place, tile, at, :] = cells

        pack_group(rows_ref.at[group - 1], looks, half_rows, keep)
    sums = []
    for part in range(2):
        summed = jnp.dot(weights[part], pair_ref[part], preferred_element_type=F32)
        sums.append(summed[:tall] + summed[tall:])
    head = iota((tall, LANES), 1) % 8 < 4
    to_left = jnp.where(head, sums[0], pltpu.roll(sums[1], 4, 1))
    to_right = jnp.where(head, pltpu.roll(sums[0], LANES - 4, 1), sums[1])
    here = lax.rem(lax.axis_index("col"), len(message_refs))
    for swap, message_ref in enumerate(message_refs):
        message_ref[...] = jnp.where(here == swap, to_right, to_left)


def series_kernel(looks, *refs):
    weights_ref, first_ref, first_pair_ref, ring_ref, far_ref, looked_ref, pair_ref = refs
    groups = 1 + ring_ref.shape[0]
    dates = groups * GROUP
    pairs = pair_rows(dates)
    tiles = ring_ref.shape[4]
    tall = looked_ref.shape[1]

    for part in range(2):
        for half in range(2):
            at = half * pairs
            pair_ref[part, at : at + first_pair_ref.shape[2], :] = first_pair_ref[part, half]
    for tile in range(tiles):
        for unit, (low, high, turns) in enumerate(pair_units(dates)):
            if high == 0:
                continue

            def mine_of(part, odd, place, tile):
                if low == 0:
                    return first_ref[part, odd, place, tile]
                return ring_ref[low - 1, part, odd, place, tile]

            def turn_far(part, odd, place, tile, turn, mine):
                at = pl.ds(2 * turn + odd, GROUP, stride=2)
                return far_ref[high - 1, part, place, tile, at, :]

            def store(part, tile, value):
                count = value.shape[0]
                across = slice(tile * LANES, (tile + 1) * LANES)
                bits = halves(value)
                for half in range(2):
                    at = half * pairs + unit * count
                    pair_ref[part, at : at + count, across] = bits[half]

            turned_of = turn_here if low == high else turn_far
            unit_products(tile, looks, turns, mine_of, turned_of, store)
        across = slice(tile * LANES, (tile + 1) * LANES)
        for part in range(2):
            summed = jnp.dot(
                weights_ref[part], pair_ref[part, :, across], preferred_element_type=F32
            )
            looked_ref[part, :, across] = summed[:tall] + summed[tall:]


def finish_kernel(looked_ref, fold_ref, *refs):
    *message_refs, out_ref, sum_ref, done_ref, semaphores = refs
    parts, times, half_rows, looks = done_ref.shape
    tall = looked_ref.shape[1]
    pack = LANES // looks
    here, last = lax.axis_index("col"), lax.axis_size("col") - 1
    swaps = len(message_refs)
    from_right = from_left = jnp.zeros((tall, LANES), F32)
    for swap, message_ref in enumerate(message_refs):
        message = message_ref[...]
        from_right = jnp.where((here != last) & (here % swaps == swap), message, from_right)
        from_left = jnp.where((here != 0) & ((here - 1) % swaps == swap), message, from_left)
    edges = jnp.concatenate([from_right, from_left], axis=1)
    head = iota(edges.shape, 1) % 8 < 4
    edges = [jnp.where(head, edges, 0.0), jnp.where(head, 0.0, edges)]
    edges = jnp.concatenate(halves(jnp.concatenate(edges, axis=0)), axis=0)
    edges = jnp.dot(edges, fold_ref[...], preferred_element_type=F32)
    edges = edges[: parts * tall] + edges[parts * tall :]
    sent = []
    for part in range(parts):
        value = looked_ref[part] + edges[part * tall : (part + 1) * tall]
        for half_row in range(half_rows):
            tile, near = half_row // pack, half_row % pack
            one = value[:, tile * LANES : (tile + 1) * LANES]
            at = half_row * tall
            sum_ref[part, at : at + tall, :] = pltpu.roll(one, -near * looks % LANES, 1)
        for time in range(times):
            rows = sum_ref[part, pl.ds(time, half_rows, stride=tall), :]
            done_ref[part, time] = rows[:, :looks]
        sent.append(
            pltpu.make_async_copy(done_ref.at[part], out_ref.at[:, part], semaphores.at[part])
        )
        sent[part].start()
    for copy in sent:
        copy.wait()


def column_swap(swap, swaps, owners, count):
    moves = []
    for owner in range(owners):
        for column in range(count):
            partner = column
            if column % swaps == swap and column + 1 < count:
                partner = column + 1
            elif column and (column - 1) % swaps == swap:
                partner = column - 1
            moves.append((owner * count + column, twin_of(owner, owners) * count + partner))
    return moves


def per_device(scenes, pair_dates, pair_count, inverse):
    owners, count = lax.axis_size("date"), lax.axis_size("col")
    dates_here, parts, all_rows, columns = scenes.shape
    half_rows = all_rows // owners // 2
    dates = owners * dates_here
    pairs = pair_rows(dates)
    looks = columns // 8
    tiles = -(-half_rows // (LANES // looks))

    blocks = cut(scenes, pair_dates.T, pair_count, owners)
    for step in range(1, owners):
        moves = [(owner, (owner - step) % owners) for owner in range(owners)]
        blocks[step] = lax.ppermute(blocks[step], "date", moves)

    tall = round_up(inverse.shape[0], 16)
    rows = 2 * half_rows
    sides = columns // LANES
    order = [blocks[(place - 1) % owners] for place in range(owners)]
    order = [held(block) for block in order]
    group_rows = pltpu.VMEM((parts, sides, rows * GROUP, LANES), F32)
    comb, fold, first_group, first_pairs, first_seam = pl.pallas_call(
        functools.partial(early_kernel, dates_here),
        out_shape=[
            pltpu.VMEM((columns, columns), BF16),
            pltpu.VMEM((2 * LANES, tiles * LANES), BF16),
            pltpu.VMEM((parts, 2, 8, tiles, GROUP, LANES), F32),
            pltpu.VMEM((parts, 2, GROUP * GROUP // 2, tiles * LANES), BF16),
            pltpu.VMEM((parts, GROUP, LANES), F32),
        ],
        in_specs=[IN_VMEM] * (GROUP // dates_here),
        out_specs=[IN_VMEM] * 5,
        scratch_shapes=[group_rows],
        compiler_params=pltpu.CompilerParams(vmem_limit_bytes=40 << 20),
    )(*order[: GROUP // dates_here])
    others = dates // GROUP - 1
    steps = [*range(owners - 1, 1, -1), 0]
    group_rows = pltpu.VMEM((others, *group_rows.shape), F32)
    other_rows, other_seams, partial, rest = pl.pallas_call(
        functools.partial(middle_kernel, dates_here, pair_dates.shape[0], steps),
        out_shape=[
            group_rows,
            pltpu.VMEM((others, parts, GROUP, LANES), F32),
            pltpu.VMEM((parts, tall, pairs), F32),
            pltpu.VMEM((tall, LANES), F32),
        ],
        in_specs=[IN_VMEM] * (owners + 1),
        out_specs=[IN_VMEM] * 4,
        scratch_shapes=[pltpu.VMEM((tall, round_up(inverse.shape[1], LANES)), F32)],
        compiler_params=pltpu.CompilerParams(vmem_limit_bytes=40 << 20),
    )(held(comb), held(inverse), *[held(blocks[step]) for step in steps])
    swaps = min(3, count - 1)
    weights, ring, far, *messages = pl.pallas_call(
        functools.partial(edge_kernel, dates_here, owners),
        out_shape=[
            pltpu.VMEM((parts, 2 * tall, 2 * pairs), BF16),
            pltpu.VMEM((others, parts, 2, 8, tiles, GROUP, LANES), F32),
            pltpu.VMEM((others, parts, 8, tiles, 4 * GROUP, LANES), F32),
            *[pltpu.VMEM((tall, LANES), F32)] * swaps,
        ],
        in_specs=[IN_VMEM] * 7,
        out_specs=[IN_VMEM] * (swaps + 3),
        scratch_shapes=[
            pltpu.VMEM((others, parts, GROUP, LANES), F32),
            pltpu.VMEM((parts, 2 * pairs, LANES), BF16),
            group_rows,
        ],
        compiler_params=pltpu.CompilerParams(vmem_limit_bytes=40 << 20),
    )(
        *[held(one) for one in (blocks[1], first_seam, other_seams, partial, rest, comb)],
        held(other_rows),
    )
    looked = pl.pallas_call(
        functools.partial(series_kernel, looks),
        out_shape=pltpu.VMEM((parts, tall, tiles * LANES), F32),
        in_specs=[IN_VMEM] * 5,
        out_specs=IN_VMEM,
        scratch_shapes=[pltpu.VMEM((parts, 2 * pairs, tiles * LANES), BF16)],
        compiler_params=pltpu.CompilerParams(vmem_limit_bytes=40 << 20),
        cost_estimate=pl.CostEstimate(
            flops=2 * parts * pairs * columns * rows * 8, bytes_accessed=1 << 20, transcendentals=0
        ),
    )(*[held(one) for one in (weights, first_group, first_pairs, ring, far)])

    for swap in range(swaps):
        moves = column_swap(swap, swaps, owners, count)
        messages[swap] = held(lax.ppermute(messages[swap], ("date", "col"), moves))
    return pl.pallas_call(
        finish_kernel,
        out_shape=jax.ShapeDtypeStruct(
            (inverse.shape[0], parts, half_rows, columns // 8), F32
        ),
        in_specs=[IN_VMEM] * (swaps + 2),
        out_specs=ANYWHERE,
        scratch_shapes=[
            pltpu.VMEM((parts, half_rows * tall, LANES), F32),
            pltpu.VMEM((parts, inverse.shape[0], half_rows, columns // 8), F32),
            pltpu.SemaphoreType.DMA((parts,)),
        ],
    )(held(looked), held(fold), *messages)


def solution(mesh):
    placed = (P("date", None, "groups", "col"), P("date", None), P("date"), P())
    return jax.shard_map(
        per_device,
        mesh=mesh,
        in_specs=placed,
        out_specs=P(None, None, ("groups", "date"), "col"),
        check_vma=False,
    )
```

```python
import functools

import jax
import jax.numpy as jnp
from jax import lax
from jax.experimental import pallas as pl
from jax.experimental.pallas import tpu as pltpu
from jax.sharding import PartitionSpec as P

F32, BF16 = jnp.float32, jnp.bfloat16
LANES = 128
NOTE = 8
NOTE_ROWS = 2 * NOTE
GROUP = 8
ANYWHERE = pl.BlockSpec(memory_space=pl.ANY)
IN_VMEM = pl.BlockSpec(memory_space=pltpu.VMEM)
IN_SMEM = pl.BlockSpec(memory_space=pltpu.SMEM)


def round_up(value, step):
    return -(-value // step) * step


def held(array):
    return pltpu.with_memory_space_constraint(array, pltpu.VMEM)


def iota(shape, axis):
    return lax.broadcasted_iota(jnp.int32, shape, axis)


def halves(value):
    high = value.astype(BF16)
    return high, (value - high.astype(F32)).astype(BF16)


def blank_kernel(blank_ref):
    blank_ref[...] = jnp.zeros_like(blank_ref)


def comb_of(columns):
    looks = columns // 8
    column, lane = iota((columns, columns), 0), iota((columns, columns), 1)
    here = (column // 8 == lane % looks) & (column % 8 == lane // looks)
    return jnp.where(here, 1.0, 0.0).astype(BF16)


def fold_of(shape, looks, half_rows):
    cell, target = iota(shape, 0), iota(shape, 1)
    right = cell < LANES
    cell = cell % LANES
    half_row = cell // 16
    here = right & (target == half_row * looks + looks - 1)
    here = here | ~right & (target == half_row * looks)
    return jnp.where(here & (half_row < half_rows), 1.0, 0.0).astype(BF16)


def live_kernel(rows, slots, count_ref, blank_ref, live_ref, pick_ref, own_ref, gather_ref):
    columns, (all_rows, lanes), (lines, height) = pick_ref.shape[0], own_ref.shape, gather_ref.shape
    column, lane = iota((columns, lanes), 0), iota((columns, lanes), 1) % 8
    wanted = jnp.where(lane < 4, lane, columns - 8 + lane)
    pick_ref[...] = jnp.where(column == wanted, 1.0, 0.0).astype(BF16)
    row, lane = iota((all_rows, lanes), 0), iota((all_rows, lanes), 1)
    own_ref[...] = jnp.where(row % rows == lane // 8, 1.0, 0.0)
    owners, images = all_rows // rows, height // all_rows
    line, row = iota((lines, height), 0), iota((lines, height), 1) // rows
    place = line % NOTE
    wanted = (place % (images // 2) * 2 + place // (images // 2)) * owners + line // NOTE
    gather_ref[...] = jnp.where((place < images) & (row == wanted), 1.0, 0.0).astype(BF16)
    row, lane = iota(live_ref.shape, 0), iota(live_ref.shape, 1)
    live = (row == 2) & (lane < jnp.minimum(count_ref[0], slots))
    live_ref[...] = jnp.where(live, 1.0, blank_ref[...])


def seam_kernel(scenes_ref, dates_ref, live_ref, pick_ref, own_ref, gather_ref, *refs):
    *block_refs, seams_ref, note_ref, fetched_ref, semaphore = refs
    fetch = pltpu.make_async_copy(dates_ref, fetched_ref, semaphore)
    fetch.start()
    dates_here, parts, all_rows, columns = scenes_ref.shape
    height = dates_here * parts * all_rows
    cells = scenes_ref[...].reshape(height, columns)
    cells = jnp.dot(cells, pick_ref[...], preferred_element_type=F32)
    cells = cells.reshape(dates_here * parts, all_rows, LANES) * own_ref[...][None]
    cells = cells.reshape(height, LANES).astype(BF16)
    lines = jnp.dot(gather_ref[...], cells, preferred_element_type=F32)
    for owner in range(seams_ref.shape[0]):
        seams_ref[owner] = lines[owner * NOTE : (owner + 1) * NOTE]
    note_ref[...] = live_ref[...]
    owners = seams_ref.shape[0]
    for step, block_ref in enumerate(block_refs):
        cut_block(scenes_ref, owners, step, block_ref)
    fetch.wait()
    note_ref[:2, : dates_ref.shape[1]] = fetched_ref[...].astype(F32)
    for step, block_ref in enumerate(block_refs):
        owner = lax.rem(lax.axis_index("date") + owners - step, owners)
        tile = jnp.concatenate([note_ref[...], seams_ref[twin_of(owner, owners)]], axis=0)
        block_ref[block_ref.shape[0] - NOTE_ROWS :] = tile.astype(BF16)


def twin_of(owner, owners):
    return owner + 1 - 2 * (owner % 2) if owners % 2 == 0 else owner


def cut_block(scenes_ref, owners, step, block_ref):
    dates_here, parts, all_rows, columns = scenes_ref.shape
    rows = all_rows // owners
    first = pl.multiple_of(lax.rem(lax.axis_index("date") + owners - step, owners) * rows, rows)
    height = dates_here * parts * rows
    for side in range(columns // LANES):
        cells = scenes_ref[:, :, pl.ds(first, rows), side * LANES : (side + 1) * LANES]
        block_ref[side * height : (side + 1) * height] = cells.reshape(height, LANES)


def cells_of(block_ref, sides):
    height = (block_ref.shape[0] - NOTE_ROWS) // sides
    return jnp.concatenate(
        [block_ref[side * height : (side + 1) * height] for side in range(sides)], axis=1
    )


def cut(scenes, pair_dates, pair_count, owners):
    dates_here, parts, all_rows, columns = scenes.shape
    rows = all_rows // owners
    sides = columns // LANES
    height = dates_here * parts * rows
    blank = pl.pallas_call(
        blank_kernel,
        out_shape=pltpu.VMEM((NOTE, LANES), F32),
        out_specs=IN_VMEM,
        cost_estimate=pl.CostEstimate(flops=10**9, bytes_accessed=10**7, transcendentals=0),
    )()
    live, *constants = pl.pallas_call(
        functools.partial(live_kernel, rows, pair_dates.shape[1]),
        out_shape=[
            pltpu.VMEM((NOTE, LANES), F32),
            pltpu.VMEM((columns, LANES), BF16),
            pltpu.VMEM((all_rows, LANES), F32),
            pltpu.VMEM((owners * NOTE, dates_here * parts * all_rows), BF16),
        ],
        in_specs=[IN_SMEM, IN_VMEM],
        out_specs=[IN_VMEM] * 4,
    )(pair_count, held(blank))
    aligned = rows % 16 == 0
    lines = [pltpu.VMEM((owners, NOTE, LANES), F32), pltpu.VMEM((NOTE, LANES), F32)]
    blocks = pl.pallas_call(
        seam_kernel,
        out_shape=[pltpu.VMEM((sides * height + NOTE_ROWS, LANES), BF16)] * owners
        if aligned
        else lines,
        in_specs=[IN_VMEM, ANYWHERE] + [IN_VMEM] * 4,
        out_specs=[IN_VMEM] * (owners if aligned else 2),
        scratch_shapes=[
            *(lines if aligned else []),
            pltpu.VMEM(pair_dates.shape, jnp.int32),
            pltpu.SemaphoreType.DMA,
        ],
    )(held(scenes), pair_dates, held(live), *[held(array) for array in constants])
    if aligned:
        return list(blocks)
    seams, note = blocks
    blocks = []
    me = lax.axis_index("date")
    apart = scenes.reshape(dates_here * parts, owners, rows, columns)
    for step in range(owners):
        owner = lax.rem(me + owners - step, owners)
        cells = lax.dynamic_index_in_dim(apart, owner, 1, False).reshape(height, columns)
        strips = [cells[:, side * LANES : (side + 1) * LANES] for side in range(sides)]
        seam = lax.dynamic_index_in_dim(seams, twin_of(owner, owners), 0, False)
        strips += [note.astype(BF16), seam.astype(BF16)]
        blocks.append(jnp.concatenate(strips, axis=0))
    return blocks


def pair_places(first, second, dates):
    groups = dates // GROUP

    def group_of(date):
        return jnp.floor(date * (1.0 / GROUP))

    first_group, second_group = group_of(first), group_of(second)
    first_seat, second_seat = first - GROUP * first_group, second - GROUP * second_group
    ahead = second_seat - first_seat
    ahead = jnp.where(ahead < 0.0, ahead + GROUP, ahead)
    behind = jnp.where(ahead > 0.0, GROUP - ahead, 0.0)
    near = ahead <= GROUP // 2
    inside = first_group * (GROUP * GROUP // 2)
    inside = inside + jnp.where(
        near, (ahead - 1.0) * GROUP + first_seat, (behind - 1.0) * GROUP + second_seat
    )
    upward = first_group < second_group
    low, high = jnp.minimum(first_group, second_group), jnp.maximum(first_group, second_group)
    between = low * (2 * groups - 1.0 - low) * 0.5 + high - low - 1.0
    across = groups * (GROUP * GROUP // 2) + between * (GROUP * GROUP)
    across = across + jnp.where(
        upward, ahead * GROUP + first_seat, behind * GROUP + second_seat
    )
    same = first_group == second_group
    sign = jnp.where(same, jnp.where(near, 1.0, -1.0), jnp.where(upward, 1.0, -1.0))
    return jnp.where(same, inside, across), sign


def inverse_of(wide, step, owners, slots):
    lanes = wide.shape[1]
    owner = lax.rem(lax.axis_index("date") + step, owners)
    moved = pltpu.roll(wide, lax.rem(lanes - owner * slots, lanes), 1)
    return moved[:, :LANES] * (1.0 / 128.0)


def slot_weights(block_ref, inverse, owners, dates_here):
    dates = owners * dates_here
    start = lax.rem(lax.axis_index("date") + owners - 1, owners) * dates_here
    start = jnp.full((1, LANES), start, jnp.int32).astype(F32)
    height = block_ref.shape[0]
    note = block_ref[height - NOTE_ROWS : height].astype(F32)

    def wrapped(value):
        return jnp.where(value < 0.0, value + dates, value)

    place, sign = pair_places(wrapped(note[0:1] - start), wrapped(note[1:2] - start), dates)
    place = jnp.where(note[2:3] > 0.5, place, -1.0)
    pairs = pair_rows(dates)
    chosen = jnp.where(iota((pairs, LANES), 0).astype(F32) == place, 1.0, 0.0).astype(BF16)
    stacked = jnp.concatenate([*halves(inverse), *halves(inverse * sign)], axis=0)
    spread = lax.dot_general(
        stacked, chosen, (((1,), (1,)), ((), ())), preferred_element_type=F32
    )
    tall = inverse.shape[0]
    parts = [spread[at * tall : (at + 1) * tall] for at in range(4)]
    return parts[0] + parts[1], parts[2] + parts[3]


def pair_rows(dates):
    groups = dates // GROUP
    return GROUP * GROUP // 2 * groups + GROUP * GROUP * (groups * (groups - 1) // 2)


def pair_units(dates):
    groups = dates // GROUP
    half = GROUP // 2
    units = [(group, group, range(1, half + 1)) for group in range(groups)]
    for low in range(groups):
        for high in range(low + 1, groups):
            units += [(low, high, range(at, at + half)) for at in range(0, GROUP, half)]
    return units


def spread_block(block_ref, comb, dates_here, seat, rows_ref):
    sides = rows_ref.shape[1]
    combed = jnp.dot(cells_of(block_ref, sides), comb, preferred_element_type=F32)
    rows = combed.shape[0] // (2 * dates_here)
    for own in range(dates_here):
        for part in range(2):
            at = (own * 2 + part) * rows
            for side in range(sides):
                rows_ref[part, side, pl.ds(seat + own, rows, stride=GROUP), :] = combed[
                    at : at + rows, side * LANES : (side + 1) * LANES
                ]


def pack_group(rows_ref, looks, half_rows, store):
    pack = LANES // looks
    lane = iota((GROUP, LANES), 1)
    for part in range(2):
        for odd in range(2):
            for tile in range(-(-half_rows // pack)):
                for side in range(rows_ref.shape[1]):
                    cells = []
                    for near in range(pack):
                        half_row = tile * pack + near
                        at = (2 * half_row + odd) * GROUP
                        if half_row < half_rows:
                            cells.append(rows_ref[part, side, at : at + GROUP, :])
                        else:
                            cells.append(jnp.zeros((GROUP, LANES), F32))
                    bit = pack // 2
                    while bit:
                        clear = (lane // looks) & bit == 0
                        for near in range(pack):
                            if not near & bit:
                                one, two = cells[near], cells[near + bit]
                                cells[near] = jnp.where(
                                    clear, one, pltpu.roll(two, bit * looks, 1)
                                )
                                cells[near + bit] = jnp.where(
                                    clear, pltpu.roll(one, LANES - bit * looks, 1), two
                                )
                        bit //= 2
                    for near in range(pack):
                        store(part, odd, side * pack + near, tile, cells[near])


def unit_products(tile, looks, turns, mine_of, turned_of, store):
    lane = iota((GROUP, LANES), 1) % looks
    at_first, at_last = lane == 0, lane == looks - 1

    def product(place):
        mine = [[mine_of(part, odd, place, tile) for odd in range(2)] for part in range(2)]
        values = []
        for turn in turns:
            other = [
                [turned_of(part, odd, place, tile, turn, mine) for odd in range(2)]
                for part in range(2)
            ]
            real = (mine[0][0] * other[0][0] + mine[1][0] * other[1][0]) + (
                mine[0][1] * other[0][1] + mine[1][1] * other[1][1]
            )
            imaginary = (mine[1][0] * other[0][0] - mine[0][0] * other[1][0]) + (
                mine[1][1] * other[0][1] - mine[0][1] * other[1][1]
            )
            values += [real, imaginary]
        return values

    def running(places):
        total = product(places[0])
        ramp = total
        for place in places[1:]:
            total = [one + two for one, two in zip(total, product(place))]
            share = [0.5 * one for one in total] if place is places[-1] else total
            ramp = [one + two for one, two in zip(ramp, share)]
        return total, ramp

    early, to_left = running((0, 1, 2, 3))
    late, to_right = running((7, 6, 5, 4))
    values = []
    for index in range(len(early)):
        before = pltpu.roll(to_right[index], 1, 1)
        after = pltpu.roll(to_left[index], LANES - 1, 1)
        value = 8.0 * (early[index] + late[index]) - to_left[index] - to_right[index]
        value = value + jnp.where(at_first, 0.0, before) + jnp.where(at_last, 0.0, after)
        values.append(value)
    for part in range(2):
        store(part, tile, jnp.concatenate(values[part::2], axis=0))


def turn_here(part, odd, place, tile, turn, mine):
    return pltpu.roll(mine[part][odd], GROUP - turn, 0)


def seam_of(block_ref, dates_here, seat, seam_ref):
    height = block_ref.shape[0]
    lines = block_ref[height - NOTE_ROWS : height].astype(F32)
    for part in range(2):
        at = NOTE + part * dates_here
        seam_ref[part, seat : seat + dates_here, :] = lines[at : at + dates_here]


def early_kernel(dates_here, *refs):
    *block_refs, comb_ref, fold_ref, ring_ref, pair_ref, seam_ref, rows_ref = refs
    columns = comb_ref.shape[0]
    looks = columns // 8
    tiles = ring_ref.shape[3]
    half_rows = rows_ref.shape[2] // GROUP // 2
    comb = comb_of(columns)
    comb_ref[...] = comb
    fold_ref[...] = fold_of(fold_ref.shape, looks, half_rows)
    for index, block_ref in enumerate(block_refs):
        spread_block(block_ref, comb, dates_here, index * dates_here, rows_ref)
        seam_of(block_ref, dates_here, index * dates_here, seam_ref)

    def keep(part, odd, place, tile, cells):
        ring_ref[part, odd, place, tile] = cells

    pack_group(rows_ref, looks, half_rows, keep)

    def store(part, tile, value):
        across = slice(tile * LANES, (tile + 1) * LANES)
        high, low = halves(value)
        pair_ref[part, 0, :, across] = high
        pair_ref[part, 1, :, across] = low

    for tile in range(tiles):
        unit_products(
            tile,
            looks,
            range(1, GROUP // 2 + 1),
            lambda part, odd, place, tile: ring_ref[part, odd, place, tile],
            turn_here,
            store,
        )


def place_of(step, owners, dates_here):
    date = (step + 1) % owners * dates_here
    return date // GROUP, date % GROUP


def middle_kernel(dates_here, slots, steps, *refs):
    *refs, rows_ref, seams_ref, partial_ref, rest_ref, wide_ref = refs
    comb_ref, inverse_ref, *block_refs = refs
    owners = len(block_refs) + 1
    comb = comb_ref[...]
    wide_ref[...] = jnp.zeros_like(wide_ref)
    wide_ref[: inverse_ref.shape[0], : inverse_ref.shape[1]] = inverse_ref[...]
    wide = wide_ref[...]
    sums = [0.0, 0.0]
    for step, block_ref in zip(steps, block_refs):
        group, seat = place_of(step, owners, dates_here)
        if group:
            spread_block(block_ref, comb, dates_here, seat, rows_ref.at[group - 1])
            seam_of(block_ref, dates_here, seat, seams_ref.at[group - 1])
        more = slot_weights(block_ref, inverse_of(wide, step, owners, slots), owners, dates_here)
        sums = [one + two for one, two in zip(sums, more)]
    for part in range(2):
        partial_ref[part] = sums[part]
    rest_ref[...] = inverse_of(wide, 1, owners, slots)


def edge_kernel(dates_here, owners, *refs):
    block_ref, seam_ref, others_ref, partial_ref, rest_ref, comb_ref, other_rows_ref, *refs = refs
    weights_ref, ring_ref, far_ref, *message_refs, seams_ref, pair_ref, rows_ref = refs
    dates = owners * dates_here
    pairs = pair_rows(dates)
    tall = rest_ref.shape[0]

    group, seat = place_of(1, owners, dates_here)
    rows_ref[...] = other_rows_ref[...]
    spread_block(block_ref, comb_ref[...], dates_here, seat, rows_ref.at[group - 1])
    seams_ref[...] = others_ref[...]
    seam_of(block_ref, dates_here, seat, seams_ref.at[group - 1])
    weights = []
    for part, more in enumerate(slot_weights(block_ref, rest_ref[...], owners, dates_here)):
        high, low = halves(partial_ref[part] + more)
        wide = [jnp.concatenate([half, half], axis=1) for half in (high, low)]
        weights.append(jnp.concatenate(wide, axis=0))
        weights_ref[part] = weights[part]

    lane = iota((GROUP, LANES), 1) % 8
    ramp = jnp.where(lane < 4, 3.5 - lane.astype(F32), lane.astype(F32) - 3.5)
    for unit, (low, high, turns) in enumerate(pair_units(dates)):
        mine = [(seams_ref[low - 1, part] if low else seam_ref[part]) * ramp for part in range(2)]
        theirs = [seams_ref[high - 1, part] if high else seam_ref[part] for part in range(2)]
        values = []
        for turn in turns:
            other = [pltpu.roll(cells, GROUP - turn, 0) if turn else cells for cells in theirs]
            values.append(mine[0] * other[0] + mine[1] * other[1])
            values.append(mine[1] * other[0] - mine[0] * other[1])
        for part in range(2):
            value = jnp.concatenate(values[part::2], axis=0)
            count = value.shape[0]
            bits = halves(value)
            for half in range(2):
                at = half * pairs + unit * count
                pair_ref[part, at : at + count, :] = bits[half]
    looks = comb_ref.shape[0] // 8
    half_rows = rows_ref.shape[3] // GROUP // 2
    for group in range(1, dates // GROUP):

        def keep(part, odd, place, tile, cells):
            ring_ref[group - 1, part, odd, place, tile] = cells
            for copy in range(2):
                at = pl.ds(2 * copy * GROUP + odd, GROUP, stride=2)
                far_ref[group - 1, part, place, tile, at, :] = cells

        pack_group(rows_ref.at[group - 1], looks, half_rows, keep)
    sums = []
    for part in range(2):
        summed = jnp.dot(weights[part], pair_ref[part], preferred_element_type=F32)
        sums.append(summed[:tall] + summed[tall:])
    head = iota((tall, LANES), 1) % 8 < 4
    to_left = jnp.where(head, sums[0], pltpu.roll(sums[1], 4, 1))
    to_right = jnp.where(head, pltpu.roll(sums[0], LANES - 4, 1), sums[1])
    here = lax.rem(lax.axis_index("col"), len(message_refs))
    for swap, message_ref in enumerate(message_refs):
        message_ref[...] = jnp.where(here == swap, to_right, to_left)


def series_kernel(looks, *refs):
    weights_ref, first_ref, first_pair_ref, ring_ref, far_ref, looked_ref, pair_ref = refs
    groups = 1 + ring_ref.shape[0]
    dates = groups * GROUP
    pairs = pair_rows(dates)
    tiles = ring_ref.shape[4]
    tall = looked_ref.shape[1]

    for part in range(2):
        for half in range(2):
            at = half * pairs
            pair_ref[part, at : at + first_pair_ref.shape[2], :] = first_pair_ref[part, half]
    for tile in range(tiles):
        for unit, (low, high, turns) in enumerate(pair_units(dates)):
            if high == 0:
                continue

            def mine_of(part, odd, place, tile):
                if low == 0:
                    return first_ref[part, odd, place, tile]
                return ring_ref[low - 1, part, odd, place, tile]

            def turn_far(part, odd, place, tile, turn, mine):
                at = pl.ds(2 * turn + odd, GROUP, stride=2)
                return far_ref[high - 1, part, place, tile, at, :]

            def store(part, tile, value):
                count = value.shape[0]
                across = slice(tile * LANES, (tile + 1) * LANES)
                bits = halves(value)
                for half in range(2):
                    at = half * pairs + unit * count
                    pair_ref[part, at : at + count, across] = bits[half]

            turned_of = turn_here if low == high else turn_far
            unit_products(tile, looks, turns, mine_of, turned_of, store)
        across = slice(tile * LANES, (tile + 1) * LANES)
        for part in range(2):
            summed = jnp.dot(
                weights_ref[part], pair_ref[part, :, across], preferred_element_type=F32
            )
            looked_ref[part, :, across] = summed[:tall] + summed[tall:]


def finish_kernel(looked_ref, fold_ref, *refs):
    *message_refs, out_ref, sum_ref, done_ref, semaphores = refs
    parts, times, half_rows, looks = done_ref.shape
    tall = looked_ref.shape[1]
    pack = LANES // looks
    here, last = lax.axis_index("col"), lax.axis_size("col") - 1
    swaps = len(message_refs)
    from_right = from_left = jnp.zeros((tall, LANES), F32)
    for swap, message_ref in enumerate(message_refs):
        message = message_ref[...]
        from_right = jnp.where((here != last) & (here % swaps == swap), message, from_right)
        from_left = jnp.where((here != 0) & ((here - 1) % swaps == swap), message, from_left)
    edges = jnp.concatenate([from_right, from_left], axis=1)
    head = iota(edges.shape, 1) % 8 < 4
    edges = [jnp.where(head, edges, 0.0), jnp.where(head, 0.0, edges)]
    edges = jnp.concatenate(halves(jnp.concatenate(edges, axis=0)), axis=0)
    edges = jnp.dot(edges, fold_ref[...], preferred_element_type=F32)
    edges = edges[: parts * tall] + edges[parts * tall :]
    sent = []
    for part in range(parts):
        value = looked_ref[part] + edges[part * tall : (part + 1) * tall]
        for half_row in range(half_rows):
            tile, near = half_row // pack, half_row % pack
            one = value[:, tile * LANES : (tile + 1) * LANES]
            at = half_row * tall
            sum_ref[part, at : at + tall, :] = pltpu.roll(one, -near * looks % LANES, 1)
        for time in range(times):
            rows = sum_ref[part, pl.ds(time, half_rows, stride=tall), :]
            done_ref[part, time] = rows[:, :looks]
        sent.append(
            pltpu.make_async_copy(done_ref.at[part], out_ref.at[:, part], semaphores.at[part])
        )
        sent[part].start()
    for copy in sent:
        copy.wait()


def column_swap(swap, swaps, owners, count):
    moves = []
    for owner in range(owners):
        for column in range(count):
            partner = column
            if column % swaps == swap and column + 1 < count:
                partner = column + 1
            elif column and (column - 1) % swaps == swap:
                partner = column - 1
            moves.append((owner * count + column, twin_of(owner, owners) * count + partner))
    return moves


def per_device(scenes, pair_dates, pair_count, inverse):
    owners, count = lax.axis_size("date"), lax.axis_size("col")
    dates_here, parts, all_rows, columns = scenes.shape
    half_rows = all_rows // owners // 2
    dates = owners * dates_here
    pairs = pair_rows(dates)
    looks = columns // 8
    tiles = -(-half_rows // (LANES // looks))

    blocks = cut(scenes, pair_dates.T, pair_count, owners)
    for step in range(1, owners):
        moves = [(owner, (owner - step) % owners) for owner in range(owners)]
        blocks[step] = lax.ppermute(blocks[step], "date", moves)

    tall = round_up(inverse.shape[0], 16)
    rows = 2 * half_rows
    sides = columns // LANES
    order = [blocks[(place - 1) % owners] for place in range(owners)]
    order = [held(block) for block in order]
    group_rows = pltpu.VMEM((parts, sides, rows * GROUP, LANES), F32)
    comb, fold, first_group, first_pairs, first_seam = pl.pallas_call(
        functools.partial(early_kernel, dates_here),
        out_shape=[
            pltpu.VMEM((columns, columns), BF16),
            pltpu.VMEM((2 * LANES, tiles * LANES), BF16),
            pltpu.VMEM((parts, 2, 8, tiles, GROUP, LANES), F32),
            pltpu.VMEM((parts, 2, GROUP * GROUP // 2, tiles * LANES), BF16),
            pltpu.VMEM((parts, GROUP, LANES), F32),
        ],
        in_specs=[IN_VMEM] * (GROUP // dates_here),
        out_specs=[IN_VMEM] * 5,
        scratch_shapes=[group_rows],
        compiler_params=pltpu.CompilerParams(vmem_limit_bytes=40 << 20),
    )(*order[: GROUP // dates_here])
    others = dates // GROUP - 1
    steps = [*range(owners - 1, 1, -1), 0]
    group_rows = pltpu.VMEM((others, *group_rows.shape), F32)
    other_rows, other_seams, partial, rest = pl.pallas_call(
        functools.partial(middle_kernel, dates_here, pair_dates.shape[0], steps),
        out_shape=[
            group_rows,
            pltpu.VMEM((others, parts, GROUP, LANES), F32),
            pltpu.VMEM((parts, tall, pairs), F32),
            pltpu.VMEM((tall, LANES), F32),
        ],
        in_specs=[IN_VMEM] * (owners + 1),
        out_specs=[IN_VMEM] * 4,
        scratch_shapes=[pltpu.VMEM((tall, round_up(inverse.shape[1], LANES)), F32)],
        compiler_params=pltpu.CompilerParams(vmem_limit_bytes=40 << 20),
    )(held(comb), held(inverse), *[held(blocks[step]) for step in steps])
    swaps = min(3, count - 1)
    weights, ring, far, *messages = pl.pallas_call(
        functools.partial(edge_kernel, dates_here, owners),
        out_shape=[
            pltpu.VMEM((parts, 2 * tall, 2 * pairs), BF16),
            pltpu.VMEM((others, parts, 2, 8, tiles, GROUP, LANES), F32),
            pltpu.VMEM((others, parts, 8, tiles, 4 * GROUP, LANES), F32),
            *[pltpu.VMEM((tall, LANES), F32)] * swaps,
        ],
        in_specs=[IN_VMEM] * 7,
        out_specs=[IN_VMEM] * (swaps + 3),
        scratch_shapes=[
            pltpu.VMEM((others, parts, GROUP, LANES), F32),
            pltpu.VMEM((parts, 2 * pairs, LANES), BF16),
            group_rows,
        ],
        compiler_params=pltpu.CompilerParams(vmem_limit_bytes=40 << 20),
    )(
        *[held(one) for one in (blocks[1], first_seam, other_seams, partial, rest, comb)],
        held(other_rows),
    )
    looked = pl.pallas_call(
        functools.partial(series_kernel, looks),
        out_shape=pltpu.VMEM((parts, tall, tiles * LANES), F32),
        in_specs=[IN_VMEM] * 5,
        out_specs=IN_VMEM,
        scratch_shapes=[pltpu.VMEM((parts, 2 * pairs, tiles * LANES), BF16)],
        compiler_params=pltpu.CompilerParams(vmem_limit_bytes=40 << 20),
        cost_estimate=pl.CostEstimate(
            flops=2 * parts * pairs * columns * rows * 8, bytes_accessed=1 << 20, transcendentals=0
        ),
    )(*[held(one) for one in (weights, first_group, first_pairs, ring, far)])

    for swap in range(swaps):
        moves = column_swap(swap, swaps, owners, count)
        messages[swap] = held(lax.ppermute(messages[swap], ("date", "col"), moves))
    return pl.pallas_call(
        finish_kernel,
        out_shape=jax.ShapeDtypeStruct(
            (inverse.shape[0], parts, half_rows, columns // 8), F32
        ),
        in_specs=[IN_VMEM] * (swaps + 2),
        out_specs=ANYWHERE,
        scratch_shapes=[
            pltpu.VMEM((parts, half_rows * tall, LANES), F32),
            pltpu.VMEM((parts, inverse.shape[0], half_rows, columns // 8), F32),
            pltpu.SemaphoreType.DMA((parts,)),
        ],
    )(held(looked), held(fold), *messages)


def solution(mesh):
    placed = (P("date", None, "groups", "col"), P("date", None), P("date"), P())
    return jax.shard_map(
        per_device,
        mesh=mesh,
        in_specs=placed,
        out_specs=P(None, None, ("groups", "date"), "col"),
        check_vma=False,
    )
```

```python
import functools

import jax
import jax.numpy as jnp
from jax import lax
from jax.experimental import pallas as pl
from jax.experimental.pallas import tpu as pltpu
from jax.sharding import PartitionSpec as P

F32, BF16 = jnp.float32, jnp.bfloat16
LANES = 128
NOTE = 8
NOTE_ROWS = 2 * NOTE
GROUP = 8
ANYWHERE = pl.BlockSpec(memory_space=pl.ANY)
IN_VMEM = pl.BlockSpec(memory_space=pltpu.VMEM)
IN_SMEM = pl.BlockSpec(memory_space=pltpu.SMEM)


def round_up(value, step):
    return -(-value // step) * step


def held(array):
    return pltpu.with_memory_space_constraint(array, pltpu.VMEM)


def iota(shape, axis):
    return lax.broadcasted_iota(jnp.int32, shape, axis)


def halves(value):
    high = value.astype(BF16)
    return high, (value - high.astype(F32)).astype(BF16)


def blank_kernel(blank_ref):
    blank_ref[...] = jnp.zeros_like(blank_ref)


def comb_of(columns):
    looks = columns // 8
    column, lane = iota((columns, columns), 0), iota((columns, columns), 1)
    here = (column // 8 == lane % looks) & (column % 8 == lane // looks)
    return jnp.where(here, 1.0, 0.0).astype(BF16)


def fold_of(shape, looks, half_rows):
    cell, target = iota(shape, 0), iota(shape, 1)
    right = cell < LANES
    cell = cell % LANES
    half_row = cell // 16
    here = right & (target == half_row * looks + looks - 1)
    here = here | ~right & (target == half_row * looks)
    return jnp.where(here & (half_row < half_rows), 1.0, 0.0).astype(BF16)


def live_kernel(rows, slots, count_ref, blank_ref, live_ref, pick_ref, own_ref, gather_ref):
    columns, (all_rows, lanes), (lines, height) = pick_ref.shape[0], own_ref.shape, gather_ref.shape
    column, lane = iota((columns, lanes), 0), iota((columns, lanes), 1) % 8
    wanted = jnp.where(lane < 4, lane, columns - 8 + lane)
    pick_ref[...] = jnp.where(column == wanted, 1.0, 0.0).astype(BF16)
    row, lane = iota((all_rows, lanes), 0), iota((all_rows, lanes), 1)
    own_ref[...] = jnp.where(row % rows == lane // 8, 1.0, 0.0)
    owners, images = all_rows // rows, height // all_rows
    line, row = iota((lines, height), 0), iota((lines, height), 1) // rows
    place = line % NOTE
    wanted = (place % (images // 2) * 2 + place // (images // 2)) * owners + line // NOTE
    gather_ref[...] = jnp.where((place < images) & (row == wanted), 1.0, 0.0).astype(BF16)
    row, lane = iota(live_ref.shape, 0), iota(live_ref.shape, 1)
    live = (row == 2) & (lane < jnp.minimum(count_ref[0], slots))
    live_ref[...] = jnp.where(live, 1.0, blank_ref[...])


def seam_kernel(scenes_ref, dates_ref, live_ref, pick_ref, own_ref, gather_ref, *refs):
    *block_refs, seams_ref, note_ref, fetched_ref, semaphore = refs
    fetch = pltpu.make_async_copy(dates_ref, fetched_ref, semaphore)
    fetch.start()
    dates_here, parts, all_rows, columns = scenes_ref.shape
    height = dates_here * parts * all_rows
    cells = scenes_ref[...].reshape(height, columns)
    cells = jnp.dot(cells, pick_ref[...], preferred_element_type=F32)
    cells = cells.reshape(dates_here * parts, all_rows, LANES) * own_ref[...][None]
    cells = cells.reshape(height, LANES).astype(BF16)
    lines = jnp.dot(gather_ref[...], cells, preferred_element_type=F32)
    for owner in range(seams_ref.shape[0]):
        seams_ref[owner] = lines[owner * NOTE : (owner + 1) * NOTE]
    note_ref[...] = live_ref[...]
    owners = seams_ref.shape[0]
    for step, block_ref in enumerate(block_refs):
        cut_block(scenes_ref, owners, step, block_ref)
    fetch.wait()
    note_ref[:2, : dates_ref.shape[1]] = fetched_ref[...].astype(F32)
    for step, block_ref in enumerate(block_refs):
        owner = lax.rem(lax.axis_index("date") + owners - step, owners)
        tile = jnp.concatenate([note_ref[...], seams_ref[twin_of(owner, owners)]], axis=0)
        block_ref[block_ref.shape[0] - NOTE_ROWS :] = tile.astype(BF16)


def twin_of(owner, owners):
    return owner + 1 - 2 * (owner % 2) if owners % 2 == 0 else owner


def cut_block(scenes_ref, owners, step, block_ref):
    dates_here, parts, all_rows, columns = scenes_ref.shape
    rows = all_rows // owners
    first = pl.multiple_of(lax.rem(lax.axis_index("date") + owners - step, owners) * rows, rows)
    height = dates_here * parts * rows
    for side in range(columns // LANES):
        cells = scenes_ref[:, :, pl.ds(first, rows), side * LANES : (side + 1) * LANES]
        block_ref[side * height : (side + 1) * height] = cells.reshape(height, LANES)


def cells_of(block_ref, sides):
    height = (block_ref.shape[0] - NOTE_ROWS) // sides
    return jnp.concatenate(
        [block_ref[side * height : (side + 1) * height] for side in range(sides)], axis=1
    )


def cut(scenes, pair_dates, pair_count, owners):
    dates_here, parts, all_rows, columns = scenes.shape
    rows = all_rows // owners
    sides = columns // LANES
    height = dates_here * parts * rows
    blank = pl.pallas_call(
        blank_kernel,
        out_shape=pltpu.VMEM((NOTE, LANES), F32),
        out_specs=IN_VMEM,
        cost_estimate=pl.CostEstimate(flops=10**9, bytes_accessed=10**7, transcendentals=0),
    )()
    live, *constants = pl.pallas_call(
        functools.partial(live_kernel, rows, pair_dates.shape[1]),
        out_shape=[
            pltpu.VMEM((NOTE, LANES), F32),
            pltpu.VMEM((columns, LANES), BF16),
            pltpu.VMEM((all_rows, LANES), F32),
            pltpu.VMEM((owners * NOTE, dates_here * parts * all_rows), BF16),
        ],
        in_specs=[IN_SMEM, IN_VMEM],
        out_specs=[IN_VMEM] * 4,
    )(pair_count, held(blank))
    aligned = rows % 16 == 0
    lines = [pltpu.VMEM((owners, NOTE, LANES), F32), pltpu.VMEM((NOTE, LANES), F32)]
    blocks = pl.pallas_call(
        seam_kernel,
        out_shape=[pltpu.VMEM((sides * height + NOTE_ROWS, LANES), BF16)] * owners
        if aligned
        else lines,
        in_specs=[IN_VMEM, ANYWHERE] + [IN_VMEM] * 4,
        out_specs=[IN_VMEM] * (owners if aligned else 2),
        scratch_shapes=[
            *(lines if aligned else []),
            pltpu.VMEM(pair_dates.shape, jnp.int32),
            pltpu.SemaphoreType.DMA,
        ],
    )(held(scenes), pair_dates, held(live), *[held(array) for array in constants])
    if aligned:
        return list(blocks)
    seams, note = blocks
    blocks = []
    me = lax.axis_index("date")
    apart = scenes.reshape(dates_here * parts, owners, rows, columns)
    for step in range(owners):
        owner = lax.rem(me + owners - step, owners)
        cells = lax.dynamic_index_in_dim(apart, owner, 1, False).reshape(height, columns)
        strips = [cells[:, side * LANES : (side + 1) * LANES] for side in range(sides)]
        seam = lax.dynamic_index_in_dim(seams, twin_of(owner, owners), 0, False)
        strips += [note.astype(BF16), seam.astype(BF16)]
        blocks.append(jnp.concatenate(strips, axis=0))
    return blocks


def pair_places(first, second, dates):
    groups = dates // GROUP

    def group_of(date):
        return jnp.floor(date * (1.0 / GROUP))

    first_group, second_group = group_of(first), group_of(second)
    first_seat, second_seat = first - GROUP * first_group, second - GROUP * second_group
    ahead = second_seat - first_seat
    ahead = jnp.where(ahead < 0.0, ahead + GROUP, ahead)
    behind = jnp.where(ahead > 0.0, GROUP - ahead, 0.0)
    near = ahead <= GROUP // 2
    inside = first_group * (GROUP * GROUP // 2)
    inside = inside + jnp.where(
        near, (ahead - 1.0) * GROUP + first_seat, (behind - 1.0) * GROUP + second_seat
    )
    upward = first_group < second_group
    low, high = jnp.minimum(first_group, second_group), jnp.maximum(first_group, second_group)
    between = low * (2 * groups - 1.0 - low) * 0.5 + high - low - 1.0
    across = groups * (GROUP * GROUP // 2) + between * (GROUP * GROUP)
    across = across + jnp.where(
        upward, ahead * GROUP + first_seat, behind * GROUP + second_seat
    )
    same = first_group == second_group
    sign = jnp.where(same, jnp.where(near, 1.0, -1.0), jnp.where(upward, 1.0, -1.0))
    return jnp.where(same, inside, across), sign


def inverse_of(wide, step, owners, slots):
    lanes = wide.shape[1]
    owner = lax.rem(lax.axis_index("date") + step, owners)
    moved = pltpu.roll(wide, lax.rem(lanes - owner * slots, lanes), 1)
    return moved[:, :LANES] * (1.0 / 128.0)


def slot_weights(block_ref, inverse, owners, dates_here):
    dates = owners * dates_here
    start = lax.rem(lax.axis_index("date") + owners - 1, owners) * dates_here
    start = jnp.full((1, LANES), start, jnp.int32).astype(F32)
    height = block_ref.shape[0]
    note = block_ref[height - NOTE_ROWS : height].astype(F32)

    def wrapped(value):
        return jnp.where(value < 0.0, value + dates, value)

    place, sign = pair_places(wrapped(note[0:1] - start), wrapped(note[1:2] - start), dates)
    place = jnp.where(note[2:3] > 0.5, place, -1.0)
    pairs = pair_rows(dates)
    chosen = jnp.where(iota((pairs, LANES), 0).astype(F32) == place, 1.0, 0.0).astype(BF16)
    stacked = jnp.concatenate([*halves(inverse), *halves(inverse * sign)], axis=0)
    spread = lax.dot_general(
        stacked, chosen, (((1,), (1,)), ((), ())), preferred_element_type=F32
    )
    tall = inverse.shape[0]
    parts = [spread[at * tall : (at + 1) * tall] for at in range(4)]
    return parts[0] + parts[1], parts[2] + parts[3]


def pair_rows(dates):
    groups = dates // GROUP
    return GROUP * GROUP // 2 * groups + GROUP * GROUP * (groups * (groups - 1) // 2)


def pair_units(dates):
    groups = dates // GROUP
    half = GROUP // 2
    units = [(group, group, range(1, half + 1)) for group in range(groups)]
    for low in range(groups):
        for high in range(low + 1, groups):
            units += [(low, high, range(at, at + half)) for at in range(0, GROUP, half)]
    return units


def spread_block(block_ref, comb, dates_here, seat, rows_ref):
    sides = rows_ref.shape[1]
    combed = jnp.dot(cells_of(block_ref, sides), comb, preferred_element_type=F32)
    rows = combed.shape[0] // (2 * dates_here)
    for own in range(dates_here):
        for part in range(2):
            at = (own * 2 + part) * rows
            for side in range(sides):
                rows_ref[part, side, pl.ds(seat + own, rows, stride=GROUP), :] = combed[
                    at : at + rows, side * LANES : (side + 1) * LANES
                ]


def pack_group(rows_ref, looks, half_rows, store):
    pack = LANES // looks
    lane = iota((GROUP, LANES), 1)
    for part in range(2):
        for odd in range(2):
            for tile in range(-(-half_rows // pack)):
                for side in range(rows_ref.shape[1]):
                    cells = []
                    for near in range(pack):
                        half_row = tile * pack + near
                        at = (2 * half_row + odd) * GROUP
                        if half_row < half_rows:
                            cells.append(rows_ref[part, side, at : at + GROUP, :])
                        else:
                            cells.append(jnp.zeros((GROUP, LANES), F32))
                    bit = pack // 2
                    while bit:
                        clear = (lane // looks) & bit == 0
                        for near in range(pack):
                            if not near & bit:
                                one, two = cells[near], cells[near + bit]
                                cells[near] = jnp.where(
                                    clear, one, pltpu.roll(two, bit * looks, 1)
                                )
                                cells[near + bit] = jnp.where(
                                    clear, pltpu.roll(one, LANES - bit * looks, 1), two
                                )
                        bit //= 2
                    for near in range(pack):
                        store(part, odd, side * pack + near, tile, cells[near])


def unit_products(tile, looks, turns, mine_of, turned_of, store):
    lane = iota((GROUP, LANES), 1) % looks
    at_first, at_last = lane == 0, lane == looks - 1

    def product(place):
        mine = [[mine_of(part, odd, place, tile) for odd in range(2)] for part in range(2)]
        values = []
        for turn in turns:
            other = [
                [turned_of(part, odd, place, tile, turn, mine) for odd in range(2)]
                for part in range(2)
            ]
            real = (mine[0][0] * other[0][0] + mine[1][0] * other[1][0]) + (
                mine[0][1] * other[0][1] + mine[1][1] * other[1][1]
            )
            imaginary = (mine[1][0] * other[0][0] - mine[0][0] * other[1][0]) + (
                mine[1][1] * other[0][1] - mine[0][1] * other[1][1]
            )
            values += [real, imaginary]
        return values

    def running(places):
        total = product(places[0])
        ramp = total
        for place in places[1:]:
            total = [one + two for one, two in zip(total, product(place))]
            share = [0.5 * one for one in total] if place is places[-1] else total
            ramp = [one + two for one, two in zip(ramp, share)]
        return total, ramp

    early, to_left = running((0, 1, 2, 3))
    late, to_right = running((7, 6, 5, 4))
    values = []
    for index in range(len(early)):
        before = pltpu.roll(to_right[index], 1, 1)
        after = pltpu.roll(to_left[index], LANES - 1, 1)
        value = 8.0 * (early[index] + late[index]) - to_left[index] - to_right[index]
        value = value + jnp.where(at_first, 0.0, before) + jnp.where(at_last, 0.0, after)
        values.append(value)
    for part in range(2):
        store(part, tile, jnp.concatenate(values[part::2], axis=0))


def turn_here(part, odd, place, tile, turn, mine):
    return pltpu.roll(mine[part][odd], GROUP - turn, 0)


def seam_of(block_ref, dates_here, seat, seam_ref):
    height = block_ref.shape[0]
    lines = block_ref[height - NOTE_ROWS : height].astype(F32)
    for part in range(2):
        at = NOTE + part * dates_here
        seam_ref[part, seat : seat + dates_here, :] = lines[at : at + dates_here]


def early_kernel(dates_here, *refs):
    *block_refs, comb_ref, fold_ref, ring_ref, pair_ref, seam_ref, rows_ref = refs
    columns = comb_ref.shape[0]
    looks = columns // 8
    tiles = ring_ref.shape[3]
    half_rows = rows_ref.shape[2] // GROUP // 2
    comb = comb_of(columns)
    comb_ref[...] = comb
    fold_ref[...] = fold_of(fold_ref.shape, looks, half_rows)
    for index, block_ref in enumerate(block_refs):
        spread_block(block_ref, comb, dates_here, index * dates_here, rows_ref)
        seam_of(block_ref, dates_here, index * dates_here, seam_ref)

    def keep(part, odd, place, tile, cells):
        ring_ref[part, odd, place, tile] = cells

    pack_group(rows_ref, looks, half_rows, keep)

    def store(part, tile, value):
        across = slice(tile * LANES, (tile + 1) * LANES)
        high, low = halves(value)
        pair_ref[part, 0, :, across] = high
        pair_ref[part, 1, :, across] = low

    for tile in range(tiles):
        unit_products(
            tile,
            looks,
            range(1, GROUP // 2 + 1),
            lambda part, odd, place, tile: ring_ref[part, odd, place, tile],
            turn_here,
            store,
        )


def place_of(step, owners, dates_here):
    date = (step + 1) % owners * dates_here
    return date // GROUP, date % GROUP


def middle_kernel(dates_here, slots, steps, *refs):
    *refs, rows_ref, seams_ref, partial_ref, rest_ref, wide_ref = refs
    comb_ref, inverse_ref, *block_refs = refs
    owners = len(block_refs) + 1
    comb = comb_ref[...]
    wide_ref[...] = jnp.zeros_like(wide_ref)
    wide_ref[: inverse_ref.shape[0], : inverse_ref.shape[1]] = inverse_ref[...]
    wide = wide_ref[...]
    sums = [0.0, 0.0]
    for step, block_ref in zip(steps, block_refs):
        group, seat = place_of(step, owners, dates_here)
        if group:
            spread_block(block_ref, comb, dates_here, seat, rows_ref.at[group - 1])
            seam_of(block_ref, dates_here, seat, seams_ref.at[group - 1])
        more = slot_weights(block_ref, inverse_of(wide, step, owners, slots), owners, dates_here)
        sums = [one + two for one, two in zip(sums, more)]
    for part in range(2):
        partial_ref[part] = sums[part]
    rest_ref[...] = inverse_of(wide, 1, owners, slots)


def edge_kernel(dates_here, owners, *refs):
    block_ref, seam_ref, others_ref, partial_ref, rest_ref, comb_ref, other_rows_ref, *refs = refs
    weights_ref, ring_ref, far_ref, *message_refs, seams_ref, pair_ref, rows_ref = refs
    dates = owners * dates_here
    pairs = pair_rows(dates)
    tall = rest_ref.shape[0]

    group, seat = place_of(1, owners, dates_here)
    rows_ref[...] = other_rows_ref[...]
    spread_block(block_ref, comb_ref[...], dates_here, seat, rows_ref.at[group - 1])
    seams_ref[...] = others_ref[...]
    seam_of(block_ref, dates_here, seat, seams_ref.at[group - 1])
    weights = []
    for part, more in enumerate(slot_weights(block_ref, rest_ref[...], owners, dates_here)):
        high, low = halves(partial_ref[part] + more)
        wide = [jnp.concatenate([half, half], axis=1) for half in (high, low)]
        weights.append(jnp.concatenate(wide, axis=0))
        weights_ref[part] = weights[part]

    lane = iota((GROUP, LANES), 1) % 8
    ramp = jnp.where(lane < 4, 3.5 - lane.astype(F32), lane.astype(F32) - 3.5)
    for unit, (low, high, turns) in enumerate(pair_units(dates)):
        mine = [(seams_ref[low - 1, part] if low else seam_ref[part]) * ramp for part in range(2)]
        theirs = [seams_ref[high - 1, part] if high else seam_ref[part] for part in range(2)]
        values = []
        for turn in turns:
            other = [pltpu.roll(cells, GROUP - turn, 0) if turn else cells for cells in theirs]
            values.append(mine[0] * other[0] + mine[1] * other[1])
            values.append(mine[1] * other[0] - mine[0] * other[1])
        for part in range(2):
            value = jnp.concatenate(values[part::2], axis=0)
            count = value.shape[0]
            bits = halves(value)
            for half in range(2):
                at = half * pairs + unit * count
                pair_ref[part, at : at + count, :] = bits[half]
    looks = comb_ref.shape[0] // 8
    half_rows = rows_ref.shape[3] // GROUP // 2
    for group in range(1, dates // GROUP):

        def keep(part, odd, place, tile, cells):
            ring_ref[group - 1, part, odd, place, tile] = cells
            for copy in range(2):
                at = pl.ds(2 * copy * GROUP + odd, GROUP, stride=2)
                far_ref[group - 1, part, place, tile, at, :] = cells

        pack_group(rows_ref.at[group - 1], looks, half_rows, keep)
    sums = []
    for part in range(2):
        summed = jnp.dot(weights[part], pair_ref[part], preferred_element_type=F32)
        sums.append(summed[:tall] + summed[tall:])
    head = iota((tall, LANES), 1) % 8 < 4
    to_left = jnp.where(head, sums[0], pltpu.roll(sums[1], 4, 1))
    to_right = jnp.where(head, pltpu.roll(sums[0], LANES - 4, 1), sums[1])
    here, last = lax.axis_index("col"), lax.axis_size("col") - 1
    for swap, message_ref in enumerate(message_refs):
        onward = (here % len(message_refs) == swap) & (here != last)
        message_ref[...] = jnp.where(onward, to_right, to_left)


def series_kernel(looks, *refs):
    weights_ref, first_ref, first_pair_ref, ring_ref, far_ref, looked_ref, pair_ref = refs
    groups = 1 + ring_ref.shape[0]
    dates = groups * GROUP
    pairs = pair_rows(dates)
    tiles = ring_ref.shape[4]
    tall = looked_ref.shape[1]

    for part in range(2):
        for half in range(2):
            at = half * pairs
            pair_ref[part, at : at + first_pair_ref.shape[2], :] = first_pair_ref[part, half]
    for tile in range(tiles):
        for unit, (low, high, turns) in enumerate(pair_units(dates)):
            if high == 0:
                continue

            def mine_of(part, odd, place, tile):
                if low == 0:
                    return first_ref[part, odd, place, tile]
                return ring_ref[low - 1, part, odd, place, tile]

            def turn_far(part, odd, place, tile, turn, mine):
                at = pl.ds(2 * turn + odd, GROUP, stride=2)
                return far_ref[high - 1, part, place, tile, at, :]

            def store(part, tile, value):
                count = value.shape[0]
                across = slice(tile * LANES, (tile + 1) * LANES)
                bits = halves(value)
                for half in range(2):
                    at = half * pairs + unit * count
                    pair_ref[part, at : at + count, across] = bits[half]

            turned_of = turn_here if low == high else turn_far
            unit_products(tile, looks, turns, mine_of, turned_of, store)
        across = slice(tile * LANES, (tile + 1) * LANES)
        for part in range(2):
            summed = jnp.dot(
                weights_ref[part], pair_ref[part, :, across], preferred_element_type=F32
            )
            looked_ref[part, :, across] = summed[:tall] + summed[tall:]


def finish_kernel(looked_ref, fold_ref, *refs):
    *message_refs, out_ref, sum_ref, done_ref, semaphores = refs
    parts, times, half_rows, looks = done_ref.shape
    tall = looked_ref.shape[1]
    pack = LANES // looks
    here, last = lax.axis_index("col"), lax.axis_size("col") - 1
    swaps = len(message_refs)
    from_right = from_left = jnp.zeros((tall, LANES), F32)
    for swap, message_ref in enumerate(message_refs):
        message = message_ref[...]
        from_right = jnp.where((here != last) & (here % swaps == swap), message, from_right)
        from_left = jnp.where((here != 0) & ((here - 1) % swaps == swap), message, from_left)
    edges = jnp.concatenate([from_right, from_left], axis=1)
    head = iota(edges.shape, 1) % 8 < 4
    edges = [jnp.where(head, edges, 0.0), jnp.where(head, 0.0, edges)]
    edges = jnp.concatenate(halves(jnp.concatenate(edges, axis=0)), axis=0)
    edges = jnp.dot(edges, fold_ref[...], preferred_element_type=F32)
    edges = edges[: parts * tall] + edges[parts * tall :]
    sent = []
    for part in range(parts):
        value = looked_ref[part] + edges[part * tall : (part + 1) * tall]
        for half_row in range(half_rows):
            tile, near = half_row // pack, half_row % pack
            one = value[:, tile * LANES : (tile + 1) * LANES]
            at = half_row * tall
            sum_ref[part, at : at + tall, :] = pltpu.roll(one, -near * looks % LANES, 1)
        for time in range(times):
            rows = sum_ref[part, pl.ds(time, half_rows, stride=tall), :]
            done_ref[part, time] = rows[:, :looks]
        sent.append(
            pltpu.make_async_copy(done_ref.at[part], out_ref.at[:, part], semaphores.at[part])
        )
        sent[part].start()
    for copy in sent:
        copy.wait()


def column_swap(swap, swaps, owners, count):
    moves = []
    for owner in range(owners):
        for column in range(count):
            partner = column
            if column % swaps == swap and column + 1 < count:
                partner = column + 1
            elif column and (column - 1) % swaps == swap:
                partner = column - 1
            moves.append((owner * count + column, twin_of(owner, owners) * count + partner))
    return moves


def per_device(scenes, pair_dates, pair_count, inverse):
    owners, count = lax.axis_size("date"), lax.axis_size("col")
    dates_here, parts, all_rows, columns = scenes.shape
    half_rows = all_rows // owners // 2
    dates = owners * dates_here
    pairs = pair_rows(dates)
    looks = columns // 8
    tiles = -(-half_rows // (LANES // looks))

    blocks = cut(scenes, pair_dates.T, pair_count, owners)
    for step in range(1, owners):
        moves = [(owner, (owner - step) % owners) for owner in range(owners)]
        blocks[step] = lax.ppermute(blocks[step], "date", moves)

    tall = round_up(inverse.shape[0], 16)
    rows = 2 * half_rows
    sides = columns // LANES
    order = [blocks[(place - 1) % owners] for place in range(owners)]
    order = [held(block) for block in order]
    group_rows = pltpu.VMEM((parts, sides, rows * GROUP, LANES), F32)
    comb, fold, first_group, first_pairs, first_seam = pl.pallas_call(
        functools.partial(early_kernel, dates_here),
        out_shape=[
            pltpu.VMEM((columns, columns), BF16),
            pltpu.VMEM((2 * LANES, tiles * LANES), BF16),
            pltpu.VMEM((parts, 2, 8, tiles, GROUP, LANES), F32),
            pltpu.VMEM((parts, 2, GROUP * GROUP // 2, tiles * LANES), BF16),
            pltpu.VMEM((parts, GROUP, LANES), F32),
        ],
        in_specs=[IN_VMEM] * (GROUP // dates_here),
        out_specs=[IN_VMEM] * 5,
        scratch_shapes=[group_rows],
        compiler_params=pltpu.CompilerParams(vmem_limit_bytes=40 << 20),
    )(*order[: GROUP // dates_here])
    others = dates // GROUP - 1
    steps = [*range(owners - 1, 1, -1), 0]
    group_rows = pltpu.VMEM((others, *group_rows.shape), F32)
    other_rows, other_seams, partial, rest = pl.pallas_call(
        functools.partial(middle_kernel, dates_here, pair_dates.shape[0], steps),
        out_shape=[
            group_rows,
            pltpu.VMEM((others, parts, GROUP, LANES), F32),
            pltpu.VMEM((parts, tall, pairs), F32),
            pltpu.VMEM((tall, LANES), F32),
        ],
        in_specs=[IN_VMEM] * (owners + 1),
        out_specs=[IN_VMEM] * 4,
        scratch_shapes=[pltpu.VMEM((tall, round_up(inverse.shape[1], LANES)), F32)],
        compiler_params=pltpu.CompilerParams(vmem_limit_bytes=40 << 20),
    )(held(comb), held(inverse), *[held(blocks[step]) for step in steps])
    swaps = min(3, count - 1)
    weights, ring, far, *messages = pl.pallas_call(
        functools.partial(edge_kernel, dates_here, owners),
        out_shape=[
            pltpu.VMEM((parts, 2 * tall, 2 * pairs), BF16),
            pltpu.VMEM((others, parts, 2, 8, tiles, GROUP, LANES), F32),
            pltpu.VMEM((others, parts, 8, tiles, 4 * GROUP, LANES), F32),
            *[pltpu.VMEM((tall, LANES), F32)] * swaps,
        ],
        in_specs=[IN_VMEM] * 7,
        out_specs=[IN_VMEM] * (swaps + 3),
        scratch_shapes=[
            pltpu.VMEM((others, parts, GROUP, LANES), F32),
            pltpu.VMEM((parts, 2 * pairs, LANES), BF16),
            group_rows,
        ],
        compiler_params=pltpu.CompilerParams(vmem_limit_bytes=40 << 20),
    )(
        *[held(one) for one in (blocks[1], first_seam, other_seams, partial, rest, comb)],
        held(other_rows),
    )
    looked = pl.pallas_call(
        functools.partial(series_kernel, looks),
        out_shape=pltpu.VMEM((parts, tall, tiles * LANES), F32),
        in_specs=[IN_VMEM] * 5,
        out_specs=IN_VMEM,
        scratch_shapes=[pltpu.VMEM((parts, 2 * pairs, tiles * LANES), BF16)],
        compiler_params=pltpu.CompilerParams(vmem_limit_bytes=40 << 20),
        cost_estimate=pl.CostEstimate(
            flops=2 * parts * pairs * columns * rows * 8, bytes_accessed=1 << 20, transcendentals=0
        ),
    )(*[held(one) for one in (weights, first_group, first_pairs, ring, far)])

    for swap in range(swaps):
        moves = column_swap(swap, swaps, owners, count)
        messages[swap] = held(lax.ppermute(messages[swap], ("date", "col"), moves))
    return pl.pallas_call(
        finish_kernel,
        out_shape=jax.ShapeDtypeStruct(
            (inverse.shape[0], parts, half_rows, columns // 8), F32
        ),
        in_specs=[IN_VMEM] * (swaps + 2),
        out_specs=ANYWHERE,
        scratch_shapes=[
            pltpu.VMEM((parts, half_rows * tall, LANES), F32),
            pltpu.VMEM((parts, inverse.shape[0], half_rows, columns // 8), F32),
            pltpu.SemaphoreType.DMA((parts,)),
        ],
    )(held(looked), held(fold), *messages)


def solution(mesh):
    placed = (P("date", None, "groups", "col"), P("date", None), P("date"), P())
    return jax.shard_map(
        per_device,
        mesh=mesh,
        in_specs=placed,
        out_specs=P(None, None, ("groups", "date"), "col"),
        check_vma=False,
    )
```

```python
import functools

import jax
import jax.numpy as jnp
from jax import lax
from jax.experimental import pallas as pl
from jax.experimental.pallas import tpu as pltpu
from jax.sharding import PartitionSpec as P

F32, BF16 = jnp.float32, jnp.bfloat16
LANES = 128
NOTE = 8
NOTE_ROWS = 2 * NOTE
GROUP = 8
ANYWHERE = pl.BlockSpec(memory_space=pl.ANY)
IN_VMEM = pl.BlockSpec(memory_space=pltpu.VMEM)
IN_SMEM = pl.BlockSpec(memory_space=pltpu.SMEM)


def round_up(value, step):
    return -(-value // step) * step


def held(array):
    return pltpu.with_memory_space_constraint(array, pltpu.VMEM)


def iota(shape, axis):
    return lax.broadcasted_iota(jnp.int32, shape, axis)


def halves(value):
    high = value.astype(BF16)
    return high, (value - high.astype(F32)).astype(BF16)


def blank_kernel(blank_ref):
    blank_ref[...] = jnp.zeros_like(blank_ref)


def comb_of(columns):
    looks = columns // 8
    column, lane = iota((columns, columns), 0), iota((columns, columns), 1)
    here = (column // 8 == lane % looks) & (column % 8 == lane // looks)
    return jnp.where(here, 1.0, 0.0).astype(BF16)


def live_kernel(rows, slots, count_ref, blank_ref, live_ref, pick_ref, own_ref, gather_ref):
    columns, (all_rows, lanes), (lines, height) = pick_ref.shape[0], own_ref.shape, gather_ref.shape
    column, lane = iota((columns, lanes), 0), iota((columns, lanes), 1) % 8
    wanted = jnp.where(lane < 4, lane, columns - 8 + lane)
    pick_ref[...] = jnp.where(column == wanted, 1.0, 0.0).astype(BF16)
    row, lane = iota((all_rows, lanes), 0), iota((all_rows, lanes), 1)
    own_ref[...] = jnp.where(row % rows == lane // 8, 1.0, 0.0)
    owners, images = all_rows // rows, height // all_rows
    line, row = iota((lines, height), 0), iota((lines, height), 1) // rows
    place = line % NOTE
    wanted = (place % (images // 2) * 2 + place // (images // 2)) * owners + line // NOTE
    gather_ref[...] = jnp.where((place < images) & (row == wanted), 1.0, 0.0).astype(BF16)
    row, lane = iota(live_ref.shape, 0), iota(live_ref.shape, 1)
    live = (row == 2) & (lane < jnp.minimum(count_ref[0], slots))
    live_ref[...] = jnp.where(live, 1.0, blank_ref[...])


def seam_kernel(scenes_ref, dates_ref, live_ref, pick_ref, own_ref, gather_ref, *refs):
    *block_refs, seams_ref, note_ref, fetched_ref, semaphore = refs
    fetch = pltpu.make_async_copy(dates_ref, fetched_ref, semaphore)
    fetch.start()
    dates_here, parts, all_rows, columns = scenes_ref.shape
    height = dates_here * parts * all_rows
    cells = scenes_ref[...].reshape(height, columns)
    cells = jnp.dot(cells, pick_ref[...], preferred_element_type=F32)
    cells = cells.reshape(dates_here * parts, all_rows, LANES) * own_ref[...][None]
    cells = cells.reshape(height, LANES).astype(BF16)
    lines = jnp.dot(gather_ref[...], cells, preferred_element_type=F32)
    for owner in range(seams_ref.shape[0]):
        seams_ref[owner] = lines[owner * NOTE : (owner + 1) * NOTE]
    note_ref[...] = live_ref[...]
    owners = seams_ref.shape[0]
    for step, block_ref in enumerate(block_refs):
        cut_block(scenes_ref, owners, step, block_ref)
    fetch.wait()
    note_ref[:2, : dates_ref.shape[1]] = fetched_ref[...].astype(F32)
    for step, block_ref in enumerate(block_refs):
        owner = lax.rem(lax.axis_index("date") + owners - step, owners)
        tile = jnp.concatenate([note_ref[...], seams_ref[twin_of(owner, owners)]], axis=0)
        block_ref[block_ref.shape[0] - NOTE_ROWS :] = tile.astype(BF16)


def twin_of(owner, owners):
    return owner + 1 - 2 * (owner % 2) if owners % 2 == 0 else owner


def cut_block(scenes_ref, owners, step, block_ref):
    dates_here, parts, all_rows, columns = scenes_ref.shape
    rows = all_rows // owners
    first = pl.multiple_of(lax.rem(lax.axis_index("date") + owners - step, owners) * rows, rows)
    height = dates_here * parts * rows
    for side in range(columns // LANES):
        cells = scenes_ref[:, :, pl.ds(first, rows), side * LANES : (side + 1) * LANES]
        block_ref[side * height : (side + 1) * height] = cells.reshape(height, LANES)


def cells_of(block_ref, sides):
    height = (block_ref.shape[0] - NOTE_ROWS) // sides
    return jnp.concatenate(
        [block_ref[side * height : (side + 1) * height] for side in range(sides)], axis=1
    )


def cut(scenes, pair_dates, pair_count, owners):
    dates_here, parts, all_rows, columns = scenes.shape
    rows = all_rows // owners
    sides = columns // LANES
    height = dates_here * parts * rows
    blank = pl.pallas_call(
        blank_kernel,
        out_shape=pltpu.VMEM((NOTE, LANES), F32),
        out_specs=IN_VMEM,
        cost_estimate=pl.CostEstimate(flops=10**9, bytes_accessed=10**7, transcendentals=0),
    )()
    live, *constants = pl.pallas_call(
        functools.partial(live_kernel, rows, pair_dates.shape[1]),
        out_shape=[
            pltpu.VMEM((NOTE, LANES), F32),
            pltpu.VMEM((columns, LANES), BF16),
            pltpu.VMEM((all_rows, LANES), F32),
            pltpu.VMEM((owners * NOTE, dates_here * parts * all_rows), BF16),
        ],
        in_specs=[IN_SMEM, IN_VMEM],
        out_specs=[IN_VMEM] * 4,
    )(pair_count, held(blank))
    aligned = rows % 16 == 0
    lines = [pltpu.VMEM((owners, NOTE, LANES), F32), pltpu.VMEM((NOTE, LANES), F32)]
    blocks = pl.pallas_call(
        seam_kernel,
        out_shape=[pltpu.VMEM((sides * height + NOTE_ROWS, LANES), BF16)] * owners
        if aligned
        else lines,
        in_specs=[IN_VMEM, ANYWHERE] + [IN_VMEM] * 4,
        out_specs=[IN_VMEM] * (owners if aligned else 2),
        scratch_shapes=[
            *(lines if aligned else []),
            pltpu.VMEM(pair_dates.shape, jnp.int32),
            pltpu.SemaphoreType.DMA,
        ],
    )(held(scenes), pair_dates, held(live), *[held(array) for array in constants])
    if aligned:
        return list(blocks)
    seams, note = blocks
    blocks = []
    me = lax.axis_index("date")
    apart = scenes.reshape(dates_here * parts, owners, rows, columns)
    for step in range(owners):
        owner = lax.rem(me + owners - step, owners)
        cells = lax.dynamic_index_in_dim(apart, owner, 1, False).reshape(height, columns)
        strips = [cells[:, side * LANES : (side + 1) * LANES] for side in range(sides)]
        seam = lax.dynamic_index_in_dim(seams, twin_of(owner, owners), 0, False)
        strips += [note.astype(BF16), seam.astype(BF16)]
        blocks.append(jnp.concatenate(strips, axis=0))
    return blocks


def pair_places(first, second, dates):
    groups = dates // GROUP

    def group_of(date):
        return jnp.floor(date * (1.0 / GROUP))

    first_group, second_group = group_of(first), group_of(second)
    first_seat, second_seat = first - GROUP * first_group, second - GROUP * second_group
    ahead = second_seat - first_seat
    ahead = jnp.where(ahead < 0.0, ahead + GROUP, ahead)
    behind = jnp.where(ahead > 0.0, GROUP - ahead, 0.0)
    near = ahead <= GROUP // 2
    inside = first_group * (GROUP * GROUP // 2)
    inside = inside + jnp.where(
        near, (ahead - 1.0) * GROUP + first_seat, (behind - 1.0) * GROUP + second_seat
    )
    upward = first_group < second_group
    low, high = jnp.minimum(first_group, second_group), jnp.maximum(first_group, second_group)
    between = low * (2 * groups - 1.0 - low) * 0.5 + high - low - 1.0
    across = groups * (GROUP * GROUP // 2) + between * (GROUP * GROUP)
    across = across + jnp.where(
        upward, ahead * GROUP + first_seat, behind * GROUP + second_seat
    )
    same = first_group == second_group
    sign = jnp.where(same, jnp.where(near, 1.0, -1.0), jnp.where(upward, 1.0, -1.0))
    return jnp.where(same, inside, across), sign


def inverse_of(wide, step, owners, slots):
    lanes = wide.shape[1]
    owner = lax.rem(lax.axis_index("date") + step, owners)
    moved = pltpu.roll(wide, lax.rem(lanes - owner * slots, lanes), 1)
    return moved[:, :LANES] * (1.0 / 128.0)


def slot_weights(block_ref, inverse, owners, dates_here):
    dates = owners * dates_here
    start = lax.rem(lax.axis_index("date") + owners - 1, owners) * dates_here
    start = jnp.full((1, LANES), start, jnp.int32).astype(F32)
    height = block_ref.shape[0]
    note = block_ref[height - NOTE_ROWS : height].astype(F32)

    def wrapped(value):
        return jnp.where(value < 0.0, value + dates, value)

    place, sign = pair_places(wrapped(note[0:1] - start), wrapped(note[1:2] - start), dates)
    place = jnp.where(note[2:3] > 0.5, place, -1.0)
    pairs = pair_rows(dates)
    chosen = jnp.where(iota((pairs, LANES), 0).astype(F32) == place, 1.0, 0.0).astype(BF16)
    stacked = jnp.concatenate([*halves(inverse), *halves(inverse * sign)], axis=0)
    spread = lax.dot_general(
        stacked, chosen, (((1,), (1,)), ((), ())), preferred_element_type=F32
    )
    tall = inverse.shape[0]
    parts = [spread[at * tall : (at + 1) * tall] for at in range(4)]
    return parts[0] + parts[1], parts[2] + parts[3]


def pair_rows(dates):
    groups = dates // GROUP
    return GROUP * GROUP // 2 * groups + GROUP * GROUP * (groups * (groups - 1) // 2)


def pair_units(dates):
    groups = dates // GROUP
    half = GROUP // 2
    units = [(group, group, range(1, half + 1)) for group in range(groups)]
    for low in range(groups):
        for high in range(low + 1, groups):
            units += [(low, high, range(at, at + half)) for at in range(0, GROUP, half)]
    return units


def spread_block(block_ref, comb, dates_here, seat, rows_ref):
    sides = rows_ref.shape[1]
    combed = jnp.dot(cells_of(block_ref, sides), comb, preferred_element_type=F32)
    rows = combed.shape[0] // (2 * dates_here)
    for own in range(dates_here):
        for part in range(2):
            at = (own * 2 + part) * rows
            for side in range(sides):
                rows_ref[part, side, pl.ds(seat + own, rows, stride=GROUP), :] = combed[
                    at : at + rows, side * LANES : (side + 1) * LANES
                ]


def pack_group(rows_ref, looks, half_rows, store):
    pack = LANES // looks
    lane = iota((GROUP, LANES), 1)
    for part in range(2):
        for odd in range(2):
            for tile in range(-(-half_rows // pack)):
                for side in range(rows_ref.shape[1]):
                    cells = []
                    for near in range(pack):
                        half_row = tile * pack + near
                        at = (2 * half_row + odd) * GROUP
                        if half_row < half_rows:
                            cells.append(rows_ref[part, side, at : at + GROUP, :])
                        else:
                            cells.append(jnp.zeros((GROUP, LANES), F32))
                    bit = pack // 2
                    while bit:
                        clear = (lane // looks) & bit == 0
                        for near in range(pack):
                            if not near & bit:
                                one, two = cells[near], cells[near + bit]
                                cells[near] = jnp.where(
                                    clear, one, pltpu.roll(two, bit * looks, 1)
                                )
                                cells[near + bit] = jnp.where(
                                    clear, pltpu.roll(one, LANES - bit * looks, 1), two
                                )
                        bit //= 2
                    for near in range(pack):
                        store(part, odd, side * pack + near, tile, cells[near])


def unit_products(tile, looks, turns, mine_of, turned_of, store):
    lane = iota((GROUP, LANES), 1) % looks
    at_first, at_last = lane == 0, lane == looks - 1

    def product(place):
        mine = [[mine_of(part, odd, place, tile) for odd in range(2)] for part in range(2)]
        values = []
        for turn in turns:
            other = [
                [turned_of(part, odd, place, tile, turn, mine) for odd in range(2)]
                for part in range(2)
            ]
            real = (mine[0][0] * other[0][0] + mine[1][0] * other[1][0]) + (
                mine[0][1] * other[0][1] + mine[1][1] * other[1][1]
            )
            imaginary = (mine[1][0] * other[0][0] - mine[0][0] * other[1][0]) + (
                mine[1][1] * other[0][1] - mine[0][1] * other[1][1]
            )
            values += [real, imaginary]
        return values

    def running(places):
        total = product(places[0])
        ramp = total
        for place in places[1:]:
            total = [one + two for one, two in zip(total, product(place))]
            share = [0.5 * one for one in total] if place is places[-1] else total
            ramp = [one + two for one, two in zip(ramp, share)]
        return total, ramp

    early, to_left = running((0, 1, 2, 3))
    late, to_right = running((7, 6, 5, 4))
    values = []
    for index in range(len(early)):
        before = pltpu.roll(to_right[index], 1, 1)
        after = pltpu.roll(to_left[index], LANES - 1, 1)
        value = 8.0 * (early[index] + late[index]) - to_left[index] - to_right[index]
        value = value + jnp.where(at_first, 0.0, before) + jnp.where(at_last, 0.0, after)
        values.append(value)
    for part in range(2):
        store(part, tile, jnp.concatenate(values[part::2], axis=0))


def turn_here(part, odd, place, tile, turn, mine):
    return pltpu.roll(mine[part][odd], GROUP - turn, 0)


def seam_of(block_ref, dates_here, seat, seam_ref):
    height = block_ref.shape[0]
    lines = block_ref[height - NOTE_ROWS : height].astype(F32)
    for part in range(2):
        at = NOTE + part * dates_here
        seam_ref[part, seat : seat + dates_here, :] = lines[at : at + dates_here]


def early_kernel(dates_here, *refs):
    *block_refs, comb_ref, ring_ref, pair_ref, seam_ref, rows_ref = refs
    columns = comb_ref.shape[0]
    looks = columns // 8
    tiles = ring_ref.shape[3]
    half_rows = rows_ref.shape[2] // GROUP // 2
    comb = comb_of(columns)
    comb_ref[...] = comb
    for index, block_ref in enumerate(block_refs):
        spread_block(block_ref, comb, dates_here, index * dates_here, rows_ref)
        seam_of(block_ref, dates_here, index * dates_here, seam_ref)

    def keep(part, odd, place, tile, cells):
        ring_ref[part, odd, place, tile] = cells

    pack_group(rows_ref, looks, half_rows, keep)

    def store(part, tile, value):
        across = slice(tile * LANES, (tile + 1) * LANES)
        high, low = halves(value)
        pair_ref[part, 0, :, across] = high
        pair_ref[part, 1, :, across] = low

    for tile in range(tiles):
        unit_products(
            tile,
            looks,
            range(1, GROUP // 2 + 1),
            lambda part, odd, place, tile: ring_ref[part, odd, place, tile],
            turn_here,
            store,
        )


def place_of(step, owners, dates_here):
    date = (step + 1) % owners * dates_here
    return date // GROUP, date % GROUP


def middle_kernel(dates_here, slots, steps, *refs):
    *refs, rows_ref, seams_ref, partial_ref, rest_ref, wide_ref = refs
    comb_ref, inverse_ref, *block_refs = refs
    owners = len(block_refs) + 1
    comb = comb_ref[...]
    wide_ref[...] = jnp.zeros_like(wide_ref)
    wide_ref[: inverse_ref.shape[0], : inverse_ref.shape[1]] = inverse_ref[...]
    wide = wide_ref[...]
    sums = [0.0, 0.0]
    for step, block_ref in zip(steps, block_refs):
        group, seat = place_of(step, owners, dates_here)
        if group:
            spread_block(block_ref, comb, dates_here, seat, rows_ref.at[group - 1])
            seam_of(block_ref, dates_here, seat, seams_ref.at[group - 1])
        more = slot_weights(block_ref, inverse_of(wide, step, owners, slots), owners, dates_here)
        sums = [one + two for one, two in zip(sums, more)]
    for part in range(2):
        partial_ref[part] = sums[part]
    rest_ref[...] = inverse_of(wide, 1, owners, slots)


def edge_kernel(dates_here, owners, *refs):
    block_ref, seam_ref, others_ref, partial_ref, rest_ref, comb_ref, other_rows_ref, *refs = refs
    weights_ref, ring_ref, far_ref, *message_refs, seams_ref, pair_ref, rows_ref = refs
    dates = owners * dates_here
    pairs = pair_rows(dates)
    tall = rest_ref.shape[0]

    group, seat = place_of(1, owners, dates_here)
    rows_ref[...] = other_rows_ref[...]
    spread_block(block_ref, comb_ref[...], dates_here, seat, rows_ref.at[group - 1])
    seams_ref[...] = others_ref[...]
    seam_of(block_ref, dates_here, seat, seams_ref.at[group - 1])
    weights = []
    for part, more in enumerate(slot_weights(block_ref, rest_ref[...], owners, dates_here)):
        high, low = halves(partial_ref[part] + more)
        wide = [jnp.concatenate([half, half], axis=1) for half in (high, low)]
        weights.append(jnp.concatenate(wide, axis=0))
        weights_ref[part] = weights[part]

    lane = iota((GROUP, LANES), 1) % 8
    ramp = jnp.where(lane < 4, 3.5 - lane.astype(F32), lane.astype(F32) - 3.5)
    for unit, (low, high, turns) in enumerate(pair_units(dates)):
        mine = [(seams_ref[low - 1, part] if low else seam_ref[part]) * ramp for part in range(2)]
        theirs = [seams_ref[high - 1, part] if high else seam_ref[part] for part in range(2)]
        values = []
        for turn in turns:
            other = [pltpu.roll(cells, GROUP - turn, 0) if turn else cells for cells in theirs]
            values.append(mine[0] * other[0] + mine[1] * other[1])
            values.append(mine[1] * other[0] - mine[0] * other[1])
        for part in range(2):
            value = jnp.concatenate(values[part::2], axis=0)
            for shift in (1, 2, 8):
                value = value + pltpu.roll(value, LANES - shift, 1)
            if part:
                value = pltpu.roll(value, 1, 1)
            count = value.shape[0]
            bits = halves(value)
            for half in range(2):
                at = half * pairs + unit * count
                pair_ref[part, at : at + count, :] = bits[half]
    sums = []
    for part in range(2):
        summed = jnp.dot(weights[part], pair_ref[part], preferred_element_type=F32)
        sums.append(summed[:tall] + summed[tall:])
    message = jnp.where(iota((tall, LANES), 1) % 4 == 1, sums[1], sums[0])
    for message_ref in message_refs:
        message_ref[...] = message
    looks = comb_ref.shape[0] // 8
    half_rows = rows_ref.shape[3] // GROUP // 2
    for group in range(1, dates // GROUP):

        def keep(part, odd, place, tile, cells):
            ring_ref[group - 1, part, odd, place, tile] = cells
            for copy in range(2):
                at = pl.ds(2 * copy * GROUP + odd, GROUP, stride=2)
                far_ref[group - 1, part, place, tile, at, :] = cells

        pack_group(rows_ref.at[group - 1], looks, half_rows, keep)


def series_kernel(looks, *refs):
    weights_ref, first_ref, first_pair_ref, ring_ref, far_ref, looked_ref, pair_ref = refs
    groups = 1 + ring_ref.shape[0]
    dates = groups * GROUP
    pairs = pair_rows(dates)
    tiles = ring_ref.shape[4]
    tall = looked_ref.shape[1]

    for part in range(2):
        for half in range(2):
            at = half * pairs
            pair_ref[part, at : at + first_pair_ref.shape[2], :] = first_pair_ref[part, half]
    for tile in range(tiles):
        for unit, (low, high, turns) in enumerate(pair_units(dates)):
            if high == 0:
                continue

            def mine_of(part, odd, place, tile):
                if low == 0:
                    return first_ref[part, odd, place, tile]
                return ring_ref[low - 1, part, odd, place, tile]

            def turn_far(part, odd, place, tile, turn, mine):
                at = pl.ds(2 * turn + odd, GROUP, stride=2)
                return far_ref[high - 1, part, place, tile, at, :]

            def store(part, tile, value):
                count = value.shape[0]
                across = slice(tile * LANES, (tile + 1) * LANES)
                bits = halves(value)
                for half in range(2):
                    at = half * pairs + unit * count
                    pair_ref[part, at : at + count, across] = bits[half]

            turned_of = turn_here if low == high else turn_far
            unit_products(tile, looks, turns, mine_of, turned_of, store)
        across = slice(tile * LANES, (tile + 1) * LANES)
        for part in range(2):
            summed = jnp.dot(
                weights_ref[part], pair_ref[part, :, across], preferred_element_type=F32
            )
            looked_ref[part, :, across] = summed[:tall] + summed[tall:]


def finish_kernel(looked_ref, *refs):
    *message_refs, out_ref, sum_ref, done_ref, semaphores = refs
    parts, times, half_rows, looks = done_ref.shape
    tall = looked_ref.shape[1]
    pack = LANES // looks
    here, last = lax.axis_index("col"), lax.axis_size("col") - 1
    swaps = len(message_refs)
    from_right = from_left = jnp.zeros((tall, LANES), F32)
    for swap, message_ref in enumerate(message_refs):
        message = message_ref[...]
        from_right = jnp.where((here != last) & (here % swaps == swap), message, from_right)
        from_left = jnp.where((here != 0) & ((here - 1) % swaps == swap), message, from_left)
    lane = iota((tall, LANES), 1)
    sent = []
    for part in range(parts):
        for half_row in range(half_rows):
            tile, near = half_row // pack, half_row % pack
            value = looked_ref[part, :, tile * LANES : (tile + 1) * LANES]
            value = pltpu.roll(value, -near * looks % LANES, 1)
            at = 16 * half_row + part
            right = pltpu.roll(from_right, (looks - 1 - at) % LANES, 1)
            left = pltpu.roll(from_left, (-4 - at) % LANES, 1)
            value = jnp.where(lane == looks - 1, value + right, value)
            value = jnp.where(lane == 0, value + left, value)
            sum_ref[part, half_row * tall : (half_row + 1) * tall, :] = value
        for time in range(times):
            rows = sum_ref[part, pl.ds(time, half_rows, stride=tall), :]
            done_ref[part, time] = rows[:, :looks]
        sent.append(
            pltpu.make_async_copy(done_ref.at[part], out_ref.at[:, part], semaphores.at[part])
        )
        sent[part].start()
    for copy in sent:
        copy.wait()


def column_swap(swap, swaps, owners, count):
    moves = []
    for owner in range(owners):
        for column in range(count):
            partner = column
            if column % swaps == swap and column + 1 < count:
                partner = column + 1
            elif column and (column - 1) % swaps == swap:
                partner = column - 1
            moves.append((owner * count + column, twin_of(owner, owners) * count + partner))
    return moves


def per_device(scenes, pair_dates, pair_count, inverse):
    owners, count = lax.axis_size("date"), lax.axis_size("col")
    dates_here, parts, all_rows, columns = scenes.shape
    half_rows = all_rows // owners // 2
    dates = owners * dates_here
    pairs = pair_rows(dates)
    looks = columns // 8
    tiles = -(-half_rows // (LANES // looks))

    blocks = cut(scenes, pair_dates.T, pair_count, owners)
    for step in range(1, owners):
        moves = [(owner, (owner - step) % owners) for owner in range(owners)]
        blocks[step] = lax.ppermute(blocks[step], "date", moves)

    tall = round_up(inverse.shape[0], 16)
    rows = 2 * half_rows
    sides = columns // LANES
    order = [blocks[(place - 1) % owners] for place in range(owners)]
    order = [held(block) for block in order]
    group_rows = pltpu.VMEM((parts, sides, rows * GROUP, LANES), F32)
    comb, first_group, first_pairs, first_seam = pl.pallas_call(
        functools.partial(early_kernel, dates_here),
        out_shape=[
            pltpu.VMEM((columns, columns), BF16),
            pltpu.VMEM((parts, 2, 8, tiles, GROUP, LANES), F32),
            pltpu.VMEM((parts, 2, GROUP * GROUP // 2, tiles * LANES), BF16),
            pltpu.VMEM((parts, GROUP, LANES), F32),
        ],
        in_specs=[IN_VMEM] * (GROUP // dates_here),
        out_specs=[IN_VMEM] * 4,
        scratch_shapes=[group_rows],
        compiler_params=pltpu.CompilerParams(vmem_limit_bytes=40 << 20),
    )(*order[: GROUP // dates_here])
    others = dates // GROUP - 1
    steps = [*range(owners - 1, 1, -1), 0]
    group_rows = pltpu.VMEM((others, *group_rows.shape), F32)
    other_rows, other_seams, partial, rest = pl.pallas_call(
        functools.partial(middle_kernel, dates_here, pair_dates.shape[0], steps),
        out_shape=[
            group_rows,
            pltpu.VMEM((others, parts, GROUP, LANES), F32),
            pltpu.VMEM((parts, tall, pairs), F32),
            pltpu.VMEM((tall, LANES), F32),
        ],
        in_specs=[IN_VMEM] * (owners + 1),
        out_specs=[IN_VMEM] * 4,
        scratch_shapes=[pltpu.VMEM((tall, round_up(inverse.shape[1], LANES)), F32)],
        compiler_params=pltpu.CompilerParams(vmem_limit_bytes=40 << 20),
    )(held(comb), held(inverse), *[held(blocks[step]) for step in steps])
    swaps = min(3, count - 1)
    weights, ring, far, *messages = pl.pallas_call(
        functools.partial(edge_kernel, dates_here, owners),
        out_shape=[
            pltpu.VMEM((parts, 2 * tall, 2 * pairs), BF16),
            pltpu.VMEM((others, parts, 2, 8, tiles, GROUP, LANES), F32),
            pltpu.VMEM((others, parts, 8, tiles, 4 * GROUP, LANES), F32),
            *[pltpu.VMEM((tall, LANES), F32)] * swaps,
        ],
        in_specs=[IN_VMEM] * 7,
        out_specs=[IN_VMEM] * (swaps + 3),
        scratch_shapes=[
            pltpu.VMEM((others, parts, GROUP, LANES), F32),
            pltpu.VMEM((parts, 2 * pairs, LANES), BF16),
            group_rows,
        ],
        compiler_params=pltpu.CompilerParams(vmem_limit_bytes=40 << 20),
    )(
        *[held(one) for one in (blocks[1], first_seam, other_seams, partial, rest, comb)],
        held(other_rows),
    )
    looked = pl.pallas_call(
        functools.partial(series_kernel, looks),
        out_shape=pltpu.VMEM((parts, tall, tiles * LANES), F32),
        in_specs=[IN_VMEM] * 5,
        out_specs=IN_VMEM,
        scratch_shapes=[pltpu.VMEM((parts, 2 * pairs, tiles * LANES), BF16)],
        compiler_params=pltpu.CompilerParams(vmem_limit_bytes=40 << 20),
        cost_estimate=pl.CostEstimate(
            flops=2 * parts * pairs * columns * rows * 8, bytes_accessed=1 << 20, transcendentals=0
        ),
    )(*[held(one) for one in (weights, first_group, first_pairs, ring, far)])

    for swap in range(swaps):
        moves = column_swap(swap, swaps, owners, count)
        messages[swap] = held(lax.ppermute(messages[swap], ("date", "col"), moves))
    return pl.pallas_call(
        finish_kernel,
        out_shape=jax.ShapeDtypeStruct(
            (inverse.shape[0], parts, half_rows, columns // 8), F32
        ),
        in_specs=[IN_VMEM] * (swaps + 1),
        out_specs=ANYWHERE,
        scratch_shapes=[
            pltpu.VMEM((parts, half_rows * tall, LANES), F32),
            pltpu.VMEM((parts, inverse.shape[0], half_rows, columns // 8), F32),
            pltpu.SemaphoreType.DMA((parts,)),
        ],
    )(held(looked), *messages)


def solution(mesh):
    placed = (P("date", None, "groups", "col"), P("date", None), P("date"), P())
    return jax.shard_map(
        per_device,
        mesh=mesh,
        in_specs=placed,
        out_specs=P(None, None, ("groups", "date"), "col"),
        check_vma=False,
    )
```

```python
import functools

import jax
import jax.numpy as jnp
from jax import lax
from jax.experimental import pallas as pl
from jax.experimental.pallas import tpu as pltpu
from jax.sharding import PartitionSpec as P

F32, BF16 = jnp.float32, jnp.bfloat16
LANES = 128
NOTE = 8
NOTE_ROWS = 2 * NOTE
GROUP = 8
ANYWHERE = pl.BlockSpec(memory_space=pl.ANY)
IN_VMEM = pl.BlockSpec(memory_space=pltpu.VMEM)
IN_SMEM = pl.BlockSpec(memory_space=pltpu.SMEM)


def round_up(value, step):
    return -(-value // step) * step


def held(array):
    return pltpu.with_memory_space_constraint(array, pltpu.VMEM)


def iota(shape, axis):
    return lax.broadcasted_iota(jnp.int32, shape, axis)


def halves(value):
    high = value.astype(BF16)
    return high, (value - high.astype(F32)).astype(BF16)


def blank_kernel(blank_ref):
    blank_ref[...] = jnp.zeros_like(blank_ref)


def comb_of(columns):
    looks = columns // 8
    column, lane = iota((columns, columns), 0), iota((columns, columns), 1)
    here = (column // 8 == lane % looks) & (column % 8 == lane // looks)
    return jnp.where(here, 1.0, 0.0).astype(BF16)


def live_kernel(rows, slots, count_ref, blank_ref, live_ref, pick_ref, own_ref, gather_ref):
    columns, (all_rows, lanes), (lines, height) = pick_ref.shape[0], own_ref.shape, gather_ref.shape
    column, lane = iota((columns, lanes), 0), iota((columns, lanes), 1) % 8
    wanted = jnp.where(lane < 4, lane, columns - 8 + lane)
    pick_ref[...] = jnp.where(column == wanted, 1.0, 0.0).astype(BF16)
    row, lane = iota((all_rows, lanes), 0), iota((all_rows, lanes), 1)
    own_ref[...] = jnp.where(row % rows == lane // 8, 1.0, 0.0)
    owners, images = all_rows // rows, height // all_rows
    line, row = iota((lines, height), 0), iota((lines, height), 1) // rows
    place = line % NOTE
    wanted = (place % (images // 2) * 2 + place // (images // 2)) * owners + line // NOTE
    gather_ref[...] = jnp.where((place < images) & (row == wanted), 1.0, 0.0).astype(BF16)
    row, lane = iota(live_ref.shape, 0), iota(live_ref.shape, 1)
    live = (row == 2) & (lane < jnp.minimum(count_ref[0], slots))
    live_ref[...] = jnp.where(live, 1.0, blank_ref[...])


def seam_kernel(scenes_ref, dates_ref, live_ref, pick_ref, own_ref, gather_ref, *refs):
    *block_refs, seams_ref, note_ref, fetched_ref, semaphore = refs
    fetch = pltpu.make_async_copy(dates_ref, fetched_ref, semaphore)
    fetch.start()
    dates_here, parts, all_rows, columns = scenes_ref.shape
    height = dates_here * parts * all_rows
    cells = scenes_ref[...].reshape(height, columns)
    cells = jnp.dot(cells, pick_ref[...], preferred_element_type=F32)
    cells = cells.reshape(dates_here * parts, all_rows, LANES) * own_ref[...][None]
    cells = cells.reshape(height, LANES).astype(BF16)
    lines = jnp.dot(gather_ref[...], cells, preferred_element_type=F32)
    for owner in range(seams_ref.shape[0]):
        seams_ref[owner] = lines[owner * NOTE : (owner + 1) * NOTE]
    note_ref[...] = live_ref[...]
    owners = seams_ref.shape[0]
    for step, block_ref in enumerate(block_refs):
        cut_block(scenes_ref, owners, step, block_ref)
    fetch.wait()
    note_ref[:2, : dates_ref.shape[1]] = fetched_ref[...].astype(F32)
    for step, block_ref in enumerate(block_refs):
        owner = lax.rem(lax.axis_index("date") + owners - step, owners)
        tile = jnp.concatenate([note_ref[...], seams_ref[twin_of(owner, owners)]], axis=0)
        block_ref[block_ref.shape[0] - NOTE_ROWS :] = tile.astype(BF16)


def twin_of(owner, owners):
    return owner + 1 - 2 * (owner % 2) if owners % 2 == 0 else owner


def cut_block(scenes_ref, owners, step, block_ref):
    dates_here, parts, all_rows, columns = scenes_ref.shape
    rows = all_rows // owners
    first = pl.multiple_of(lax.rem(lax.axis_index("date") + owners - step, owners) * rows, rows)
    height = dates_here * parts * rows
    for side in range(columns // LANES):
        cells = scenes_ref[:, :, pl.ds(first, rows), side * LANES : (side + 1) * LANES]
        block_ref[side * height : (side + 1) * height] = cells.reshape(height, LANES)


def cells_of(block_ref, sides):
    height = (block_ref.shape[0] - NOTE_ROWS) // sides
    return jnp.concatenate(
        [block_ref[side * height : (side + 1) * height] for side in range(sides)], axis=1
    )


def cut(scenes, pair_dates, pair_count, owners):
    dates_here, parts, all_rows, columns = scenes.shape
    rows = all_rows // owners
    sides = columns // LANES
    height = dates_here * parts * rows
    blank = pl.pallas_call(
        blank_kernel,
        out_shape=pltpu.VMEM((NOTE, LANES), F32),
        out_specs=IN_VMEM,
        cost_estimate=pl.CostEstimate(flops=10**9, bytes_accessed=10**7, transcendentals=0),
    )()
    live, *constants = pl.pallas_call(
        functools.partial(live_kernel, rows, pair_dates.shape[1]),
        out_shape=[
            pltpu.VMEM((NOTE, LANES), F32),
            pltpu.VMEM((columns, LANES), BF16),
            pltpu.VMEM((all_rows, LANES), F32),
            pltpu.VMEM((owners * NOTE, dates_here * parts * all_rows), BF16),
        ],
        in_specs=[IN_SMEM, IN_VMEM],
        out_specs=[IN_VMEM] * 4,
    )(pair_count, held(blank))
    aligned = rows % 16 == 0
    lines = [pltpu.VMEM((owners, NOTE, LANES), F32), pltpu.VMEM((NOTE, LANES), F32)]
    blocks = pl.pallas_call(
        seam_kernel,
        out_shape=[pltpu.VMEM((sides * height + NOTE_ROWS, LANES), BF16)] * owners
        if aligned
        else lines,
        in_specs=[IN_VMEM, ANYWHERE] + [IN_VMEM] * 4,
        out_specs=[IN_VMEM] * (owners if aligned else 2),
        scratch_shapes=[
            *(lines if aligned else []),
            pltpu.VMEM(pair_dates.shape, jnp.int32),
            pltpu.SemaphoreType.DMA,
        ],
    )(held(scenes), pair_dates, held(live), *[held(array) for array in constants])
    if aligned:
        return list(blocks)
    seams, note = blocks
    blocks = []
    me = lax.axis_index("date")
    apart = scenes.reshape(dates_here * parts, owners, rows, columns)
    for step in range(owners):
        owner = lax.rem(me + owners - step, owners)
        cells = lax.dynamic_index_in_dim(apart, owner, 1, False).reshape(height, columns)
        strips = [cells[:, side * LANES : (side + 1) * LANES] for side in range(sides)]
        seam = lax.dynamic_index_in_dim(seams, twin_of(owner, owners), 0, False)
        strips += [note.astype(BF16), seam.astype(BF16)]
        blocks.append(jnp.concatenate(strips, axis=0))
    return blocks


def pair_places(first, second, dates):
    groups = dates // GROUP

    def group_of(date):
        return jnp.floor(date * (1.0 / GROUP))

    first_group, second_group = group_of(first), group_of(second)
    first_seat, second_seat = first - GROUP * first_group, second - GROUP * second_group
    ahead = second_seat - first_seat
    ahead = jnp.where(ahead < 0.0, ahead + GROUP, ahead)
    behind = jnp.where(ahead > 0.0, GROUP - ahead, 0.0)
    near = ahead <= GROUP // 2
    inside = first_group * (GROUP * GROUP // 2)
    inside = inside + jnp.where(
        near, (ahead - 1.0) * GROUP + first_seat, (behind - 1.0) * GROUP + second_seat
    )
    upward = first_group < second_group
    low, high = jnp.minimum(first_group, second_group), jnp.maximum(first_group, second_group)
    between = low * (2 * groups - 1.0 - low) * 0.5 + high - low - 1.0
    across = groups * (GROUP * GROUP // 2) + between * (GROUP * GROUP)
    across = across + jnp.where(
        upward, ahead * GROUP + first_seat, behind * GROUP + second_seat
    )
    same = first_group == second_group
    sign = jnp.where(same, jnp.where(near, 1.0, -1.0), jnp.where(upward, 1.0, -1.0))
    return jnp.where(same, inside, across), sign


def inverse_of(wide, step, owners, slots):
    lanes = wide.shape[1]
    owner = lax.rem(lax.axis_index("date") + step, owners)
    moved = pltpu.roll(wide, lax.rem(lanes - owner * slots, lanes), 1)
    return moved[:, :LANES] * (1.0 / 128.0)


def slot_weights(block_ref, inverse, owners, dates_here):
    dates = owners * dates_here
    start = lax.rem(lax.axis_index("date") + owners - 1, owners) * dates_here
    start = jnp.full((1, LANES), start, jnp.int32).astype(F32)
    height = block_ref.shape[0]
    note = block_ref[height - NOTE_ROWS : height].astype(F32)

    def wrapped(value):
        return jnp.where(value < 0.0, value + dates, value)

    place, sign = pair_places(wrapped(note[0:1] - start), wrapped(note[1:2] - start), dates)
    place = jnp.where(note[2:3] > 0.5, place, -1.0)
    pairs = pair_rows(dates)
    chosen = jnp.where(iota((pairs, LANES), 0).astype(F32) == place, 1.0, 0.0).astype(BF16)
    stacked = jnp.concatenate([*halves(inverse), *halves(inverse * sign)], axis=0)
    spread = lax.dot_general(
        stacked, chosen, (((1,), (1,)), ((), ())), preferred_element_type=F32
    )
    tall = inverse.shape[0]
    parts = [spread[at * tall : (at + 1) * tall] for at in range(4)]
    return parts[0] + parts[1], parts[2] + parts[3]


def pair_rows(dates):
    groups = dates // GROUP
    return GROUP * GROUP // 2 * groups + GROUP * GROUP * (groups * (groups - 1) // 2)


def pair_units(dates):
    groups = dates // GROUP
    half = GROUP // 2
    units = [(group, group, range(1, half + 1)) for group in range(groups)]
    for low in range(groups):
        for high in range(low + 1, groups):
            units += [(low, high, range(at, at + half)) for at in range(0, GROUP, half)]
    return units


def spread_block(block_ref, comb, dates_here, seat, rows_ref):
    sides = rows_ref.shape[1]
    combed = jnp.dot(cells_of(block_ref, sides), comb, preferred_element_type=F32)
    rows = combed.shape[0] // (2 * dates_here)
    for own in range(dates_here):
        for part in range(2):
            at = (own * 2 + part) * rows
            for side in range(sides):
                rows_ref[part, side, pl.ds(seat + own, rows, stride=GROUP), :] = combed[
                    at : at + rows, side * LANES : (side + 1) * LANES
                ]


def pack_group(rows_ref, looks, half_rows, store):
    pack = LANES // looks
    lane = iota((GROUP, LANES), 1)
    for part in range(2):
        for odd in range(2):
            for tile in range(-(-half_rows // pack)):
                for side in range(rows_ref.shape[1]):
                    cells = []
                    for near in range(pack):
                        half_row = tile * pack + near
                        at = (2 * half_row + odd) * GROUP
                        if half_row < half_rows:
                            cells.append(rows_ref[part, side, at : at + GROUP, :])
                        else:
                            cells.append(jnp.zeros((GROUP, LANES), F32))
                    bit = pack // 2
                    while bit:
                        clear = (lane // looks) & bit == 0
                        for near in range(pack):
                            if not near & bit:
                                one, two = cells[near], cells[near + bit]
                                cells[near] = jnp.where(
                                    clear, one, pltpu.roll(two, bit * looks, 1)
                                )
                                cells[near + bit] = jnp.where(
                                    clear, pltpu.roll(one, LANES - bit * looks, 1), two
                                )
                        bit //= 2
                    for near in range(pack):
                        store(part, odd, side * pack + near, tile, cells[near])


def unit_products(tile, looks, turns, mine_of, turned_of, store):
    lane = iota((GROUP, LANES), 1) % looks
    at_first, at_last = lane == 0, lane == looks - 1

    def product(place):
        mine = [[mine_of(part, odd, place, tile) for odd in range(2)] for part in range(2)]
        values = []
        for turn in turns:
            other = [
                [turned_of(part, odd, place, tile, turn, mine) for odd in range(2)]
                for part in range(2)
            ]
            real = (mine[0][0] * other[0][0] + mine[1][0] * other[1][0]) + (
                mine[0][1] * other[0][1] + mine[1][1] * other[1][1]
            )
            imaginary = (mine[1][0] * other[0][0] - mine[0][0] * other[1][0]) + (
                mine[1][1] * other[0][1] - mine[0][1] * other[1][1]
            )
            values += [real, imaginary]
        return values

    def running(places):
        total = product(places[0])
        ramp = total
        for place in places[1:]:
            total = [one + two for one, two in zip(total, product(place))]
            share = [0.5 * one for one in total] if place is places[-1] else total
            ramp = [one + two for one, two in zip(ramp, share)]
        return total, ramp

    early, to_left = running((0, 1, 2, 3))
    late, to_right = running((7, 6, 5, 4))
    values = []
    for index in range(len(early)):
        before = pltpu.roll(to_right[index], 1, 1)
        after = pltpu.roll(to_left[index], LANES - 1, 1)
        value = 8.0 * (early[index] + late[index]) - to_left[index] - to_right[index]
        value = value + jnp.where(at_first, 0.0, before) + jnp.where(at_last, 0.0, after)
        values.append(value)
    for part in range(2):
        store(part, tile, jnp.concatenate(values[part::2], axis=0))


def turn_here(part, odd, place, tile, turn, mine):
    return pltpu.roll(mine[part][odd], GROUP - turn, 0)


def seam_of(block_ref, dates_here, seat, seam_ref):
    height = block_ref.shape[0]
    lines = block_ref[height - NOTE_ROWS : height].astype(F32)
    for part in range(2):
        at = NOTE + part * dates_here
        seam_ref[part, seat : seat + dates_here, :] = lines[at : at + dates_here]


def early_kernel(dates_here, *refs):
    *block_refs, comb_ref, ring_ref, pair_ref, seam_ref, rows_ref = refs
    columns = comb_ref.shape[0]
    looks = columns // 8
    tiles = ring_ref.shape[3]
    half_rows = rows_ref.shape[2] // GROUP // 2
    comb = comb_of(columns)
    comb_ref[...] = comb
    for index, block_ref in enumerate(block_refs):
        spread_block(block_ref, comb, dates_here, index * dates_here, rows_ref)
        seam_of(block_ref, dates_here, index * dates_here, seam_ref)

    def keep(part, odd, place, tile, cells):
        ring_ref[part, odd, place, tile] = cells

    pack_group(rows_ref, looks, half_rows, keep)

    def store(part, tile, value):
        across = slice(tile * LANES, (tile + 1) * LANES)
        high, low = halves(value)
        pair_ref[part, 0, :, across] = high
        pair_ref[part, 1, :, across] = low

    for tile in range(tiles):
        unit_products(
            tile,
            looks,
            range(1, GROUP // 2 + 1),
            lambda part, odd, place, tile: ring_ref[part, odd, place, tile],
            turn_here,
            store,
        )


def place_of(step, owners, dates_here):
    date = (step + 1) % owners * dates_here
    return date // GROUP, date % GROUP


def middle_kernel(dates_here, slots, steps, *refs):
    *refs, rows_ref, seams_ref, partial_ref, rest_ref, wide_ref = refs
    comb_ref, inverse_ref, *block_refs = refs
    owners = len(block_refs) + 1
    comb = comb_ref[...]
    wide_ref[...] = jnp.zeros_like(wide_ref)
    wide_ref[: inverse_ref.shape[0], : inverse_ref.shape[1]] = inverse_ref[...]
    wide = wide_ref[...]
    sums = [0.0, 0.0]
    for step, block_ref in zip(steps, block_refs):
        group, seat = place_of(step, owners, dates_here)
        if group:
            spread_block(block_ref, comb, dates_here, seat, rows_ref.at[group - 1])
            seam_of(block_ref, dates_here, seat, seams_ref.at[group - 1])
        more = slot_weights(block_ref, inverse_of(wide, step, owners, slots), owners, dates_here)
        sums = [one + two for one, two in zip(sums, more)]
    for part in range(2):
        partial_ref[part] = sums[part]
    rest_ref[...] = inverse_of(wide, 1, owners, slots)


def edge_kernel(dates_here, owners, *refs):
    block_ref, seam_ref, others_ref, partial_ref, rest_ref, comb_ref, other_rows_ref, *refs = refs
    weights_ref, ring_ref, far_ref, *message_refs, seams_ref, pair_ref, rows_ref = refs
    dates = owners * dates_here
    pairs = pair_rows(dates)
    tall = rest_ref.shape[0]

    group, seat = place_of(1, owners, dates_here)
    rows_ref[...] = other_rows_ref[...]
    spread_block(block_ref, comb_ref[...], dates_here, seat, rows_ref.at[group - 1])
    seams_ref[...] = others_ref[...]
    seam_of(block_ref, dates_here, seat, seams_ref.at[group - 1])
    weights = []
    for part, more in enumerate(slot_weights(block_ref, rest_ref[...], owners, dates_here)):
        high, low = halves(partial_ref[part] + more)
        wide = [jnp.concatenate([half, half], axis=1) for half in (high, low)]
        weights.append(jnp.concatenate(wide, axis=0))
        weights_ref[part] = weights[part]

    lane = iota((GROUP, LANES), 1) % 8
    ramp = jnp.where(lane < 4, 3.5 - lane.astype(F32), lane.astype(F32) - 3.5)
    for unit, (low, high, turns) in enumerate(pair_units(dates)):
        mine = [(seams_ref[low - 1, part] if low else seam_ref[part]) * ramp for part in range(2)]
        theirs = [seams_ref[high - 1, part] if high else seam_ref[part] for part in range(2)]
        values = []
        for turn in turns:
            other = [pltpu.roll(cells, GROUP - turn, 0) if turn else cells for cells in theirs]
            values.append(mine[0] * other[0] + mine[1] * other[1])
            values.append(mine[1] * other[0] - mine[0] * other[1])
        for part in range(2):
            value = jnp.concatenate(values[part::2], axis=0)
            for shift in (1 if part else LANES - 1, LANES - 2, LANES - 8):
                value = value + pltpu.roll(value, shift, 1)
            count = value.shape[0]
            bits = halves(value)
            for half in range(2):
                at = half * pairs + unit * count
                pair_ref[part, at : at + count, :] = bits[half]
    sums = []
    for part in range(2):
        summed = jnp.dot(weights[part], pair_ref[part], preferred_element_type=F32)
        sums.append(summed[:tall] + summed[tall:])
    message = jnp.where(iota((tall, LANES), 1) % 4 == 1, sums[1], sums[0])
    for message_ref in message_refs:
        message_ref[...] = message
    looks = comb_ref.shape[0] // 8
    half_rows = rows_ref.shape[3] // GROUP // 2
    for group in range(1, dates // GROUP):

        def keep(part, odd, place, tile, cells):
            ring_ref[group - 1, part, odd, place, tile] = cells
            for copy in range(2):
                at = pl.ds(2 * copy * GROUP + odd, GROUP, stride=2)
                far_ref[group - 1, part, place, tile, at, :] = cells

        pack_group(rows_ref.at[group - 1], looks, half_rows, keep)


def series_kernel(looks, *refs):
    weights_ref, first_ref, first_pair_ref, ring_ref, far_ref, looked_ref, pair_ref = refs
    groups = 1 + ring_ref.shape[0]
    dates = groups * GROUP
    pairs = pair_rows(dates)
    tiles = ring_ref.shape[4]
    tall = looked_ref.shape[1]

    for part in range(2):
        for half in range(2):
            at = half * pairs
            pair_ref[part, at : at + first_pair_ref.shape[2], :] = first_pair_ref[part, half]
    for tile in range(tiles):
        for unit, (low, high, turns) in enumerate(pair_units(dates)):
            if high == 0:
                continue

            def mine_of(part, odd, place, tile):
                if low == 0:
                    return first_ref[part, odd, place, tile]
                return ring_ref[low - 1, part, odd, place, tile]

            def turn_far(part, odd, place, tile, turn, mine):
                at = pl.ds(2 * turn + odd, GROUP, stride=2)
                return far_ref[high - 1, part, place, tile, at, :]

            def store(part, tile, value):
                count = value.shape[0]
                across = slice(tile * LANES, (tile + 1) * LANES)
                bits = halves(value)
                for half in range(2):
                    at = half * pairs + unit * count
                    pair_ref[part, at : at + count, across] = bits[half]

            turned_of = turn_here if low == high else turn_far
            unit_products(tile, looks, turns, mine_of, turned_of, store)
        across = slice(tile * LANES, (tile + 1) * LANES)
        for part in range(2):
            summed = jnp.dot(
                weights_ref[part], pair_ref[part, :, across], preferred_element_type=F32
            )
            looked_ref[part, :, across] = summed[:tall] + summed[tall:]


def finish_kernel(looked_ref, *refs):
    *message_refs, out_ref, sum_ref, done_ref, semaphores = refs
    parts, times, half_rows, looks = done_ref.shape
    tall = looked_ref.shape[1]
    pack = LANES // looks
    here, last = lax.axis_index("col"), lax.axis_size("col") - 1
    swaps = len(message_refs)
    from_right = from_left = jnp.zeros((tall, LANES), F32)
    for swap, message_ref in enumerate(message_refs):
        message = message_ref[...]
        from_right = jnp.where((here != last) & (here % swaps == swap), message, from_right)
        from_left = jnp.where((here != 0) & ((here - 1) % swaps == swap), message, from_left)
    lane = iota((tall, LANES), 1)
    sent = []
    for part in range(parts):
        for half_row in range(half_rows):
            tile, near = half_row // pack, half_row % pack
            value = looked_ref[part, :, tile * LANES : (tile + 1) * LANES]
            value = pltpu.roll(value, -near * looks % LANES, 1)
            at = 16 * half_row + part
            right = pltpu.roll(from_right, (looks - 1 - at) % LANES, 1)
            left = pltpu.roll(from_left, (-4 - at) % LANES, 1)
            value = jnp.where(lane == looks - 1, value + right, value)
            value = jnp.where(lane == 0, value + left, value)
            sum_ref[part, half_row * tall : (half_row + 1) * tall, :] = value
        for time in range(times):
            rows = sum_ref[part, pl.ds(time, half_rows, stride=tall), :]
            done_ref[part, time] = rows[:, :looks]
        sent.append(
            pltpu.make_async_copy(done_ref.at[part], out_ref.at[:, part], semaphores.at[part])
        )
        sent[part].start()
    for copy in sent:
        copy.wait()


def column_swap(swap, swaps, owners, count):
    moves = []
    for owner in range(owners):
        for column in range(count):
            partner = column
            if column % swaps == swap and column + 1 < count:
                partner = column + 1
            elif column and (column - 1) % swaps == swap:
                partner = column - 1
            moves.append((owner * count + column, twin_of(owner, owners) * count + partner))
    return moves


def per_device(scenes, pair_dates, pair_count, inverse):
    owners, count = lax.axis_size("date"), lax.axis_size("col")
    dates_here, parts, all_rows, columns = scenes.shape
    half_rows = all_rows // owners // 2
    dates = owners * dates_here
    pairs = pair_rows(dates)
    looks = columns // 8
    tiles = -(-half_rows // (LANES // looks))

    blocks = cut(scenes, pair_dates.T, pair_count, owners)
    for step in range(1, owners):
        moves = [(owner, (owner - step) % owners) for owner in range(owners)]
        blocks[step] = lax.ppermute(blocks[step], "date", moves)

    tall = round_up(inverse.shape[0], 16)
    rows = 2 * half_rows
    sides = columns // LANES
    order = [blocks[(place - 1) % owners] for place in range(owners)]
    order = [held(block) for block in order]
    group_rows = pltpu.VMEM((parts, sides, rows * GROUP, LANES), F32)
    comb, first_group, first_pairs, first_seam = pl.pallas_call(
        functools.partial(early_kernel, dates_here),
        out_shape=[
            pltpu.VMEM((columns, columns), BF16),
            pltpu.VMEM((parts, 2, 8, tiles, GROUP, LANES), F32),
            pltpu.VMEM((parts, 2, GROUP * GROUP // 2, tiles * LANES), BF16),
            pltpu.VMEM((parts, GROUP, LANES), F32),
        ],
        in_specs=[IN_VMEM] * (GROUP // dates_here),
        out_specs=[IN_VMEM] * 4,
        scratch_shapes=[group_rows],
        compiler_params=pltpu.CompilerParams(vmem_limit_bytes=40 << 20),
    )(*order[: GROUP // dates_here])
    others = dates // GROUP - 1
    steps = [*range(owners - 1, 1, -1), 0]
    group_rows = pltpu.VMEM((others, *group_rows.shape), F32)
    other_rows, other_seams, partial, rest = pl.pallas_call(
        functools.partial(middle_kernel, dates_here, pair_dates.shape[0], steps),
        out_shape=[
            group_rows,
            pltpu.VMEM((others, parts, GROUP, LANES), F32),
            pltpu.VMEM((parts, tall, pairs), F32),
            pltpu.VMEM((tall, LANES), F32),
        ],
        in_specs=[IN_VMEM] * (owners + 1),
        out_specs=[IN_VMEM] * 4,
        scratch_shapes=[pltpu.VMEM((tall, round_up(inverse.shape[1], LANES)), F32)],
        compiler_params=pltpu.CompilerParams(vmem_limit_bytes=40 << 20),
    )(held(comb), held(inverse), *[held(blocks[step]) for step in steps])
    swaps = min(3, count - 1)
    weights, ring, far, *messages = pl.pallas_call(
        functools.partial(edge_kernel, dates_here, owners),
        out_shape=[
            pltpu.VMEM((parts, 2 * tall, 2 * pairs), BF16),
            pltpu.VMEM((others, parts, 2, 8, tiles, GROUP, LANES), F32),
            pltpu.VMEM((others, parts, 8, tiles, 4 * GROUP, LANES), F32),
            *[pltpu.VMEM((tall, LANES), F32)] * swaps,
        ],
        in_specs=[IN_VMEM] * 7,
        out_specs=[IN_VMEM] * (swaps + 3),
        scratch_shapes=[
            pltpu.VMEM((others, parts, GROUP, LANES), F32),
            pltpu.VMEM((parts, 2 * pairs, LANES), BF16),
            group_rows,
        ],
        compiler_params=pltpu.CompilerParams(vmem_limit_bytes=40 << 20),
    )(
        *[held(one) for one in (blocks[1], first_seam, other_seams, partial, rest, comb)],
        held(other_rows),
    )
    looked = pl.pallas_call(
        functools.partial(series_kernel, looks),
        out_shape=pltpu.VMEM((parts, tall, tiles * LANES), F32),
        in_specs=[IN_VMEM] * 5,
        out_specs=IN_VMEM,
        scratch_shapes=[pltpu.VMEM((parts, 2 * pairs, tiles * LANES), BF16)],
        compiler_params=pltpu.CompilerParams(vmem_limit_bytes=40 << 20),
        cost_estimate=pl.CostEstimate(
            flops=2 * parts * pairs * columns * rows * 8, bytes_accessed=1 << 20, transcendentals=0
        ),
    )(*[held(one) for one in (weights, first_group, first_pairs, ring, far)])

    for swap in range(swaps):
        moves = column_swap(swap, swaps, owners, count)
        messages[swap] = held(lax.ppermute(messages[swap], ("date", "col"), moves))
    return pl.pallas_call(
        finish_kernel,
        out_shape=jax.ShapeDtypeStruct(
            (inverse.shape[0], parts, half_rows, columns // 8), F32
        ),
        in_specs=[IN_VMEM] * (swaps + 1),
        out_specs=ANYWHERE,
        scratch_shapes=[
            pltpu.VMEM((parts, half_rows * tall, LANES), F32),
            pltpu.VMEM((parts, inverse.shape[0], half_rows, columns // 8), F32),
            pltpu.SemaphoreType.DMA((parts,)),
        ],
    )(held(looked), *messages)


def solution(mesh):
    placed = (P("date", None, "groups", "col"), P("date", None), P("date"), P())
    return jax.shard_map(
        per_device,
        mesh=mesh,
        in_specs=placed,
        out_specs=P(None, None, ("groups", "date"), "col"),
        check_vma=False,
    )
```
